32 devices in a mesh: groups: 2 (over x), expert: 16 (over z, y, core).
Axes of the slice: x: 2, y: 2, z: 4, core: 2. Of those that a mesh axis runs over, the one named last changes fastest.
Arguments:
- tokens: bfloat16 [2048, 7168], P(('groups', 'expert')), parts along dimension 0, may hold values from -6 to 6
- expert_ids: int32 [2048, 8], P(('groups', 'expert')), parts along dimension 0, may hold values from 0 to 255, as said below
- route_logits: float32 [2048, 8], P(('groups', 'expert')), parts along dimension 0, may hold values from -6 to 6
- w_gate: bfloat16 [7168, 4096], P(None, 'expert'), may hold values from -0.0625 to 0.0625
- w_up: bfloat16 [7168, 4096], P(None, 'expert'), may hold values from -0.0625 to 0.0625
- w_down: bfloat16 [4096, 7168], P('expert'), may hold values from -0.125 to 0.125
Outputs:
- blended: bfloat16 [2048, 7168], P(('groups', 'expert')), parts along dimension 0
The draws below stay inside these ranges and needn't reach their ends.
There are 2 independent parts, one for each index of `groups`. The reference program is written for one: setup_inputs(seed, part) draws one part's arguments, and reference() takes and returns one part's arrays. A program takes and returns all parts, laid end to end along the dimension named above; an argument that names none is the same for every part. Nothing has to cross between parts.
Inputs may be any that keep to these rules, and one draw needn't show every extreme that they name: `expert_ids`: each row names 8 different experts. Within the rows of one device (aligned blocks of 64 rows) no expert is named by more than 5 rows, and one and the same expert below 2 is named by exactly 5 rows in every block.
All inputs are finite; a program needn't handle non-finite values.
Results may differ from the reference program's by a relative error of at most 0.0049.
Values may be sent and summed in bfloat16 or wider, within the bound.
No kernel may reach another device: no remote copies, remote signals or barrier semaphores. Data moves between devices by JAX's collectives and lax.ppermute only.
A program may use at most 128 MiB of HBM per device.

```python
import jax
import jax.numpy as jnp
import numpy as np
from jax import lax

D = 7168
FF = 2048
EXPERTS = 256
TOP = 8
TOK_DEV = 64
SPLIT = 8
CAP = 5
UNITS = 4096
TOKENS = 1024
N_EXPERT = 16


length_patterns = np.array([[2, 2, 2, 2], [3, 2, 2, 1], [1, 3, 2, 2], [4, 2, 1, 1], [1, 1, 4, 2], [3, 3, 1, 1], [1, 2, 3, 2], [2, 1, 1, 4], [1, 2, 1, 4], [2, 4, 1, 1]], dtype=np.int32)


full_patterns = np.array([[5, 1, 1, 1], [1, 5, 1, 1], [1, 1, 5, 1], [1, 1, 1, 5]], dtype=np.int32)


def draw_expert_ids(key, part):
    key = jax.random.fold_in(key, 11)
    blocks = TOKENS // TOK_DEV
    group_count = TOK_DEV * TOP // 8
    run_count = group_count * 4
    full_key, order_key = jax.random.split(key, 2)
    full_expert = jax.random.randint(full_key, (), 0, N_EXPERT // SPLIT).astype(jnp.int32)
    pattern_table = jnp.asarray(length_patterns)
    full_table = jnp.asarray(full_patterns)

    def one_block(block_key):
        pattern_key, group_key, place_key, shuffle_key = jax.random.split(block_key, 4)
        pattern_pick = jax.random.randint(pattern_key, (group_count,), 0, pattern_table.shape[0])
        sequence_length = pattern_table[pattern_pick]
        forced_group = jax.random.randint(group_key, (), 0, group_count)
        forced_place = jax.random.randint(place_key, (), 0, 4)
        sequence_length = sequence_length.at[forced_group].set(full_table[forced_place]).reshape(run_count)
        forced_run = forced_group * 4 + forced_place
        starts = jnp.cumsum(sequence_length) - sequence_length
        pick_index = jnp.arange(TOK_DEV * TOP, dtype=jnp.int32)
        run_index = jnp.sum((starts[None, :] <= pick_index[:, None]).astype(jnp.int32), axis=1) - 1
        expert_order = jax.random.permutation(shuffle_key, EXPERTS).astype(jnp.int32)
        where_full = jnp.argmax((expert_order == full_expert).astype(jnp.int32))
        displaced = expert_order[forced_run]
        expert_order = expert_order.at[where_full].set(displaced).at[forced_run].set(full_expert)
        chosen = expert_order[run_index]
        return jnp.transpose(chosen.reshape(TOP, TOK_DEV))
    block_keys = jax.random.split(order_key, blocks)
    return jax.vmap(one_block)(block_keys).reshape(TOKENS, TOP).astype(jnp.int32)


def block_scale(rng, dims, cuts, smallest, top_value):
    level = 1.0
    for dim, parts in cuts:
        draws = jax.random.uniform(jax.random.fold_in(jax.random.fold_in(rng, 6), dim), (parts,), jnp.float32, smallest / len(cuts), top_value / len(cuts))
        level = level * jnp.repeat(jnp.exp(draws), dims[dim] // parts).reshape((-1,) + (1,) * (len(dims) - 1 - dim))
    return level


def normal_values(stream_key, extent, deviation, bound, pieces=(), kind=jnp.bfloat16):
    drawn = jax.random.normal(stream_key, extent, jnp.float32) * deviation
    if len(pieces) > 0:
        drawn = block_scale(stream_key, extent, pieces, -0.22, 0.18) * drawn
    return jnp.clip(drawn, min=-bound, max=bound).astype(kind)


def setup_inputs(seed: int = 0, part: int = 0) -> dict:
    splits = jax.random.split(jax.random.key(seed), 7)
    part_keys = jax.random.split(jax.random.fold_in(splits[6], part), 7)
    tokens = normal_values(part_keys[0], (TOKENS, D), 1.0, 6.0, ((0, 16),))
    expert_ids = draw_expert_ids(jax.random.fold_in(jax.random.fold_in(splits[6], part), 71), part)
    route_logits = normal_values(part_keys[2], (TOKENS, TOP), 1.5, 6.0, ((0, 16),), jnp.float32)
    w_gate = normal_values(splits[3], (D, UNITS), D ** -0.5, 0.0625, ((1, 16),))
    w_up = normal_values(splits[4], (D, UNITS), D ** -0.5, 0.0625, ((1, 16),))
    w_down = normal_values(splits[5], (UNITS, D), FF ** -0.5, 0.125, ((0, 16),))
    return dict(tokens=tokens, expert_ids=expert_ids, route_logits=route_logits, w_gate=w_gate, w_up=w_up, w_down=w_down)


route_scale = 2.5


def route_tables(expert_ids, route_logits, in_flight, capacity):
    count_of_rows, pick_count = expert_ids.shape
    flat_ids = expert_ids.reshape(count_of_rows * pick_count)
    labels = jnp.arange(in_flight, dtype=jnp.int32)
    hit_table = (flat_ids[:, None] == labels[None, :]).astype(jnp.int32)
    earlier = jnp.cumsum(hit_table, axis=0) - hit_table
    slot_index = jnp.sum(earlier * hit_table, axis=1)
    live_mask = jnp.sum(hit_table, axis=1)
    target = jnp.sum(hit_table * labels[None, :], axis=1)
    column = jnp.where(live_mask > 0, target * capacity + slot_index, -1)
    positions = jnp.arange(in_flight * capacity, dtype=jnp.int32)
    pick_place = (column[:, None] == positions[None, :]).reshape(count_of_rows, pick_count, in_flight * capacity)
    lifted = jax.nn.sigmoid(route_logits)
    gate_values = route_scale * lifted / jnp.sum(lifted, axis=1, keepdims=True)
    expert_weight = jnp.sum(pick_place.astype(gate_values.dtype) * gate_values[:, :, None], axis=1)
    device_assignment = jnp.transpose(jnp.sum(pick_place.astype(jnp.int32), axis=1)).astype(jnp.bfloat16)
    return device_assignment, expert_weight


def expert_rows(rows_in, gate_cols, up_cols, down_rows):
    gate_act = jnp.dot(rows_in, gate_cols, preferred_element_type=jnp.float32)
    up_act = jnp.dot(rows_in, up_cols, preferred_element_type=jnp.float32)
    hidden = (jax.nn.silu(gate_act) * up_act).astype(jnp.bfloat16)
    return jnp.dot(hidden, down_rows, preferred_element_type=jnp.float32)


def reference(tokens, expert_ids, route_logits, w_gate, w_up, w_down):
    in_flight = N_EXPERT // SPLIT
    blocks = TOKENS // TOK_DEV
    features = tokens.shape[1]

    def tables(block_ids, block_logits):
        return route_tables(block_ids, block_logits, in_flight, CAP)

    device_assignment, expert_weight = jax.vmap(tables)(expert_ids.reshape(blocks, TOK_DEV, TOP), route_logits.reshape(blocks, TOK_DEV, TOP))
    token_groupings = tokens.reshape(blocks, TOK_DEV, features)
    holding_areas = jnp.einsum("fml,fln->fmn", device_assignment.astype(jnp.float32), token_groupings.astype(jnp.float32)).astype(jnp.bfloat16)
    grouped_rows = jnp.transpose(holding_areas.reshape(blocks, in_flight, CAP, features), (1, 0, 2, 3)).reshape(in_flight, blocks * CAP, features)
    gate_stack = jnp.transpose(w_gate.reshape(features, in_flight, FF), (1, 0, 2))
    up_stack = jnp.transpose(w_up.reshape(features, in_flight, FF), (1, 0, 2))
    down_stack = w_down.reshape(in_flight, FF, features)

    def one_expert(operands):
        return expert_rows(operands[0], operands[1], operands[2], operands[3])

    outputs = lax.map(one_expert, (grouped_rows, gate_stack, up_stack, down_stack))
    expert_results = jnp.transpose(outputs.reshape(in_flight, blocks, CAP, features), (1, 0, 2, 3)).reshape(blocks, in_flight * CAP, features)
    blended = jnp.einsum("aov,avn->aon", expert_weight, expert_results, precision=lax.Precision.HIGHEST)
    return blended.reshape(TOKENS, features).astype(jnp.bfloat16)
```

```python
import jax
import jax.numpy as jnp
from jax import lax
from jax.sharding import PartitionSpec as P

SPLIT = 8
CAP = 5


route_scale = 2.5


def route_tables(expert_ids, route_logits, in_flight, capacity):
    count_of_rows, pick_count = expert_ids.shape
    flat_ids = expert_ids.reshape(count_of_rows * pick_count)
    labels = jnp.arange(in_flight, dtype=jnp.int32)
    hit_table = (flat_ids[:, None] == labels[None, :]).astype(jnp.int32)
    earlier = jnp.cumsum(hit_table, axis=0) - hit_table
    slot_index = jnp.sum(earlier * hit_table, axis=1)
    live_mask = jnp.sum(hit_table, axis=1)
    target = jnp.sum(hit_table * labels[None, :], axis=1)
    column = jnp.where(live_mask > 0, target * capacity + slot_index, -1)
    positions = jnp.arange(in_flight * capacity, dtype=jnp.int32)
    pick_place = (column[:, None] == positions[None, :]).reshape(
        count_of_rows, pick_count, in_flight * capacity
    )
    lifted = jax.nn.sigmoid(route_logits)
    gate_values = route_scale * lifted / jnp.sum(lifted, axis=1, keepdims=True)
    expert_weight = jnp.sum(pick_place.astype(gate_values.dtype) * gate_values[:, :, None], axis=1)
    device_assignment = jnp.transpose(jnp.sum(pick_place.astype(jnp.int32), axis=1)).astype(
        jnp.bfloat16
    )
    return (device_assignment, expert_weight)


def expert_rows(rows_in, gate_cols, up_cols, down_rows):
    gate_act = jnp.dot(rows_in, gate_cols, preferred_element_type=jnp.float32)
    up_act = jnp.dot(rows_in, up_cols, preferred_element_type=jnp.float32)
    hidden = (jax.nn.silu(gate_act) * up_act).astype(jnp.bfloat16)
    return jnp.dot(hidden, down_rows, preferred_element_type=jnp.float32)


def swap_teams(blocks, teams):
    got = [blocks[0]]
    count = teams * SPLIT
    for k in range(1, teams):
        pairs = [(i, (i + k * SPLIT) % count) for i in range(count)]
        got.append(lax.ppermute(blocks[k], "expert", pairs))
    return got


def body(tokens, expert_ids, route_logits, w_gate, w_up, w_down):
    devices = lax.axis_size("expert")
    teams = devices // SPLIT
    mine = lax.axis_index("expert") // SPLIT
    features = tokens.shape[1]
    groups = [[t * SPLIT + p for p in range(SPLIT)] for t in range(teams)]
    device_assignment, expert_weight = route_tables(expert_ids, route_logits, teams, CAP)
    assignment = jnp.roll(device_assignment.reshape(teams, CAP, -1), -mine, axis=0)
    weight = jnp.roll(expert_weight.reshape(-1, teams, CAP), -mine, axis=1)
    sent = [
        jnp.dot(assignment[k], tokens, preferred_element_type=jnp.float32).astype(jnp.bfloat16)
        for k in range(teams)
    ]
    got = swap_teams(sent, teams)
    rows = lax.all_gather(
        jnp.concatenate(got, axis=0), "expert", axis_index_groups=groups, tiled=True
    )
    produced = expert_rows(rows, w_gate, w_up, w_down)
    mixed = lax.psum_scatter(
        produced, "expert", scatter_dimension=0, axis_index_groups=groups, tiled=True
    )
    mixed = mixed.reshape(teams, CAP, features)
    count = devices
    back = [mixed[0]]
    for k in range(1, teams):
        pairs = [(i, (i - k * SPLIT) % count) for i in range(count)]
        back.append(lax.ppermute(mixed[k], "expert", pairs))
    blended = jnp.dot(
        weight.reshape(-1, teams * CAP),
        jnp.concatenate(back, axis=0),
        precision=lax.Precision.HIGHEST,
        preferred_element_type=jnp.float32,
    )
    return blended.astype(jnp.bfloat16)


def solution(mesh):
    placed = (
        P(("groups", "expert"), None),
        P(("groups", "expert"), None),
        P(("groups", "expert"), None),
        P(None, "expert"),
        P(None, "expert"),
        P("expert", None),
    )
    return jax.shard_map(
        body, mesh=mesh, in_specs=placed, out_specs=P(("groups", "expert"), None), check_vma=False
    )
```

```python
import jax
import jax.numpy as jnp
from jax import lax
from jax.sharding import PartitionSpec as P

SPLIT = 8
CAP = 5


route_scale = 2.5


def route_tables(expert_ids, route_logits, in_flight, capacity):
    count_of_rows, pick_count = expert_ids.shape
    flat_ids = expert_ids.reshape(count_of_rows * pick_count)
    labels = jnp.arange(in_flight, dtype=jnp.int32)
    hit_table = (flat_ids[:, None] == labels[None, :]).astype(jnp.int32)
    earlier = jnp.cumsum(hit_table, axis=0) - hit_table
    slot_index = jnp.sum(earlier * hit_table, axis=1)
    live_mask = jnp.sum(hit_table, axis=1)
    target = jnp.sum(hit_table * labels[None, :], axis=1)
    column = jnp.where(live_mask > 0, target * capacity + slot_index, -1)
    positions = jnp.arange(in_flight * capacity, dtype=jnp.int32)
    pick_place = (column[:, None] == positions[None, :]).reshape(
        count_of_rows, pick_count, in_flight * capacity
    )
    lifted = jax.nn.sigmoid(route_logits)
    gate_values = route_scale * lifted / jnp.sum(lifted, axis=1, keepdims=True)
    expert_weight = jnp.sum(pick_place.astype(gate_values.dtype) * gate_values[:, :, None], axis=1)
    device_assignment = jnp.transpose(jnp.sum(pick_place.astype(jnp.int32), axis=1)).astype(
        jnp.bfloat16
    )
    return (device_assignment, expert_weight)


def expert_rows(rows_in, gate_cols, up_cols, down_rows):
    gate_act = jnp.dot(rows_in, gate_cols, preferred_element_type=jnp.float32)
    up_act = jnp.dot(rows_in, up_cols, preferred_element_type=jnp.float32)
    hidden = (jax.nn.silu(gate_act) * up_act).astype(jnp.bfloat16)
    return jnp.dot(hidden, down_rows, preferred_element_type=jnp.float32)


CORES = 2
SEGMENTS = 8


def body(tokens, expert_ids, route_logits, w_gate, w_up, w_down):
    devices = lax.axis_size("expert")
    teams = devices // SPLIT
    chips = SPLIT // CORES
    features = tokens.shape[1]
    wide = features // SEGMENTS
    same_core = [[i for i in range(devices) if i % CORES == c] for c in range(CORES)]
    other_core = [(i, i + 1 - 2 * (i % CORES)) for i in range(devices)]
    device_assignment, expert_weight = route_tables(expert_ids, route_logits, teams, CAP)
    buffer = jnp.dot(device_assignment, tokens, preferred_element_type=jnp.float32).astype(
        jnp.bfloat16
    )
    packed = buffer.reshape(teams, CAP * SEGMENTS, wide)
    outbound = jnp.broadcast_to(
        packed[:, None], (teams, chips, CAP * SEGMENTS, wide)
    ).reshape(teams * chips, CAP * SEGMENTS, wide)
    here = lax.all_to_all(
        outbound, "expert", split_axis=0, concat_axis=0, axis_index_groups=same_core, tiled=True
    )
    there = lax.ppermute(here, "expert", other_core)
    count = teams * chips * CAP
    rows = jnp.concatenate([here.reshape(count, features), there.reshape(count, features)], axis=0)
    produced = expert_rows(rows, w_gate, w_up, w_down)
    kept, given = produced[:count], produced[count:].astype(jnp.bfloat16)
    taken = lax.ppermute(given, "expert", other_core)
    part = (kept + taken.astype(jnp.float32)).astype(jnp.bfloat16)
    returned = lax.all_to_all(
        part.reshape(teams * chips, CAP * SEGMENTS, wide),
        "expert",
        split_axis=0,
        concat_axis=0,
        axis_index_groups=same_core,
        tiled=True,
    )
    summed = jnp.sum(
        returned.astype(jnp.float32).reshape(teams, chips, CAP * SEGMENTS, wide), axis=1
    )
    blended = jnp.dot(
        expert_weight,
        summed.reshape(teams * CAP, features),
        precision=lax.Precision.HIGHEST,
        preferred_element_type=jnp.float32,
    )
    return blended.astype(jnp.bfloat16)


def solution(mesh):
    placed = (
        P(("groups", "expert"), None),
        P(("groups", "expert"), None),
        P(("groups", "expert"), None),
        P(None, "expert"),
        P(None, "expert"),
        P("expert", None),
    )
    return jax.shard_map(
        body, mesh=mesh, in_specs=placed, out_specs=P(("groups", "expert"), None), check_vma=False
    )
```

```python
import jax
import jax.numpy as jnp
from jax import lax
from jax.sharding import PartitionSpec as P

SPLIT = 8
CAP = 5


route_scale = 2.5


def route_tables(expert_ids, route_logits, mine, in_flight, capacity):
    count_of_rows, pick_count = expert_ids.shape
    flat_ids = expert_ids.reshape(count_of_rows * pick_count)
    labels = jnp.arange(in_flight, dtype=jnp.int32)
    flat_ids = jnp.where(flat_ids < in_flight, (flat_ids - mine) % in_flight, in_flight)
    hit_table = (flat_ids[:, None] == labels[None, :]).astype(jnp.int32)
    earlier = jnp.cumsum(hit_table, axis=0) - hit_table
    slot_index = jnp.sum(earlier * hit_table, axis=1)
    live_mask = jnp.sum(hit_table, axis=1)
    target = jnp.sum(hit_table * labels[None, :], axis=1)
    column = jnp.where(live_mask > 0, target * capacity + slot_index, -1)
    positions = jnp.arange(in_flight * capacity, dtype=jnp.int32)
    pick_place = (column[:, None] == positions[None, :]).reshape(
        count_of_rows, pick_count, in_flight * capacity
    )
    lifted = jax.nn.sigmoid(route_logits)
    gate_values = route_scale * lifted / jnp.sum(lifted, axis=1, keepdims=True)
    expert_weight = jnp.sum(pick_place.astype(gate_values.dtype) * gate_values[:, :, None], axis=1)
    device_assignment = jnp.transpose(jnp.sum(pick_place.astype(jnp.int32), axis=1)).astype(
        jnp.bfloat16
    )
    return (device_assignment, expert_weight)


def expert_rows(rows_in, gate_cols, up_cols, down_rows):
    gate_act = jnp.dot(rows_in, gate_cols, preferred_element_type=jnp.float32)
    up_act = jnp.dot(rows_in, up_cols, preferred_element_type=jnp.float32)
    hidden = (jax.nn.silu(gate_act) * up_act).astype(jnp.bfloat16)
    return jnp.dot(hidden, down_rows, preferred_element_type=jnp.float32)


CORES = 2
SEGMENTS = 8


def gather_team(block, devices, chips):
    blocks = [block]
    for m in range(1, chips):
        pairs = [(i, i ^ (m * CORES)) for i in range(devices)]
        blocks.append(lax.ppermute(block, "expert", pairs))
    return blocks


def body(tokens, expert_ids, route_logits, w_gate, w_up, w_down):
    devices = lax.axis_size("expert")
    teams = devices // SPLIT
    chips = SPLIT // CORES
    features = tokens.shape[1]
    wide = features // SEGMENTS
    tall = CAP * SEGMENTS
    other_core = [(i, i ^ 1) for i in range(devices)]
    mine = lax.axis_index("expert") // SPLIT
    device_assignment, expert_weight = route_tables(expert_ids, route_logits, mine, teams, CAP)
    buffer = jnp.dot(device_assignment, tokens, preferred_element_type=jnp.float32).astype(
        jnp.bfloat16
    )
    packed = buffer.reshape(teams, tall, wide)
    blocks = []
    for k in range(teams):
        block = packed[k]
        if k > 0:
            pairs = [(i, (i + k * SPLIT) % devices) for i in range(devices)]
            block = lax.ppermute(block, "expert", pairs)
        blocks.append(jnp.stack(gather_team(block, devices, chips)))
    swapped = [lax.ppermute(b, "expert", other_core) for b in blocks]
    count = teams * chips * CAP
    rows = jnp.concatenate(blocks + swapped, axis=0).reshape(2 * count, features)
    produced = expert_rows(rows, w_gate, w_up, w_down)
    kept, given = produced[:count], produced[count:].astype(jnp.bfloat16)
    kept = kept.reshape(teams, chips, tall, wide)
    given = given.reshape(teams, chips, tall, wide)
    summed = [None] * teams
    for k in reversed(range(teams)):
        part = kept[k] + lax.ppermute(given[k], "expert", other_core).astype(jnp.float32)
        total = part[0]
        for m in range(1, chips):
            pairs = [(i, i ^ (m * CORES)) for i in range(devices)]
            total = total + lax.ppermute(
                part[m].astype(jnp.bfloat16), "expert", pairs
            ).astype(jnp.float32)
        if k > 0:
            pairs = [(i, (i - k * SPLIT) % devices) for i in range(devices)]
            total = lax.ppermute(total.astype(jnp.bfloat16), "expert", pairs).astype(jnp.float32)
        summed[k] = total
    blended = jnp.dot(
        expert_weight,
        jnp.stack(summed).reshape(teams * CAP, features),
        precision=lax.Precision.HIGHEST,
        preferred_element_type=jnp.float32,
    )
    return blended.astype(jnp.bfloat16)


def solution(mesh):
    placed = (
        P(("groups", "expert"), None),
        P(("groups", "expert"), None),
        P(("groups", "expert"), None),
        P(None, "expert"),
        P(None, "expert"),
        P("expert", None),
    )
    return jax.shard_map(
        body, mesh=mesh, in_specs=placed, out_specs=P(("groups", "expert"), None), check_vma=False
    )
```

```python
import functools

import jax
import jax.numpy as jnp
from jax import lax
from jax.experimental import pallas as pl
from jax.experimental.pallas import tpu as pltpu
from jax.sharding import PartitionSpec as P

SPLIT = 8
CAP = 5
CORES = 2
SEGMENTS = 8

route_scale = 2.5

VMEM = pl.BlockSpec(memory_space=pltpu.VMEM)
MIB = 1024 * 1024


def hits(ids, mine, teams):
    count = ids.shape[1]
    row = lax.broadcasted_iota(jnp.int32, (8 * pl.cdiv(teams, 8), count), 0)
    wanted = lax.rem(mine + row, teams)
    hit = jnp.zeros(row.shape, jnp.int32)
    for j in range(ids.shape[0]):
        hit = hit + jnp.where(ids[j : j + 1, :] == wanted, 1, 0)
    hit = jnp.where(row < teams, hit, 0).astype(jnp.float32)
    before = lax.broadcasted_iota(jnp.int32, (count, count), 0)
    after = lax.broadcasted_iota(jnp.int32, (count, count), 1)
    earlier = jnp.where(before < after, 1.0, 0.0).astype(jnp.bfloat16)
    slot = jnp.dot(hit.astype(jnp.bfloat16), earlier, preferred_element_type=jnp.float32)
    return hit, jnp.where(hit > 0, slot, -1.0)


def pack_kernel(teams, ids_ref, tokens_ref, *out_refs):
    mine = lax.axis_index("expert") // SPLIT
    _, slot = hits(ids_ref[...], mine, teams)
    count, features = tokens_ref.shape
    wide = features // SEGMENTS
    tall = CAP * SEGMENTS
    stacked = jnp.concatenate(
        [tokens_ref[:, s * wide : (s + 1) * wide] for s in range(SEGMENTS)], axis=0
    )
    shape = (tall, SEGMENTS * count)
    row = lax.broadcasted_iota(jnp.int32, shape, 0)
    column = lax.broadcasted_iota(jnp.int32, shape, 1)
    same = (row // CAP) == (column // count)
    place = lax.rem(row, CAP).astype(jnp.float32)
    picks = []
    for k in range(teams):
        slots = jnp.concatenate([slot[k : k + 1, :]] * SEGMENTS, axis=1)
        picks.append(jnp.where(same & (slots == place), 1.0, 0.0))
    packed = jnp.dot(
        jnp.concatenate(picks, axis=0).astype(jnp.bfloat16),
        stacked,
        preferred_element_type=jnp.float32,
    )
    for k in range(teams):
        out_refs[k][...] = packed[k * tall : (k + 1) * tall].astype(jnp.bfloat16)


def pack_rows(ids, tokens, teams):
    wide = tokens.shape[1] // SEGMENTS
    block = jax.ShapeDtypeStruct((CAP * SEGMENTS, wide), jnp.bfloat16)
    return pl.pallas_call(
        functools.partial(pack_kernel, teams),
        out_shape=[block] * teams,
        in_specs=[VMEM, VMEM],
        out_specs=[VMEM] * teams,
        name="pack_rows",
    )(ids, tokens)


def weight_kernel(teams, ids_ref, logits_ref, high_ref, low_ref):
    mine = lax.axis_index("expert") // SPLIT
    ids = ids_ref[...]
    hit, slot = hits(ids, mine, teams)
    count = ids.shape[1]
    lifted = jax.nn.sigmoid(logits_ref[...])
    gates = route_scale * lifted / jnp.sum(lifted, axis=0, keepdims=True)
    row = lax.broadcasted_iota(jnp.int32, hit.shape, 0)
    wanted = lax.rem(mine + row, teams)
    gate = jnp.zeros(hit.shape, jnp.float32)
    for j in range(ids.shape[0]):
        gate = gate + jnp.where(ids[j : j + 1, :] == wanted, gates[j : j + 1, :], 0.0)
    slot = jnp.transpose(slot)
    gate = jnp.transpose(gate)
    tall = CAP * SEGMENTS
    shape = (SEGMENTS * count, tall)
    down = lax.broadcasted_iota(jnp.int32, shape, 0)
    across = lax.broadcasted_iota(jnp.int32, shape, 1)
    same = (down // count) == (across // CAP)
    place = lax.rem(across, CAP).astype(jnp.float32)
    for k in range(teams):
        slots = jnp.concatenate([slot[:, k : k + 1]] * SEGMENTS, axis=0)
        factor = jnp.concatenate([gate[:, k : k + 1]] * SEGMENTS, axis=0)
        full = jnp.where(same & (slots == place), factor, 0.0)
        high = full.astype(jnp.bfloat16)
        high_ref[k] = high
        low_ref[k] = (full - high.astype(jnp.float32)).astype(jnp.bfloat16)


def blend_weights(ids, logits, teams):
    shape = (teams, SEGMENTS * ids.shape[1], CAP * SEGMENTS)
    out = jax.ShapeDtypeStruct(shape, jnp.bfloat16)
    return pl.pallas_call(
        functools.partial(weight_kernel, teams),
        out_shape=[out, out],
        in_specs=[VMEM, VMEM],
        out_specs=[VMEM, VMEM],
        name="blend_weights",
    )(ids, logits)


def down_rows(hidden, down_ref, out_ref):
    features = out_ref.shape[1]
    step = features // SEGMENTS
    for s in range(SEGMENTS):
        columns = slice(s * step, (s + 1) * step)
        out_ref[:, columns] = jnp.dot(
            hidden, down_ref[:, columns], preferred_element_type=jnp.float32
        ).astype(out_ref.dtype)


def expert_kernel(rows_ref, gate_ref, up_ref, down_ref, given_ref, hidden_ref):
    count, features = rows_ref.shape
    units = gate_ref.shape[1]
    step = features // 7

    def add_chunk(i, sums):
        columns = pl.ds(pl.multiple_of(i * step, step), step)
        rows = rows_ref[:, columns]
        return tuple(
            total + jnp.dot(rows, ref[columns, :], preferred_element_type=jnp.float32)
            for total, ref in zip(sums, (gate_ref, up_ref))
        )

    zero = jnp.zeros((count, units), jnp.float32)
    gate_act, up_act = lax.fori_loop(0, 7, add_chunk, (zero, zero))
    hidden = (jax.nn.silu(gate_act) * up_act).astype(jnp.bfloat16)
    half = count // 2
    hidden_ref[...] = hidden[:half]
    down_rows(hidden[half:], down_ref, given_ref)


def expert_half(rows, w_gate, w_up, w_down):
    count, features = rows.shape
    units = w_gate.shape[1]
    return pl.pallas_call(
        expert_kernel,
        out_shape=[
            jax.ShapeDtypeStruct((count // 2, features), jnp.bfloat16),
            jax.ShapeDtypeStruct((count // 2, units), jnp.bfloat16),
        ],
        in_specs=[VMEM] * 4,
        out_specs=[VMEM] * 2,
        compiler_params=pltpu.CompilerParams(vmem_limit_bytes=40 * MIB),
        cost_estimate=pl.CostEstimate(
            flops=5 * count * units * features,
            bytes_accessed=6 * features * units,
            transcendentals=count * units,
        ),
        name="expert_half",
    )(rows, w_gate, w_up, w_down)


def kept_kernel(hidden_ref, down_ref, kept_ref):
    down_rows(hidden_ref[...], down_ref, kept_ref)


def kept_half(hidden, w_down):
    count, units = hidden.shape
    features = w_down.shape[1]
    return pl.pallas_call(
        kept_kernel,
        out_shape=jax.ShapeDtypeStruct((count, features), jnp.float32),
        in_specs=[VMEM] * 2,
        out_specs=VMEM,
        compiler_params=pltpu.CompilerParams(vmem_limit_bytes=24 * MIB),
        cost_estimate=pl.CostEstimate(
            flops=2 * count * units * features,
            bytes_accessed=2 * features * units,
            transcendentals=0,
        ),
        name="kept_half",
    )(hidden, w_down)


def repack_kernel(chips, kept_ref, taken_ref, *out_refs):
    features = kept_ref.shape[1]
    wide = features // SEGMENTS
    for b, out_ref in enumerate(out_refs):
        for s in range(SEGMENTS):
            columns = slice(s * wide, (s + 1) * wide)
            rows = slice(b * CAP, (b + 1) * CAP)
            part = kept_ref[rows, columns] + taken_ref[rows, columns].astype(jnp.float32)
            out_ref[s * CAP : (s + 1) * CAP, :] = part.astype(out_ref.dtype)


def repack(kept, taken, teams, chips):
    count, features = kept.shape
    shape = (CAP * SEGMENTS, features // SEGMENTS)
    outs = [
        jax.ShapeDtypeStruct(shape, jnp.bfloat16 if m else jnp.float32)
        for k in range(teams)
        for m in range(chips)
    ]
    return pl.pallas_call(
        functools.partial(repack_kernel, chips),
        out_shape=outs,
        in_specs=[VMEM] * 2,
        out_specs=[VMEM] * len(outs),
        name="repack",
    )(kept, taken)


def sum_kernel(*refs):
    total = refs[0][...]
    for ref in refs[1:-1]:
        total = total + ref[...].astype(jnp.float32)
    refs[-1][...] = total.astype(refs[-1].dtype)


def sum_blocks(blocks):
    return pl.pallas_call(
        sum_kernel,
        out_shape=jax.ShapeDtypeStruct(blocks[0].shape, jnp.bfloat16),
        in_specs=[VMEM] * len(blocks),
        out_specs=VMEM,
        name="sum_blocks",
    )(*blocks)


def blend_kernel(chips, high_ref, low_ref, *refs):
    out_ref = refs[-1]
    teams = high_ref.shape[0]
    count, features = out_ref.shape
    wide = features // SEGMENTS
    own = refs[0][...]
    for ref in refs[1:chips]:
        own = own + ref[...].astype(jnp.float32)
    own_high = own.astype(jnp.bfloat16)
    own_low = (own - own_high.astype(jnp.float32)).astype(jnp.bfloat16)
    dot = functools.partial(jnp.dot, preferred_element_type=jnp.float32)
    total = dot(high_ref[0], own_high) + dot(high_ref[0], own_low) + dot(low_ref[0], own_high)
    for k in range(1, teams):
        rows = refs[chips + k - 1][...]
        total = total + dot(high_ref[k], rows) + dot(low_ref[k], rows)
    for s in range(SEGMENTS):
        out_ref[:, s * wide : (s + 1) * wide] = total[s * count : (s + 1) * count].astype(
            jnp.bfloat16
        )


def blend(high, low, own_blocks, other_blocks, count):
    chips = len(own_blocks)
    features = own_blocks[0].shape[1] * SEGMENTS
    return pl.pallas_call(
        functools.partial(blend_kernel, chips),
        out_shape=jax.ShapeDtypeStruct((count, features), jnp.bfloat16),
        in_specs=[VMEM] * (2 + chips + len(other_blocks)),
        out_specs=VMEM,
        compiler_params=pltpu.CompilerParams(vmem_limit_bytes=40 * MIB),
        name="blend",
    )(high, low, *own_blocks, *other_blocks)


def body(tokens, expert_ids, route_logits, w_gate, w_up, w_down):
    devices = lax.axis_size("expert")
    teams = devices // SPLIT
    chips = SPLIT // CORES
    features = tokens.shape[1]
    other_core = [(i, i ^ 1) for i in range(devices)]
    other_chip = [[(i, i ^ (m * CORES)) for i in range(devices)] for m in range(chips)]
    ids = expert_ids.T
    packed = pack_rows(ids, tokens, teams)
    high, low = blend_weights(ids, route_logits.T, teams)
    blocks = []
    for k in range(teams):
        block = packed[k]
        if k > 0:
            pairs = [(i, (i + k * SPLIT) % devices) for i in range(devices)]
            block = lax.ppermute(block, "expert", pairs)
        team = [block]
        for m in range(1, chips):
            team.append(lax.ppermute(block, "expert", other_chip[m]))
        blocks.append(jnp.stack(team))
    swapped = [lax.ppermute(b, "expert", other_core) for b in blocks]
    count = teams * chips * CAP
    both = jnp.concatenate(blocks + swapped, axis=0)
    wide = features // SEGMENTS
    both = both.reshape(2 * teams * chips, SEGMENTS, CAP, wide)
    rows = jnp.transpose(both, (0, 2, 1, 3)).reshape(2 * count, features)
    given, hidden = expert_half(rows, w_gate, w_up, w_down)
    taken = lax.ppermute(given, "expert", other_core)
    kept = kept_half(hidden, w_down)
    parts = repack(kept, taken, teams, chips)
    others = []
    own = None
    for k in reversed(range(teams)):
        team = [parts[k * chips]]
        for m in range(1, chips):
            team.append(lax.ppermute(parts[k * chips + m], "expert", other_chip[m]))
        if k > 0:
            pairs = [(i, (i - k * SPLIT) % devices) for i in range(devices)]
            others.insert(0, lax.ppermute(sum_blocks(team), "expert", pairs))
        else:
            own = team
    return blend(high, low, own, others, tokens.shape[0])


def solution(mesh):
    placed = (
        P(("groups", "expert"), None),
        P(("groups", "expert"), None),
        P(("groups", "expert"), None),
        P(None, "expert"),
        P(None, "expert"),
        P("expert", None),
    )
    return jax.shard_map(
        body, mesh=mesh, in_specs=placed, out_specs=P(("groups", "expert"), None), check_vma=False
    )
```

```python
import functools

import jax
import jax.numpy as jnp
from jax import lax
from jax.experimental import pallas as pl
from jax.experimental.pallas import tpu as pltpu
from jax.sharding import PartitionSpec as P

SPLIT = 8
CAP = 5
CORES = 2
SEGMENTS = 8

route_scale = 2.5

VMEM = pl.BlockSpec(memory_space=pltpu.VMEM)
MIB = 1024 * 1024


def hits(ids, mine, teams):
    count = ids.shape[1]
    row = lax.broadcasted_iota(jnp.int32, (8 * pl.cdiv(teams, 8), count), 0)
    wanted = lax.rem(mine + row, teams)
    hit = jnp.zeros(row.shape, jnp.int32)
    for j in range(ids.shape[0]):
        hit = hit + jnp.where(ids[j : j + 1, :] == wanted, 1, 0)
    hit = jnp.where(row < teams, hit, 0).astype(jnp.float32)
    before = lax.broadcasted_iota(jnp.int32, (count, count), 0)
    after = lax.broadcasted_iota(jnp.int32, (count, count), 1)
    earlier = jnp.where(before < after, 1.0, 0.0).astype(jnp.bfloat16)
    slot = jnp.dot(hit.astype(jnp.bfloat16), earlier, preferred_element_type=jnp.float32)
    return hit, jnp.where(hit > 0, slot, -1.0)


def fifth(shape, axis):
    at = lax.broadcasted_iota(jnp.int32, shape, axis)
    segment = jnp.zeros(shape, jnp.int32)
    for s in range(1, SEGMENTS):
        segment = segment + jnp.where(at >= s * CAP, 1, 0)
    return segment, (at - CAP * segment).astype(jnp.float32)


def params(mib):
    return pltpu.CompilerParams(vmem_limit_bytes=mib * MIB)


def pack_kernel(teams, ids_ref, tokens_ref, *out_refs):
    mine = lax.axis_index("expert") // SPLIT
    _, slot = hits(ids_ref[...], mine, teams)
    count, features = tokens_ref.shape
    wide = features // SEGMENTS
    tall = CAP * SEGMENTS
    stacked = jnp.concatenate(
        [tokens_ref[:, s * wide : (s + 1) * wide] for s in range(SEGMENTS)], axis=0
    )
    segment, place = fifth((tall, 1), 0)
    column = lax.broadcasted_iota(jnp.int32, (1, SEGMENTS * count), 1)
    same = segment == column // count
    picks = []
    for k in range(teams):
        slots = jnp.concatenate([slot[k : k + 1, :]] * SEGMENTS, axis=1)
        picks.append(jnp.where(same & (slots == place), 1.0, 0.0))
    packed = jnp.dot(
        jnp.concatenate(picks, axis=0).astype(jnp.bfloat16),
        stacked,
        preferred_element_type=jnp.float32,
    )
    for k in range(teams):
        out_refs[k][...] = packed[k * tall : (k + 1) * tall].astype(jnp.bfloat16)


def pack_rows(ids, tokens, teams):
    wide = tokens.shape[1] // SEGMENTS
    block = jax.ShapeDtypeStruct((CAP * SEGMENTS, wide), jnp.bfloat16)
    return pl.pallas_call(
        functools.partial(pack_kernel, teams),
        out_shape=[block] * teams,
        in_specs=[VMEM, VMEM],
        out_specs=[VMEM] * teams,
        compiler_params=params(8),
        name="pack_rows",
    )(ids, tokens)


def weight_kernel(teams, ids_ref, logits_ref, out_ref):
    mine = lax.axis_index("expert") // SPLIT
    ids = ids_ref[...]
    hit, slot = hits(ids, mine, teams)
    count = ids.shape[1]
    lifted = jax.nn.sigmoid(logits_ref[...])
    gates = route_scale * lifted / jnp.sum(lifted, axis=0, keepdims=True)
    row = lax.broadcasted_iota(jnp.int32, hit.shape, 0)
    wanted = lax.rem(mine + row, teams)
    gate = jnp.zeros(hit.shape, jnp.float32)
    for j in range(ids.shape[0]):
        gate = gate + jnp.where(ids[j : j + 1, :] == wanted, gates[j : j + 1, :], 0.0)
    slot = jnp.transpose(slot)
    gate = jnp.transpose(gate)
    tall = CAP * SEGMENTS
    depth = out_ref.shape[1]
    column = lax.broadcasted_iota(jnp.int32, (1, depth), 1)
    part = jnp.zeros((1, depth), jnp.int32)
    for g in range(1, depth // tall):
        part = part + jnp.where(column >= g * tall, 1, 0)
    column = column - tall * part
    segment = jnp.zeros((1, depth), jnp.int32)
    for s in range(1, SEGMENTS):
        segment = segment + jnp.where(column >= s * CAP, 1, 0)
    place = (column - CAP * segment).astype(jnp.float32)
    team = jnp.where(part < 3, 0, (part - 1) >> 1)
    low = jnp.where(part < 3, part >> 1, (part - 3) & 1) == 1
    for s in range(SEGMENTS):
        full = jnp.zeros((count, depth), jnp.float32)
        for k in range(teams):
            chosen = (team == k) & (segment == s) & (slot[:, k : k + 1] == place)
            full = full + jnp.where(chosen, gate[:, k : k + 1], 0.0)
        high = full.astype(jnp.bfloat16).astype(jnp.float32)
        out_ref[s * count : (s + 1) * count, :] = jnp.where(low, full - high, high).astype(
            jnp.bfloat16
        )


def blend_weights(ids, logits, teams):
    shape = (SEGMENTS * ids.shape[1], CAP * SEGMENTS * (1 + 2 * teams))
    return pl.pallas_call(
        functools.partial(weight_kernel, teams),
        out_shape=jax.ShapeDtypeStruct(shape, jnp.bfloat16),
        in_specs=[VMEM, VMEM],
        out_specs=VMEM,
        compiler_params=params(4 + teams),
        name="blend_weights",
    )(ids, logits)


def join_kernel(*refs):
    tall = refs[0].shape[0]
    for i, ref in enumerate(refs[:-1]):
        refs[-1][i * tall : (i + 1) * tall, :] = ref[...]


def join(blocks):
    tall, wide = blocks[0].shape
    return pl.pallas_call(
        join_kernel,
        out_shape=jax.ShapeDtypeStruct((tall * len(blocks), wide), blocks[0].dtype),
        in_specs=[VMEM] * len(blocks),
        out_specs=VMEM,
        compiler_params=params(4),
        name="join",
    )(*blocks)


def packed_down(hidden, down_ref, out_ref, flat):
    count, wide = flat.shape[1:]
    tall = CAP * SEGMENTS
    for s in range(SEGMENTS):
        slot = flat.at[s % 2]
        slot[...] = jnp.dot(
            hidden, down_ref[:, s * wide : (s + 1) * wide], preferred_element_type=jnp.float32
        )
        for b in range(count // CAP):
            start = b * tall + s * CAP
            out_ref[start : start + CAP, :] = slot[b * CAP : (b + 1) * CAP, :]


def expert_kernel(own, *refs):
    blocks, joined = refs[:own], refs[own : own + own // (SPLIT // CORES)]
    gate_ref, up_ref, down_ref, given_ref, hidden_ref, packed, flat, out = refs[-8:]
    tall = CAP * SEGMENTS
    wide = packed.shape[1]
    units = gate_ref.shape[1]
    for b, ref in enumerate(blocks):
        packed[b * tall : (b + 1) * tall, :] = ref[...].astype(jnp.float32)
    start = own * tall
    for ref in joined:
        packed[start : start + ref.shape[0], :] = ref[...].astype(jnp.float32)
        start += ref.shape[0]
    count = 2 * own * CAP
    gate_act = jnp.zeros((count, units), jnp.float32)
    up_act = jnp.zeros((count, units), jnp.float32)
    for s in range(SEGMENTS):
        slot = flat.at[s % 2]
        for b in range(2 * own):
            start = b * tall + s * CAP
            slot[b * CAP : (b + 1) * CAP, :] = packed[start : start + CAP, :]
        rows = slot[...].astype(jnp.bfloat16)
        columns = slice(s * wide, (s + 1) * wide)
        gate_act += jnp.dot(rows, gate_ref[columns, :], preferred_element_type=jnp.float32)
        up_act += jnp.dot(rows, up_ref[columns, :], preferred_element_type=jnp.float32)
    hidden = (jax.nn.silu(gate_act) * up_act).astype(jnp.bfloat16)
    half = count // 2
    hidden_ref[...] = hidden[:half]
    packed_down(hidden[half:], down_ref, out, flat.at[:, :half, :])
    given_ref[...] = out[...].astype(jnp.bfloat16)


def expert_half(blocks, joined, w_gate, w_up, w_down):
    own = len(blocks)
    tall, wide = blocks[0].shape
    features, units = w_gate.shape
    rows = 2 * own * CAP
    return pl.pallas_call(
        functools.partial(expert_kernel, own),
        out_shape=[
            jax.ShapeDtypeStruct((own * tall, wide), jnp.bfloat16),
            jax.ShapeDtypeStruct((own * CAP, units), jnp.bfloat16),
        ],
        in_specs=[VMEM] * (own + len(joined) + 3),
        out_specs=[VMEM] * 2,
        scratch_shapes=[
            pltpu.VMEM((2 * own * tall, wide), jnp.float32),
            pltpu.VMEM((2, rows, wide), jnp.float32),
            pltpu.VMEM((own * tall, wide), jnp.float32),
        ],
        compiler_params=params(16 + own),
        cost_estimate=pl.CostEstimate(
            flops=5 * rows * units * features,
            bytes_accessed=6 * features * units,
            transcendentals=rows * units,
        ),
        name="expert_half",
    )(*blocks, *joined, w_gate, w_up, w_down)


def kept_kernel(hidden_ref, down_ref, kept_ref, flat):
    packed_down(hidden_ref[...], down_ref, kept_ref, flat)


def kept_half(hidden, w_down):
    count, units = hidden.shape
    features = w_down.shape[1]
    wide = features // SEGMENTS
    return pl.pallas_call(
        kept_kernel,
        out_shape=jax.ShapeDtypeStruct((count * SEGMENTS, wide), jnp.float32),
        in_specs=[VMEM] * 2,
        out_specs=VMEM,
        scratch_shapes=[pltpu.VMEM((2, count, wide), jnp.float32)],
        compiler_params=params(8 + count // 10),
        cost_estimate=pl.CostEstimate(
            flops=2 * count * units * features,
            bytes_accessed=2 * features * units,
            transcendentals=0,
        ),
        name="kept_half",
    )(hidden, w_down)


def add_kernel(kept_ref, taken_ref, *out_refs):
    tall = out_refs[0].shape[0]
    for b, out_ref in enumerate(out_refs):
        rows = slice(b * tall, (b + 1) * tall)
        total = kept_ref[rows, :] + taken_ref[rows, :].astype(jnp.float32)
        out_ref[...] = total.astype(out_ref.dtype)


def add_cores(kept, taken, teams, chips):
    shape = (CAP * SEGMENTS, kept.shape[1])
    outs = [
        jax.ShapeDtypeStruct(shape, jnp.bfloat16 if m else jnp.float32)
        for k in range(teams)
        for m in range(chips)
    ]
    return pl.pallas_call(
        add_kernel,
        out_shape=outs,
        in_specs=[VMEM] * 2,
        out_specs=[VMEM] * len(outs),
        compiler_params=params(4 + 4 * teams),
        name="add_cores",
    )(kept, taken)


def sum_kernel(*refs):
    total = refs[0][...]
    for ref in refs[1:-1]:
        total = total + ref[...].astype(jnp.float32)
    refs[-1][...] = total.astype(refs[-1].dtype)


def sum_blocks(blocks):
    return pl.pallas_call(
        sum_kernel,
        out_shape=jax.ShapeDtypeStruct(blocks[0].shape, jnp.bfloat16),
        in_specs=[VMEM] * len(blocks),
        out_specs=VMEM,
        compiler_params=params(4),
        name="sum_blocks",
    )(*blocks)


def blend_kernel(chips, weight_ref, *refs):
    out_ref = refs[-1]
    count, features = out_ref.shape
    wide = features // SEGMENTS
    own = refs[0][...]
    for ref in refs[1:chips]:
        own = own + ref[...].astype(jnp.float32)
    high = own.astype(jnp.bfloat16).astype(jnp.float32)
    terms = [high, own - high, high]
    for ref in refs[chips:-1]:
        terms += [ref[...].astype(jnp.float32)] * 2
    rows = jnp.concatenate(terms, axis=0).astype(jnp.bfloat16)
    total = jnp.dot(weight_ref[...], rows, preferred_element_type=jnp.float32)
    for s in range(SEGMENTS):
        out_ref[:, s * wide : (s + 1) * wide] = total[s * count : (s + 1) * count].astype(
            jnp.bfloat16
        )


def blend(weights, own_blocks, other_blocks, count):
    chips = len(own_blocks)
    features = own_blocks[0].shape[1] * SEGMENTS
    return pl.pallas_call(
        functools.partial(blend_kernel, chips),
        out_shape=jax.ShapeDtypeStruct((count, features), jnp.bfloat16),
        in_specs=[VMEM] * (1 + chips + len(other_blocks)),
        out_specs=VMEM,
        compiler_params=params(16),
        name="blend",
    )(weights, *own_blocks, *other_blocks)


def body(tokens, expert_ids, route_logits, w_gate, w_up, w_down):
    devices = lax.axis_size("expert")
    teams = devices // SPLIT
    chips = SPLIT // CORES
    other_core = [(i, i ^ 1) for i in range(devices)]
    other_chip = [[(i, i ^ (m * CORES)) for i in range(devices)] for m in range(chips)]
    ids = expert_ids.T
    packed = pack_rows(ids, tokens, teams)
    ids, logits, packed = lax.optimization_barrier((ids, route_logits.T, packed))
    weights = blend_weights(ids, logits, teams)
    arrived = [packed[0]]
    for k in range(1, teams):
        pairs = [(i, (i + k * SPLIT) % devices) for i in range(devices)]
        arrived.append(lax.ppermute(packed[k], "expert", pairs))
    *arrived[1:], weights = lax.optimization_barrier((*arrived[1:], weights))
    blocks, swapped = [], []
    for block in arrived:
        team = [block]
        for m in range(1, chips):
            team.append(lax.ppermute(block, "expert", other_chip[m]))
        blocks += team
        swapped.append(lax.ppermute(join(team), "expert", other_core))
    given, hidden = expert_half(blocks, swapped, w_gate, w_up, w_down)
    taken = lax.ppermute(given, "expert", other_core)
    kept = kept_half(hidden, w_down)
    parts = add_cores(kept, taken, teams, chips)
    others = []
    for k in range(1, teams):
        team = [parts[k * chips]]
        for m in range(1, chips):
            team.append(lax.ppermute(parts[k * chips + m], "expert", other_chip[m]))
        pairs = [(i, (i - k * SPLIT) % devices) for i in range(devices)]
        total, parts = lax.optimization_barrier((sum_blocks(team), parts))
        others.append(lax.ppermute(total, "expert", pairs))
    own = [parts[0]]
    for m in range(1, chips):
        own.append(lax.ppermute(parts[m], "expert", other_chip[m]))
    return blend(weights, own, others, tokens.shape[0])


def solution(mesh):
    placed = (
        P(("groups", "expert"), None),
        P(("groups", "expert"), None),
        P(("groups", "expert"), None),
        P(None, "expert"),
        P(None, "expert"),
        P("expert", None),
    )
    return jax.shard_map(
        body, mesh=mesh, in_specs=placed, out_specs=P(("groups", "expert"), None), check_vma=False
    )
```

```python
import functools

import jax
import jax.numpy as jnp
from jax import lax
from jax.experimental import pallas as pl
from jax.experimental.pallas import tpu as pltpu
from jax.sharding import PartitionSpec as P

SPLIT = 8
CAP = 5
CORES = 2
SEGMENTS = 8

route_scale = 2.5

VMEM = pl.BlockSpec(memory_space=pltpu.VMEM)
HBM = pl.BlockSpec(memory_space=pltpu.HBM)
MIB = 1024 * 1024


def hits(ids, mine, teams):
    count = ids.shape[1]
    row = lax.broadcasted_iota(jnp.int32, (8 * pl.cdiv(teams, 8), count), 0)
    wanted = lax.rem(mine + row, teams)
    hit = jnp.zeros(row.shape, jnp.int32)
    for j in range(ids.shape[0]):
        hit = hit + jnp.where(ids[j : j + 1, :] == wanted, 1, 0)
    hit = jnp.where(row < teams, hit, 0).astype(jnp.float32)
    before = lax.broadcasted_iota(jnp.int32, (count, count), 0)
    after = lax.broadcasted_iota(jnp.int32, (count, count), 1)
    earlier = jnp.where(before < after, 1.0, 0.0).astype(jnp.bfloat16)
    slot = jnp.dot(hit.astype(jnp.bfloat16), earlier, preferred_element_type=jnp.float32)
    return hit, jnp.where(hit > 0, slot, -1.0)


def fifth(shape, axis):
    at = lax.broadcasted_iota(jnp.int32, shape, axis)
    segment = jnp.zeros(shape, jnp.int32)
    for s in range(1, SEGMENTS):
        segment = segment + jnp.where(at >= s * CAP, 1, 0)
    return segment, (at - CAP * segment).astype(jnp.float32)


def params(mib):
    return pltpu.CompilerParams(vmem_limit_bytes=int(mib * MIB))


def bring(source, target, semaphores, parts):
    step = source.shape[0] // parts
    copies = []
    for i in range(parts):
        rows = pl.ds(i * step, step)
        copies.append(pltpu.make_async_copy(source.at[rows], target.at[rows], semaphores.at[i]))
        copies[-1].start()
    return copies


def wait_all(copies):
    for copy in copies:
        copy.wait()


def pack_kernel(teams, ids_hbm, logits_hbm, tokens_hbm, *refs):
    *out_refs, table_ref, ids_ref, logits_ref, tokens_ref, ids_sem, logits_sem, tokens_sem = refs
    ids_copy = bring(ids_hbm, ids_ref, ids_sem, 1)
    tokens_copy = bring(tokens_hbm, tokens_ref, tokens_sem, 4)
    logits_copy = bring(logits_hbm, logits_ref, logits_sem, 1)
    wait_all(ids_copy)
    mine = lax.axis_index("expert") // SPLIT
    ids = ids_ref[...]
    hit, slot = hits(ids, mine, teams)
    wait_all(logits_copy)
    lifted = jax.nn.sigmoid(logits_ref[...])
    gates = route_scale * lifted / jnp.sum(lifted, axis=0, keepdims=True)
    row = lax.broadcasted_iota(jnp.int32, hit.shape, 0)
    wanted = lax.rem(mine + row, teams)
    gate = jnp.zeros(hit.shape, jnp.float32)
    for j in range(ids.shape[0]):
        gate = gate + jnp.where(ids[j : j + 1, :] == wanted, gates[j : j + 1, :], 0.0)
    table_ref[: hit.shape[0], :] = slot
    table_ref[hit.shape[0] :, :] = gate
    count, features = tokens_ref.shape
    wide = features // SEGMENTS
    tall = CAP * SEGMENTS
    segment, place = fifth((tall, 1), 0)
    column = lax.broadcasted_iota(jnp.int32, (1, SEGMENTS * count), 1)
    same = segment == column // count
    picks = []
    for k in range(teams):
        slots = jnp.concatenate([slot[k : k + 1, :]] * SEGMENTS, axis=1)
        picks.append(jnp.where(same & (slots == place), 1.0, 0.0))
    wait_all(tokens_copy)
    stacked = jnp.concatenate(
        [tokens_ref[:, s * wide : (s + 1) * wide] for s in range(SEGMENTS)], axis=0
    )
    packed = jnp.dot(
        jnp.concatenate(picks, axis=0).astype(jnp.bfloat16),
        stacked,
        preferred_element_type=jnp.float32,
    )
    for k in range(teams):
        out_refs[k][...] = packed[k * tall : (k + 1) * tall].astype(jnp.bfloat16)


def pack_rows(ids, logits, tokens, teams):
    wide = tokens.shape[1] // SEGMENTS
    block = jax.ShapeDtypeStruct((CAP * SEGMENTS, wide), jnp.bfloat16)
    table = jax.ShapeDtypeStruct((16 * pl.cdiv(teams, 8), ids.shape[1]), jnp.float32)
    *packed, table = pl.pallas_call(
        functools.partial(pack_kernel, teams),
        out_shape=[block] * teams + [table],
        in_specs=[HBM] * 3,
        out_specs=[VMEM] * (teams + 1),
        scratch_shapes=[
            pltpu.VMEM(ids.shape, ids.dtype),
            pltpu.VMEM(logits.shape, logits.dtype),
            pltpu.VMEM(tokens.shape, tokens.dtype),
            pltpu.SemaphoreType.DMA((1,)),
            pltpu.SemaphoreType.DMA((1,)),
            pltpu.SemaphoreType.DMA((4,)),
        ],
        name="pack_rows",
    )(ids, logits, tokens)
    return packed, table


PARTS = 4


def load_kernel(teams, *refs):
    table_ref, *weights = refs[:4]
    out_ref, *held = refs[4:8]
    sem = refs[8]
    copies = []
    for i, (source, target) in enumerate(zip(weights, held)):
        copies += bring(source, target, sem.at[pl.ds(i * PARTS, PARTS)], PARTS)
    blend_matrix(teams, table_ref, out_ref)
    wait_all(copies)


def blend_matrix(teams, table_ref, out_ref):
    rows, count = table_ref.shape
    slot = jnp.transpose(table_ref[: rows // 2, :])
    gate = jnp.transpose(table_ref[rows // 2 :, :])
    tall = CAP * SEGMENTS
    depth = out_ref.shape[1]
    column = lax.broadcasted_iota(jnp.int32, (1, depth), 1)
    part = jnp.zeros((1, depth), jnp.int32)
    for g in range(1, depth // tall):
        part = part + jnp.where(column >= g * tall, 1, 0)
    column = column - tall * part
    segment = jnp.zeros((1, depth), jnp.int32)
    for s in range(1, SEGMENTS):
        segment = segment + jnp.where(column >= s * CAP, 1, 0)
    place = (column - CAP * segment).astype(jnp.float32)
    team = jnp.where(part < 3, 0, (part - 1) >> 1)
    low = jnp.where(part < 3, part >> 1, (part - 3) & 1) == 1
    for s in range(SEGMENTS):
        full = jnp.zeros((count, depth), jnp.float32)
        for k in range(teams):
            chosen = (team == k) & (segment == s) & (slot[:, k : k + 1] == place)
            full = full + jnp.where(chosen, gate[:, k : k + 1], 0.0)
        high = full.astype(jnp.bfloat16).astype(jnp.float32)
        out_ref[s * count : (s + 1) * count, :] = jnp.where(low, full - high, high).astype(
            jnp.bfloat16
        )


def load(table, weights, teams):
    shape = (SEGMENTS * table.shape[1], CAP * SEGMENTS * (1 + 2 * teams))
    return pl.pallas_call(
        functools.partial(load_kernel, teams),
        out_shape=[jax.ShapeDtypeStruct(shape, jnp.bfloat16)]
        + [jax.ShapeDtypeStruct(w.shape, w.dtype) for w in weights],
        in_specs=[VMEM] + [HBM] * len(weights),
        out_specs=[VMEM] * (1 + len(weights)),
        scratch_shapes=[pltpu.SemaphoreType.DMA((PARTS * len(weights),))],
        compiler_params=params(41),
        cost_estimate=pl.CostEstimate(
            flops=0, bytes_accessed=2 * sum(2 * w.size for w in weights), transcendentals=0
        ),
        name="load",
    )(table, *weights)


def join_kernel(*refs):
    tall = refs[0].shape[0]
    for i, ref in enumerate(refs[:-1]):
        refs[-1][i * tall : (i + 1) * tall, :] = ref[...]


def join(blocks):
    tall, wide = blocks[0].shape
    return pl.pallas_call(
        join_kernel,
        out_shape=jax.ShapeDtypeStruct((tall * len(blocks), wide), blocks[0].dtype),
        in_specs=[VMEM] * len(blocks),
        out_specs=VMEM,
        compiler_params=params(4),
        name="join",
    )(*blocks)


def packed_down(hidden, down_ref, out_ref, flat):
    count, wide = flat.shape[1:]
    tall = CAP * SEGMENTS
    for s in range(SEGMENTS):
        slot = flat.at[s % 2]
        slot[...] = jnp.dot(
            hidden, down_ref[:, s * wide : (s + 1) * wide], preferred_element_type=jnp.float32
        )
        for b in range(count // CAP):
            start = b * tall + s * CAP
            out_ref[start : start + CAP, :] = slot[b * CAP : (b + 1) * CAP, :]


def expert_kernel(own, *refs):
    blocks, joined = refs[:own], refs[own : own + own // (SPLIT // CORES)]
    gate_ref, up_ref, down_ref, given_ref, hidden_ref, packed, flat, out = refs[-8:]
    tall = CAP * SEGMENTS
    wide = packed.shape[1]
    units = gate_ref.shape[1]
    for b, ref in enumerate(blocks):
        packed[b * tall : (b + 1) * tall, :] = ref[...].astype(jnp.float32)
    start = own * tall
    for ref in joined:
        packed[start : start + ref.shape[0], :] = ref[...].astype(jnp.float32)
        start += ref.shape[0]
    count = 2 * own * CAP
    gate_act = jnp.zeros((count, units), jnp.float32)
    up_act = jnp.zeros((count, units), jnp.float32)
    for s in range(SEGMENTS):
        slot = flat.at[s % 2]
        for b in range(2 * own):
            start = b * tall + s * CAP
            slot[b * CAP : (b + 1) * CAP, :] = packed[start : start + CAP, :]
        rows = slot[...].astype(jnp.bfloat16)
        columns = slice(s * wide, (s + 1) * wide)
        gate_act += jnp.dot(rows, gate_ref[columns, :], preferred_element_type=jnp.float32)
        up_act += jnp.dot(rows, up_ref[columns, :], preferred_element_type=jnp.float32)
    hidden = (jax.nn.silu(gate_act) * up_act).astype(jnp.bfloat16)
    half = count // 2
    hidden_ref[...] = hidden[:half]
    packed_down(hidden[half:], down_ref, out, flat.at[:, :half, :])
    given_ref[...] = out[...].astype(jnp.bfloat16)


def expert_half(blocks, joined, w_gate, w_up, w_down):
    own = len(blocks)
    tall, wide = blocks[0].shape
    features, units = w_gate.shape
    rows = 2 * own * CAP
    return pl.pallas_call(
        functools.partial(expert_kernel, own),
        out_shape=[
            jax.ShapeDtypeStruct((own * tall, wide), jnp.bfloat16),
            jax.ShapeDtypeStruct((own * CAP, units), jnp.bfloat16),
        ],
        in_specs=[VMEM] * (own + len(joined) + 3),
        out_specs=[VMEM] * 2,
        scratch_shapes=[
            pltpu.VMEM((2 * own * tall, wide), jnp.float32),
            pltpu.VMEM((2, rows, wide), jnp.float32),
            pltpu.VMEM((own * tall, wide), jnp.float32),
        ],
        compiler_params=params(16 + own),
        cost_estimate=pl.CostEstimate(
            flops=5 * rows * units * features,
            bytes_accessed=6 * features * units,
            transcendentals=rows * units,
        ),
        name="expert_half",
    )(*blocks, *joined, w_gate, w_up, w_down)


def kept_kernel(hidden_ref, down_ref, kept_ref, flat):
    packed_down(hidden_ref[...], down_ref, kept_ref, flat)


def kept_half(hidden, w_down):
    count, units = hidden.shape
    features = w_down.shape[1]
    wide = features // SEGMENTS
    return pl.pallas_call(
        kept_kernel,
        out_shape=jax.ShapeDtypeStruct((count * SEGMENTS, wide), jnp.float32),
        in_specs=[VMEM] * 2,
        out_specs=VMEM,
        scratch_shapes=[pltpu.VMEM((2, count, wide), jnp.float32)],
        compiler_params=params(8 + count // 10),
        cost_estimate=pl.CostEstimate(
            flops=2 * count * units * features,
            bytes_accessed=2 * features * units,
            transcendentals=0,
        ),
        name="kept_half",
    )(hidden, w_down)


def add_kernel(kept_ref, taken_ref, *out_refs):
    tall = out_refs[0].shape[0]
    for b, out_ref in enumerate(out_refs):
        rows = slice(b * tall, (b + 1) * tall)
        total = kept_ref[rows, :] + taken_ref[rows, :].astype(jnp.float32)
        out_ref[...] = total.astype(out_ref.dtype)


def add_cores(kept, taken, teams, chips):
    shape = (CAP * SEGMENTS, kept.shape[1])
    outs = [
        jax.ShapeDtypeStruct(shape, jnp.bfloat16 if m else jnp.float32)
        for k in range(teams)
        for m in range(chips)
    ]
    return pl.pallas_call(
        add_kernel,
        out_shape=outs,
        in_specs=[VMEM] * 2,
        out_specs=[VMEM] * len(outs),
        compiler_params=params(4 + 4 * teams),
        name="add_cores",
    )(kept, taken)


def sum_kernel(*refs):
    total = refs[0][...]
    for ref in refs[1:-1]:
        total = total + ref[...].astype(jnp.float32)
    refs[-1][...] = total.astype(refs[-1].dtype)


def sum_blocks(blocks):
    return pl.pallas_call(
        sum_kernel,
        out_shape=jax.ShapeDtypeStruct(blocks[0].shape, jnp.bfloat16),
        in_specs=[VMEM] * len(blocks),
        out_specs=VMEM,
        compiler_params=params(4),
        name="sum_blocks",
    )(*blocks)


def blend_kernel(chips, weight_ref, *refs):
    *refs, out_hbm, out_ref, sem = refs
    count, features = out_ref.shape
    wide = features // SEGMENTS
    own = refs[0][...]
    for ref in refs[1:chips]:
        own = own + ref[...].astype(jnp.float32)
    high = own.astype(jnp.bfloat16).astype(jnp.float32)
    terms = [high, own - high, high]
    for ref in refs[chips:]:
        terms += [ref[...].astype(jnp.float32)] * 2
    rows = jnp.concatenate(terms, axis=0).astype(jnp.bfloat16)
    copies = []
    for s in range(SEGMENTS):
        columns = pl.ds(s * wide, wide)
        out_ref[:, columns] = jnp.dot(
            weight_ref[s * count : (s + 1) * count, :], rows, preferred_element_type=jnp.float32
        ).astype(jnp.bfloat16)
        copies.append(
            pltpu.make_async_copy(out_ref.at[:, columns], out_hbm.at[:, columns], sem.at[s])
        )
        copies[-1].start()
    wait_all(copies)


def blend(weights, own_blocks, other_blocks, count):
    chips = len(own_blocks)
    features = own_blocks[0].shape[1] * SEGMENTS
    return pl.pallas_call(
        functools.partial(blend_kernel, chips),
        out_shape=jax.ShapeDtypeStruct((count, features), jnp.bfloat16),
        in_specs=[VMEM] * (1 + chips + len(other_blocks)),
        out_specs=HBM,
        scratch_shapes=[
            pltpu.VMEM((count, features), jnp.bfloat16),
            pltpu.SemaphoreType.DMA((SEGMENTS,)),
        ],
        compiler_params=params(16),
        name="blend",
    )(weights, *own_blocks, *other_blocks)


def body(tokens, expert_ids, route_logits, w_gate, w_up, w_down):
    devices = lax.axis_size("expert")
    teams = devices // SPLIT
    chips = SPLIT // CORES
    other_core = [(i, i ^ 1) for i in range(devices)]
    other_chip = [[(i, i ^ (m * CORES)) for i in range(devices)] for m in range(chips)]
    packed, table = pack_rows(expert_ids.T, route_logits.T, tokens, teams)
    blocks, swapped = [], []
    for k in range(teams):
        block = packed[k]
        if k > 0:
            pairs = [(i, (i + k * SPLIT) % devices) for i in range(devices)]
            block = lax.ppermute(block, "expert", pairs)
        team = [block]
        for m in range(1, chips):
            team.append(lax.ppermute(block, "expert", other_chip[m]))
        if k == teams - 1:
            start = (table, w_gate, w_up, w_down)
            start, swapped = lax.optimization_barrier((start, swapped))
            held = load(start[0], start[1:], teams)
            team, (weights, w_gate, w_up, w_down) = lax.optimization_barrier((team, held))
        blocks += team
        joined = join(team)
        swapped.append(joined)
    swapped = [lax.ppermute(joined, "expert", other_core) for joined in swapped]
    given, hidden = expert_half(blocks, swapped, w_gate, w_up, w_down)
    taken = lax.ppermute(given, "expert", other_core)
    kept = kept_half(hidden, w_down)
    parts = add_cores(kept, taken, teams, chips)
    others = []
    for k in range(1, teams):
        team = [parts[k * chips]]
        for m in range(1, chips):
            team.append(lax.ppermute(parts[k * chips + m], "expert", other_chip[m]))
        pairs = [(i, (i - k * SPLIT) % devices) for i in range(devices)]
        others.append(lax.ppermute(sum_blocks(team), "expert", pairs))
    own = [parts[0]]
    for m in range(1, chips):
        own.append(lax.ppermute(parts[m], "expert", other_chip[m]))
    return blend(weights, own, others, tokens.shape[0])


def solution(mesh):
    placed = (
        P(("groups", "expert"), None),
        P(("groups", "expert"), None),
        P(("groups", "expert"), None),
        P(None, "expert"),
        P(None, "expert"),
        P("expert", None),
    )
    return jax.shard_map(
        body, mesh=mesh, in_specs=placed, out_specs=P(("groups", "expert"), None), check_vma=False
    )
```

```python
import functools

import jax
import jax.numpy as jnp
from jax import lax
from jax.experimental import pallas as pl
from jax.experimental.pallas import tpu as pltpu
from jax.sharding import PartitionSpec as P

SPLIT = 8
CAP = 5
CORES = 2
SEGMENTS = 8

route_scale = 2.5

VMEM = pl.BlockSpec(memory_space=pltpu.VMEM)
HBM = pl.BlockSpec(memory_space=pltpu.HBM)
MIB = 1024 * 1024


def hits(ids, mine, teams):
    count = ids.shape[1]
    row = lax.broadcasted_iota(jnp.int32, (8 * pl.cdiv(teams, 8), count), 0)
    wanted = lax.rem(mine + row, teams)
    hit = jnp.zeros(row.shape, jnp.int32)
    for j in range(ids.shape[0]):
        hit = hit + jnp.where(ids[j : j + 1, :] == wanted, 1, 0)
    hit = jnp.where(row < teams, hit, 0).astype(jnp.float32)
    before = lax.broadcasted_iota(jnp.int32, (count, count), 0)
    after = lax.broadcasted_iota(jnp.int32, (count, count), 1)
    earlier = jnp.where(before < after, 1.0, 0.0).astype(jnp.bfloat16)
    slot = jnp.dot(hit.astype(jnp.bfloat16), earlier, preferred_element_type=jnp.float32)
    return hit, jnp.where(hit > 0, slot, -1.0)


def fifth(shape, axis):
    at = lax.broadcasted_iota(jnp.int32, shape, axis)
    segment = jnp.zeros(shape, jnp.int32)
    for s in range(1, SEGMENTS):
        segment = segment + jnp.where(at >= s * CAP, 1, 0)
    return segment, (at - CAP * segment).astype(jnp.float32)


def params(mib):
    return pltpu.CompilerParams(vmem_limit_bytes=int(mib * MIB))


def bring(source, target, semaphores, parts):
    step = source.shape[0] // parts
    copies = []
    for i in range(parts):
        rows = pl.ds(i * step, step)
        copies.append(pltpu.make_async_copy(source.at[rows], target.at[rows], semaphores.at[i]))
        copies[-1].start()
    return copies


def wait_all(copies):
    for copy in copies:
        copy.wait()


def pack_kernel(teams, routes_ref, tokens_ref, *refs):
    *out_refs, table_ref = refs
    mine = lax.axis_index("expert") // SPLIT
    picks = routes_ref.shape[0] // 2
    ids = routes_ref[:picks, :].astype(jnp.int32)
    hit, slot = hits(ids, mine, teams)
    lifted = jax.nn.sigmoid(routes_ref[picks:, :])
    gates = route_scale * lifted / jnp.sum(lifted, axis=0, keepdims=True)
    row = lax.broadcasted_iota(jnp.int32, hit.shape, 0)
    wanted = lax.rem(mine + row, teams)
    gate = jnp.zeros(hit.shape, jnp.float32)
    for j in range(ids.shape[0]):
        gate = gate + jnp.where(ids[j : j + 1, :] == wanted, gates[j : j + 1, :], 0.0)
    table_ref[: hit.shape[0], :] = slot
    table_ref[hit.shape[0] :, :] = gate
    count, features = tokens_ref.shape
    wide = features // SEGMENTS
    tall = CAP * SEGMENTS
    segment, place = fifth((tall, 1), 0)
    column = lax.broadcasted_iota(jnp.int32, (1, SEGMENTS * count), 1)
    same = segment == column // count
    picks = []
    for k in range(teams):
        slots = jnp.concatenate([slot[k : k + 1, :]] * SEGMENTS, axis=1)
        picks.append(jnp.where(same & (slots == place), 1.0, 0.0))
    stacked = jnp.concatenate(
        [tokens_ref[:, s * wide : (s + 1) * wide] for s in range(SEGMENTS)], axis=0
    )
    packed = jnp.dot(
        jnp.concatenate(picks, axis=0).astype(jnp.bfloat16),
        stacked,
        preferred_element_type=jnp.float32,
    )
    for k in range(teams):
        out_refs[k][...] = packed[k * tall : (k + 1) * tall].astype(jnp.bfloat16)


def pack_rows(routes, tokens, teams):
    wide = tokens.shape[1] // SEGMENTS
    block = jax.ShapeDtypeStruct((CAP * SEGMENTS, wide), jnp.bfloat16)
    table = jax.ShapeDtypeStruct((16 * pl.cdiv(teams, 8), routes.shape[1]), jnp.float32)
    *packed, table = pl.pallas_call(
        functools.partial(pack_kernel, teams),
        out_shape=[block] * teams + [table],
        in_specs=[VMEM] * 2,
        out_specs=[VMEM] * (teams + 1),
        compiler_params=params(8),
        name="pack_rows",
    )(routes, tokens)
    return packed, table


def weight_kernel(teams, table_ref, out_ref):
    rows, count = table_ref.shape
    slot = jnp.transpose(table_ref[: rows // 2, :])
    gate = jnp.transpose(table_ref[rows // 2 :, :])
    tall = CAP * SEGMENTS
    depth = out_ref.shape[1]
    column = lax.broadcasted_iota(jnp.int32, (1, depth), 1)
    part = jnp.zeros((1, depth), jnp.int32)
    for g in range(1, depth // tall):
        part = part + jnp.where(column >= g * tall, 1, 0)
    column = column - tall * part
    segment = jnp.zeros((1, depth), jnp.int32)
    for s in range(1, SEGMENTS):
        segment = segment + jnp.where(column >= s * CAP, 1, 0)
    place = (column - CAP * segment).astype(jnp.float32)
    team = jnp.where(part < 3, 0, (part - 1) >> 1)
    low = jnp.where(part < 3, part >> 1, (part - 3) & 1) == 1
    for s in range(SEGMENTS):
        full = jnp.zeros((count, depth), jnp.float32)
        for k in range(teams):
            chosen = (team == k) & (segment == s) & (slot[:, k : k + 1] == place)
            full = full + jnp.where(chosen, gate[:, k : k + 1], 0.0)
        high = full.astype(jnp.bfloat16).astype(jnp.float32)
        out_ref[s * count : (s + 1) * count, :] = jnp.where(low, full - high, high).astype(
            jnp.bfloat16
        )


def blend_weights(table, teams):
    shape = (SEGMENTS * table.shape[1], CAP * SEGMENTS * (1 + 2 * teams))
    return pl.pallas_call(
        functools.partial(weight_kernel, teams),
        out_shape=jax.ShapeDtypeStruct(shape, jnp.bfloat16),
        in_specs=[VMEM],
        out_specs=VMEM,
        compiler_params=params(4 + teams),
        cost_estimate=pl.CostEstimate(flops=6 * 10**9, bytes_accessed=8 * MIB, transcendentals=0),
        name="blend_weights",
    )(table)


def join_kernel(*refs):
    tall = refs[0].shape[0]
    for i, ref in enumerate(refs[:-1]):
        refs[-1][i * tall : (i + 1) * tall, :] = ref[...]


def join(blocks):
    tall, wide = blocks[0].shape
    return pl.pallas_call(
        join_kernel,
        out_shape=jax.ShapeDtypeStruct((tall * len(blocks), wide), blocks[0].dtype),
        in_specs=[VMEM] * len(blocks),
        out_specs=VMEM,
        compiler_params=params(4),
        name="join",
    )(*blocks)


def packed_down(hidden, down_ref, out_ref, flat):
    count, wide = flat.shape[1:]
    tall = CAP * SEGMENTS
    for s in range(SEGMENTS):
        slot = flat.at[s % 2]
        slot[...] = jnp.dot(
            hidden, down_ref[:, s * wide : (s + 1) * wide], preferred_element_type=jnp.float32
        )
        for b in range(count // CAP):
            start = b * tall + s * CAP
            out_ref[start : start + CAP, :] = slot[b * CAP : (b + 1) * CAP, :]


def expert_kernel(own, *refs):
    blocks, joined = refs[:own], refs[own : own + own // (SPLIT // CORES)]
    gate_ref, up_ref, down_ref, given_ref, hidden_ref, packed, flat, out = refs[-8:]
    tall = CAP * SEGMENTS
    wide = packed.shape[1]
    units = gate_ref.shape[1]
    for b, ref in enumerate(blocks):
        packed[b * tall : (b + 1) * tall, :] = ref[...].astype(jnp.float32)
    start = own * tall
    for ref in joined:
        packed[start : start + ref.shape[0], :] = ref[...].astype(jnp.float32)
        start += ref.shape[0]
    count = 2 * own * CAP
    gate_act = jnp.zeros((count, units), jnp.float32)
    up_act = jnp.zeros((count, units), jnp.float32)
    for s in range(SEGMENTS):
        slot = flat.at[s % 2]
        for b in range(2 * own):
            start = b * tall + s * CAP
            slot[b * CAP : (b + 1) * CAP, :] = packed[start : start + CAP, :]
        rows = slot[...].astype(jnp.bfloat16)
        columns = slice(s * wide, (s + 1) * wide)
        gate_act += jnp.dot(rows, gate_ref[columns, :], preferred_element_type=jnp.float32)
        up_act += jnp.dot(rows, up_ref[columns, :], preferred_element_type=jnp.float32)
    hidden = (jax.nn.silu(gate_act) * up_act).astype(jnp.bfloat16)
    half = count // 2
    hidden_ref[...] = hidden[:half]
    packed_down(hidden[half:], down_ref, out, flat.at[:, :half, :])
    given_ref[...] = out[...].astype(jnp.bfloat16)


def expert_half(blocks, joined, w_gate, w_up, w_down):
    own = len(blocks)
    tall, wide = blocks[0].shape
    features, units = w_gate.shape
    rows = 2 * own * CAP
    return pl.pallas_call(
        functools.partial(expert_kernel, own),
        out_shape=[
            jax.ShapeDtypeStruct((own * tall, wide), jnp.bfloat16),
            jax.ShapeDtypeStruct((own * CAP, units), jnp.bfloat16),
        ],
        in_specs=[VMEM] * (own + len(joined) + 3),
        out_specs=[VMEM] * 2,
        scratch_shapes=[
            pltpu.VMEM((2 * own * tall, wide), jnp.float32),
            pltpu.VMEM((2, rows, wide), jnp.float32),
            pltpu.VMEM((own * tall, wide), jnp.float32),
        ],
        compiler_params=params(16 + own),
        cost_estimate=pl.CostEstimate(
            flops=5 * rows * units * features,
            bytes_accessed=6 * features * units,
            transcendentals=rows * units,
        ),
        name="expert_half",
    )(*blocks, *joined, w_gate, w_up, w_down)


def kept_kernel(hidden_ref, down_ref, kept_ref, flat):
    packed_down(hidden_ref[...], down_ref, kept_ref, flat)


def kept_half(hidden, w_down):
    count, units = hidden.shape
    features = w_down.shape[1]
    wide = features // SEGMENTS
    return pl.pallas_call(
        kept_kernel,
        out_shape=jax.ShapeDtypeStruct((count * SEGMENTS, wide), jnp.float32),
        in_specs=[VMEM] * 2,
        out_specs=VMEM,
        scratch_shapes=[pltpu.VMEM((2, count, wide), jnp.float32)],
        compiler_params=params(8 + count // 10),
        cost_estimate=pl.CostEstimate(
            flops=2 * count * units * features,
            bytes_accessed=2 * features * units,
            transcendentals=0,
        ),
        name="kept_half",
    )(hidden, w_down)


def add_kernel(kept_ref, taken_ref, *out_refs):
    tall = out_refs[0].shape[0]
    for b, out_ref in enumerate(out_refs):
        rows = slice(b * tall, (b + 1) * tall)
        total = kept_ref[rows, :] + taken_ref[rows, :].astype(jnp.float32)
        out_ref[...] = total.astype(out_ref.dtype)


def add_cores(kept, taken, teams, chips):
    shape = (CAP * SEGMENTS, kept.shape[1])
    outs = [
        jax.ShapeDtypeStruct(shape, jnp.bfloat16 if m else jnp.float32)
        for k in range(teams)
        for m in range(chips)
    ]
    return pl.pallas_call(
        add_kernel,
        out_shape=outs,
        in_specs=[VMEM] * 2,
        out_specs=[VMEM] * len(outs),
        compiler_params=params(4 + 4 * teams),
        name="add_cores",
    )(kept, taken)


def sum_kernel(*refs):
    total = refs[0][...]
    for ref in refs[1:-1]:
        total = total + ref[...].astype(jnp.float32)
    refs[-1][...] = total.astype(refs[-1].dtype)


def sum_blocks(blocks):
    return pl.pallas_call(
        sum_kernel,
        out_shape=jax.ShapeDtypeStruct(blocks[0].shape, jnp.bfloat16),
        in_specs=[VMEM] * len(blocks),
        out_specs=VMEM,
        compiler_params=params(4),
        name="sum_blocks",
    )(*blocks)


def settle_kernel(block_ref, out_ref):
    out_ref[...] = block_ref[...].astype(jnp.float32)


def settle(block):
    return pl.pallas_call(
        settle_kernel,
        out_shape=jax.ShapeDtypeStruct(block.shape, jnp.float32),
        in_specs=[VMEM],
        out_specs=VMEM,
        compiler_params=params(4),
        cost_estimate=pl.CostEstimate(flops=0, bytes_accessed=16 * MIB, transcendentals=0),
        name="settle",
    )(block)


def blend_kernel(chips, weight_ref, *refs):
    *refs, out_hbm, out_ref, sem = refs
    count, features = out_ref.shape
    wide = features // SEGMENTS
    own = refs[0][...]
    for ref in refs[1:chips]:
        own = own + ref[...].astype(jnp.float32)
    high = own.astype(jnp.bfloat16).astype(jnp.float32)
    terms = [high, own - high, high]
    for ref in refs[chips:]:
        terms += [ref[...]] * 2
    rows = jnp.concatenate(terms, axis=0).astype(jnp.bfloat16)
    copies = []
    for s in range(SEGMENTS):
        columns = pl.ds(s * wide, wide)
        out_ref[:, columns] = jnp.dot(
            weight_ref[s * count : (s + 1) * count, :], rows, preferred_element_type=jnp.float32
        ).astype(jnp.bfloat16)
        copies.append(
            pltpu.make_async_copy(out_ref.at[:, columns], out_hbm.at[:, columns], sem.at[s])
        )
        copies[-1].start()
    wait_all(copies)


def blend(weights, own_blocks, other_blocks, count):
    chips = len(own_blocks)
    features = own_blocks[0].shape[1] * SEGMENTS
    return pl.pallas_call(
        functools.partial(blend_kernel, chips),
        out_shape=jax.ShapeDtypeStruct((count, features), jnp.bfloat16),
        in_specs=[VMEM] * (1 + chips + len(other_blocks)),
        out_specs=HBM,
        scratch_shapes=[
            pltpu.VMEM((count, features), jnp.bfloat16),
            pltpu.SemaphoreType.DMA((SEGMENTS,)),
        ],
        compiler_params=params(16),
        name="blend",
    )(weights, *own_blocks, *other_blocks)


def body(tokens, expert_ids, route_logits, w_gate, w_up, w_down):
    devices = lax.axis_size("expert")
    teams = devices // SPLIT
    chips = SPLIT // CORES
    other_core = [(i, i ^ 1) for i in range(devices)]
    other_chip = [[(i, i ^ (m * CORES)) for i in range(devices)] for m in range(chips)]
    routes = jnp.concatenate([expert_ids.T.astype(jnp.float32), route_logits.T], axis=0)
    packed, table = pack_rows(routes, tokens, teams)
    crowds = []
    for k in range(teams):
        block = packed[k]
        if k > 0:
            pairs = [(i, (i + k * SPLIT) % devices) for i in range(devices)]
            block = lax.ppermute(block, "expert", pairs)
        if k == teams - 1:
            block, table = lax.optimization_barrier((block, table))
            weights = blend_weights(table, teams)
        team = [block]
        for m in range(1, chips):
            team.append(lax.ppermute(block, "expert", other_chip[m]))
        crowds.append(team)
    crowds[0], weights = lax.optimization_barrier((crowds[0], weights))
    blocks, joined = [], []
    for team in crowds:
        if joined:
            team, joined = lax.optimization_barrier((team, joined))
        blocks += team
        joined.append(join(team))
    swapped = [lax.ppermute(j, "expert", other_core) for j in joined]
    given, hidden = expert_half(blocks, swapped, w_gate, w_up, w_down)
    taken = lax.ppermute(given, "expert", other_core)
    kept = kept_half(hidden, w_down)
    parts = add_cores(kept, taken, teams, chips)
    others = []
    for k in range(1, teams):
        team = [parts[k * chips]]
        for m in range(1, chips):
            team.append(lax.ppermute(parts[k * chips + m], "expert", other_chip[m]))
        pairs = [(i, (i - k * SPLIT) % devices) for i in range(devices)]
        total, parts = lax.optimization_barrier((sum_blocks(team), parts))
        others.append(settle(lax.ppermute(total, "expert", pairs)))
    own = [parts[0]]
    for m in range(1, chips):
        own.append(lax.ppermute(parts[m], "expert", other_chip[m]))
    return blend(weights, own, others, tokens.shape[0])


def solution(mesh):
    placed = (
        P(("groups", "expert"), None),
        P(("groups", "expert"), None),
        P(("groups", "expert"), None),
        P(None, "expert"),
        P(None, "expert"),
        P("expert", None),
    )
    return jax.shard_map(
        body, mesh=mesh, in_specs=placed, out_specs=P(("groups", "expert"), None), check_vma=False
    )
```

```python
import functools

import jax
import jax.numpy as jnp
from jax import lax
from jax.experimental import pallas as pl
from jax.experimental.pallas import tpu as pltpu
from jax.sharding import PartitionSpec as P

SPLIT = 8
CAP = 5
CORES = 2
SEGMENTS = 8

route_scale = 2.5

VMEM = pl.BlockSpec(memory_space=pltpu.VMEM)
HBM = pl.BlockSpec(memory_space=pltpu.HBM)
MIB = 1024 * 1024


def hits(ids, mine, teams):
    count = ids.shape[1]
    row = lax.broadcasted_iota(jnp.int32, (8 * pl.cdiv(teams, 8), count), 0)
    wanted = lax.rem(mine + row, teams)
    hit = jnp.zeros(row.shape, jnp.int32)
    for j in range(ids.shape[0]):
        hit = hit + jnp.where(ids[j : j + 1, :] == wanted, 1, 0)
    hit = jnp.where(row < teams, hit, 0).astype(jnp.float32)
    before = lax.broadcasted_iota(jnp.int32, (count, count), 0)
    after = lax.broadcasted_iota(jnp.int32, (count, count), 1)
    earlier = jnp.where(before < after, 1.0, 0.0).astype(jnp.bfloat16)
    slot = jnp.dot(hit.astype(jnp.bfloat16), earlier, preferred_element_type=jnp.float32)
    return hit, jnp.where(hit > 0, slot, -1.0)


def fifth(shape, axis):
    at = lax.broadcasted_iota(jnp.int32, shape, axis)
    segment = jnp.zeros(shape, jnp.int32)
    for s in range(1, SEGMENTS):
        segment = segment + jnp.where(at >= s * CAP, 1, 0)
    return segment, (at - CAP * segment).astype(jnp.float32)


def params(mib):
    return pltpu.CompilerParams(vmem_limit_bytes=int(mib * MIB))


def bring(source, target, semaphores, parts):
    step = source.shape[0] // parts
    copies = []
    for i in range(parts):
        rows = pl.ds(i * step, step)
        copies.append(pltpu.make_async_copy(source.at[rows], target.at[rows], semaphores.at[i]))
        copies[-1].start()
    return copies


def wait_all(copies):
    for copy in copies:
        copy.wait()


def pack_kernel(teams, ids_hbm, logits_hbm, tokens_hbm, *refs):
    *out_refs, table_ref, ids_ref, logits_ref, tokens_ref, ids_sem, logits_sem, tokens_sem = refs
    ids_copy = bring(ids_hbm, ids_ref, ids_sem, 1)
    tokens_copy = bring(tokens_hbm, tokens_ref, tokens_sem, 4)
    logits_copy = bring(logits_hbm, logits_ref, logits_sem, 1)
    wait_all(ids_copy)
    mine = lax.axis_index("expert") // SPLIT
    ids = ids_ref[...]
    hit, slot = hits(ids, mine, teams)
    wait_all(logits_copy)
    lifted = jax.nn.sigmoid(logits_ref[...])
    gates = route_scale * lifted / jnp.sum(lifted, axis=0, keepdims=True)
    row = lax.broadcasted_iota(jnp.int32, hit.shape, 0)
    wanted = lax.rem(mine + row, teams)
    gate = jnp.zeros(hit.shape, jnp.float32)
    for j in range(ids.shape[0]):
        gate = gate + jnp.where(ids[j : j + 1, :] == wanted, gates[j : j + 1, :], 0.0)
    table_ref[: hit.shape[0], :] = slot
    table_ref[hit.shape[0] :, :] = gate
    count, features = tokens_ref.shape
    wide = features // SEGMENTS
    tall = CAP * SEGMENTS
    segment, place = fifth((tall, 1), 0)
    column = lax.broadcasted_iota(jnp.int32, (1, SEGMENTS * count), 1)
    same = segment == column // count
    picks = []
    for k in range(teams):
        slots = jnp.concatenate([slot[k : k + 1, :]] * SEGMENTS, axis=1)
        picks.append(jnp.where(same & (slots == place), 1.0, 0.0))
    wait_all(tokens_copy)
    stacked = jnp.concatenate(
        [tokens_ref[:, s * wide : (s + 1) * wide] for s in range(SEGMENTS)], axis=0
    )
    packed = jnp.dot(
        jnp.concatenate(picks, axis=0).astype(jnp.bfloat16),
        stacked,
        preferred_element_type=jnp.float32,
    )
    for k in range(teams):
        out_refs[k][...] = packed[k * tall : (k + 1) * tall].astype(jnp.bfloat16)


def pack_rows(ids, logits, tokens, teams):
    wide = tokens.shape[1] // SEGMENTS
    block = jax.ShapeDtypeStruct((CAP * SEGMENTS, wide), jnp.bfloat16)
    table = jax.ShapeDtypeStruct((16 * pl.cdiv(teams, 8), ids.shape[1]), jnp.float32)
    *packed, table = pl.pallas_call(
        functools.partial(pack_kernel, teams),
        out_shape=[block] * teams + [table],
        in_specs=[HBM] * 3,
        out_specs=[VMEM] * (teams + 1),
        scratch_shapes=[
            pltpu.VMEM(ids.shape, ids.dtype),
            pltpu.VMEM(logits.shape, logits.dtype),
            pltpu.VMEM(tokens.shape, tokens.dtype),
            pltpu.SemaphoreType.DMA((1,)),
            pltpu.SemaphoreType.DMA((1,)),
            pltpu.SemaphoreType.DMA((4,)),
        ],
        name="pack_rows",
    )(ids, logits, tokens)
    return packed, table


def weight_kernel(teams, table_ref, out_ref):
    rows, count = table_ref.shape
    slot = jnp.transpose(table_ref[: rows // 2, :])
    gate = jnp.transpose(table_ref[rows // 2 :, :])
    tall = CAP * SEGMENTS
    depth = out_ref.shape[1]
    column = lax.broadcasted_iota(jnp.int32, (1, depth), 1)
    part = jnp.zeros((1, depth), jnp.int32)
    for g in range(1, depth // tall):
        part = part + jnp.where(column >= g * tall, 1, 0)
    column = column - tall * part
    segment = jnp.zeros((1, depth), jnp.int32)
    for s in range(1, SEGMENTS):
        segment = segment + jnp.where(column >= s * CAP, 1, 0)
    place = (column - CAP * segment).astype(jnp.float32)
    team = jnp.where(part < 3, 0, (part - 1) >> 1)
    low = jnp.where(part < 3, part >> 1, (part - 3) & 1) == 1
    for s in range(SEGMENTS):
        full = jnp.zeros((count, depth), jnp.float32)
        for k in range(teams):
            chosen = (team == k) & (segment == s) & (slot[:, k : k + 1] == place)
            full = full + jnp.where(chosen, gate[:, k : k + 1], 0.0)
        high = full.astype(jnp.bfloat16).astype(jnp.float32)
        out_ref[s * count : (s + 1) * count, :] = jnp.where(low, full - high, high).astype(
            jnp.bfloat16
        )


def blend_weights(table, teams):
    shape = (SEGMENTS * table.shape[1], CAP * SEGMENTS * (1 + 2 * teams))
    return pl.pallas_call(
        functools.partial(weight_kernel, teams),
        out_shape=jax.ShapeDtypeStruct(shape, jnp.bfloat16),
        in_specs=[VMEM],
        out_specs=VMEM,
        compiler_params=params(4 + teams),
        cost_estimate=pl.CostEstimate(flops=6 * 10**9, bytes_accessed=8 * MIB, transcendentals=0),
        name="blend_weights",
    )(table)


def join_kernel(*refs):
    tall = refs[0].shape[0]
    for i, ref in enumerate(refs[:-1]):
        refs[-1][i * tall : (i + 1) * tall, :] = ref[...]


def join(blocks):
    tall, wide = blocks[0].shape
    return pl.pallas_call(
        join_kernel,
        out_shape=jax.ShapeDtypeStruct((tall * len(blocks), wide), blocks[0].dtype),
        in_specs=[VMEM] * len(blocks),
        out_specs=VMEM,
        compiler_params=params(4),
        name="join",
    )(*blocks)


def packed_down(hidden, down_ref, out_ref, flat):
    count, wide = flat.shape[1:]
    tall = CAP * SEGMENTS
    for s in range(SEGMENTS):
        slot = flat.at[s % 2]
        slot[...] = jnp.dot(
            hidden, down_ref[:, s * wide : (s + 1) * wide], preferred_element_type=jnp.float32
        )
        for b in range(count // CAP):
            start = b * tall + s * CAP
            out_ref[start : start + CAP, :] = slot[b * CAP : (b + 1) * CAP, :]


def expert_kernel(own, *refs):
    blocks, joined = refs[:own], refs[own : own + own // (SPLIT // CORES)]
    gate_ref, up_ref, down_ref, given_ref, hidden_ref, packed, flat, out = refs[-8:]
    tall = CAP * SEGMENTS
    wide = packed.shape[1]
    units = gate_ref.shape[1]
    for b, ref in enumerate(blocks):
        packed[b * tall : (b + 1) * tall, :] = ref[...].astype(jnp.float32)
    start = own * tall
    for ref in joined:
        packed[start : start + ref.shape[0], :] = ref[...].astype(jnp.float32)
        start += ref.shape[0]
    count = 2 * own * CAP
    gate_act = jnp.zeros((count, units), jnp.float32)
    up_act = jnp.zeros((count, units), jnp.float32)
    for s in range(SEGMENTS):
        slot = flat.at[s % 2]
        for b in range(2 * own):
            start = b * tall + s * CAP
            slot[b * CAP : (b + 1) * CAP, :] = packed[start : start + CAP, :]
        rows = slot[...].astype(jnp.bfloat16)
        columns = slice(s * wide, (s + 1) * wide)
        gate_act += jnp.dot(rows, gate_ref[columns, :], preferred_element_type=jnp.float32)
        up_act += jnp.dot(rows, up_ref[columns, :], preferred_element_type=jnp.float32)
    hidden = (jax.nn.silu(gate_act) * up_act).astype(jnp.bfloat16)
    half = count // 2
    hidden_ref[...] = hidden[:half]
    packed_down(hidden[half:], down_ref, out, flat.at[:, :half, :])
    given_ref[...] = out[...].astype(jnp.bfloat16)


def expert_half(blocks, joined, w_gate, w_up, w_down):
    own = len(blocks)
    tall, wide = blocks[0].shape
    features, units = w_gate.shape
    rows = 2 * own * CAP
    return pl.pallas_call(
        functools.partial(expert_kernel, own),
        out_shape=[
            jax.ShapeDtypeStruct((own * tall, wide), jnp.bfloat16),
            jax.ShapeDtypeStruct((own * CAP, units), jnp.bfloat16),
        ],
        in_specs=[VMEM] * (own + len(joined) + 3),
        out_specs=[VMEM] * 2,
        scratch_shapes=[
            pltpu.VMEM((2 * own * tall, wide), jnp.float32),
            pltpu.VMEM((2, rows, wide), jnp.float32),
            pltpu.VMEM((own * tall, wide), jnp.float32),
        ],
        compiler_params=params(16 + own),
        cost_estimate=pl.CostEstimate(
            flops=5 * rows * units * features,
            bytes_accessed=6 * features * units,
            transcendentals=rows * units,
        ),
        name="expert_half",
    )(*blocks, *joined, w_gate, w_up, w_down)


def kept_kernel(hidden_ref, down_ref, kept_ref, flat):
    packed_down(hidden_ref[...], down_ref, kept_ref, flat)


def kept_half(hidden, w_down):
    count, units = hidden.shape
    features = w_down.shape[1]
    wide = features // SEGMENTS
    return pl.pallas_call(
        kept_kernel,
        out_shape=jax.ShapeDtypeStruct((count * SEGMENTS, wide), jnp.float32),
        in_specs=[VMEM] * 2,
        out_specs=VMEM,
        scratch_shapes=[pltpu.VMEM((2, count, wide), jnp.float32)],
        compiler_params=params(8 + count // 10),
        cost_estimate=pl.CostEstimate(
            flops=2 * count * units * features,
            bytes_accessed=2 * features * units,
            transcendentals=0,
        ),
        name="kept_half",
    )(hidden, w_down)


def add_kernel(kept_ref, taken_ref, *out_refs):
    tall = out_refs[0].shape[0]
    for b, out_ref in enumerate(out_refs):
        rows = slice(b * tall, (b + 1) * tall)
        total = kept_ref[rows, :] + taken_ref[rows, :].astype(jnp.float32)
        out_ref[...] = total.astype(out_ref.dtype)


def add_cores(kept, taken, teams, chips):
    shape = (CAP * SEGMENTS, kept.shape[1])
    outs = [
        jax.ShapeDtypeStruct(shape, jnp.bfloat16 if m else jnp.float32)
        for k in range(teams)
        for m in range(chips)
    ]
    return pl.pallas_call(
        add_kernel,
        out_shape=outs,
        in_specs=[VMEM] * 2,
        out_specs=[VMEM] * len(outs),
        compiler_params=params(4 + 4 * teams),
        name="add_cores",
    )(kept, taken)


def sum_kernel(*refs):
    total = refs[0][...]
    for ref in refs[1:-1]:
        total = total + ref[...].astype(jnp.float32)
    refs[-1][...] = total.astype(refs[-1].dtype)


def sum_blocks(blocks):
    return pl.pallas_call(
        sum_kernel,
        out_shape=jax.ShapeDtypeStruct(blocks[0].shape, jnp.bfloat16),
        in_specs=[VMEM] * len(blocks),
        out_specs=VMEM,
        compiler_params=params(4),
        name="sum_blocks",
    )(*blocks)


def blend_kernel(chips, weight_ref, *refs):
    *refs, out_hbm, out_ref, sem = refs
    count, features = out_ref.shape
    wide = features // SEGMENTS
    own = refs[0][...]
    for ref in refs[1:chips]:
        own = own + ref[...].astype(jnp.float32)
    high = own.astype(jnp.bfloat16).astype(jnp.float32)
    terms = [high, own - high, high]
    for ref in refs[chips:]:
        terms += [ref[...].astype(jnp.float32)] * 2
    rows = jnp.concatenate(terms, axis=0).astype(jnp.bfloat16)
    copies = []
    for s in range(SEGMENTS):
        columns = pl.ds(s * wide, wide)
        out_ref[:, columns] = jnp.dot(
            weight_ref[s * count : (s + 1) * count, :], rows, preferred_element_type=jnp.float32
        ).astype(jnp.bfloat16)
        copies.append(
            pltpu.make_async_copy(out_ref.at[:, columns], out_hbm.at[:, columns], sem.at[s])
        )
        copies[-1].start()
    wait_all(copies)


def blend(weights, own_blocks, other_blocks, count):
    chips = len(own_blocks)
    features = own_blocks[0].shape[1] * SEGMENTS
    return pl.pallas_call(
        functools.partial(blend_kernel, chips),
        out_shape=jax.ShapeDtypeStruct((count, features), jnp.bfloat16),
        in_specs=[VMEM] * (1 + chips + len(other_blocks)),
        out_specs=HBM,
        scratch_shapes=[
            pltpu.VMEM((count, features), jnp.bfloat16),
            pltpu.SemaphoreType.DMA((SEGMENTS,)),
        ],
        compiler_params=params(16),
        name="blend",
    )(weights, *own_blocks, *other_blocks)


def body(tokens, expert_ids, route_logits, w_gate, w_up, w_down):
    devices = lax.axis_size("expert")
    teams = devices // SPLIT
    chips = SPLIT // CORES
    other_core = [(i, i ^ 1) for i in range(devices)]
    other_chip = [[(i, i ^ (m * CORES)) for i in range(devices)] for m in range(chips)]
    packed, table = pack_rows(expert_ids.T, route_logits.T, tokens, teams)
    crowds = []
    for k in range(teams):
        block = packed[k]
        if k > 0:
            pairs = [(i, (i + k * SPLIT) % devices) for i in range(devices)]
            block = lax.ppermute(block, "expert", pairs)
        if k == teams - 1:
            block, table = lax.optimization_barrier((block, table))
            weights = blend_weights(table, teams)
        team = [block]
        for m in range(1, chips):
            team.append(lax.ppermute(block, "expert", other_chip[m]))
        crowds.append(team)
    crowds[0], weights = lax.optimization_barrier((crowds[0], weights))
    blocks, joined = [], []
    for team in crowds:
        if joined:
            team, joined = lax.optimization_barrier((team, joined))
        blocks += team
        joined.append(join(team))
    swapped = [lax.ppermute(j, "expert", other_core) for j in joined]
    given, hidden = expert_half(blocks, swapped, w_gate, w_up, w_down)
    taken = lax.ppermute(given, "expert", other_core)
    kept = kept_half(hidden, w_down)
    parts = add_cores(kept, taken, teams, chips)
    others = []
    for k in range(1, teams):
        team = [parts[k * chips]]
        for m in range(1, chips):
            team.append(lax.ppermute(parts[k * chips + m], "expert", other_chip[m]))
        pairs = [(i, (i - k * SPLIT) % devices) for i in range(devices)]
        others.append(lax.ppermute(sum_blocks(team), "expert", pairs))
    own = [parts[0]]
    for m in range(1, chips):
        own.append(lax.ppermute(parts[m], "expert", other_chip[m]))
    return blend(weights, own, others, tokens.shape[0])


def solution(mesh):
    placed = (
        P(("groups", "expert"), None),
        P(("groups", "expert"), None),
        P(("groups", "expert"), None),
        P(None, "expert"),
        P(None, "expert"),
        P("expert", None),
    )
    return jax.shard_map(
        body, mesh=mesh, in_specs=placed, out_specs=P(("groups", "expert"), None), check_vma=False
    )
```

```python
import functools

import jax
import jax.numpy as jnp
from jax import lax
from jax.experimental import pallas as pl
from jax.experimental.pallas import tpu as pltpu
from jax.sharding import PartitionSpec as P

SPLIT = 8
CAP = 5
CORES = 2
SEGMENTS = 8

route_scale = 2.5

VMEM = pl.BlockSpec(memory_space=pltpu.VMEM)
HBM = pl.BlockSpec(memory_space=pltpu.HBM)
MIB = 1024 * 1024


def hits(ids, mine, teams):
    count = ids.shape[1]
    row = lax.broadcasted_iota(jnp.int32, (8 * pl.cdiv(teams, 8), count), 0)
    wanted = lax.rem(mine + row, teams)
    hit = jnp.zeros(row.shape, jnp.int32)
    for j in range(ids.shape[0]):
        hit = hit + jnp.where(ids[j : j + 1, :] == wanted, 1, 0)
    hit = jnp.where(row < teams, hit, 0).astype(jnp.float32)
    before = lax.broadcasted_iota(jnp.int32, (count, count), 0)
    after = lax.broadcasted_iota(jnp.int32, (count, count), 1)
    earlier = jnp.where(before < after, 1.0, 0.0).astype(jnp.bfloat16)
    slot = jnp.dot(hit.astype(jnp.bfloat16), earlier, preferred_element_type=jnp.float32)
    return hit, jnp.where(hit > 0, slot, -1.0)


def fifth(shape, axis):
    at = lax.broadcasted_iota(jnp.int32, shape, axis)
    segment = jnp.zeros(shape, jnp.int32)
    for s in range(1, SEGMENTS):
        segment = segment + jnp.where(at >= s * CAP, 1, 0)
    return segment, (at - CAP * segment).astype(jnp.float32)


def params(mib):
    return pltpu.CompilerParams(vmem_limit_bytes=int(mib * MIB))


def bring(source, target, semaphores, parts):
    step = source.shape[0] // parts
    copies = []
    for i in range(parts):
        rows = pl.ds(i * step, step)
        copies.append(pltpu.make_async_copy(source.at[rows], target.at[rows], semaphores.at[i]))
        copies[-1].start()
    return copies


def wait_all(copies):
    for copy in copies:
        copy.wait()


def pack_kernel(teams, ids_hbm, logits_hbm, tokens_hbm, *refs):
    *out_refs, table_ref, ids_ref, logits_ref, tokens_ref, ids_sem, logits_sem, tokens_sem = refs
    ids_copy = bring(ids_hbm, ids_ref, ids_sem, 1)
    tokens_copy = bring(tokens_hbm, tokens_ref, tokens_sem, 4)
    logits_copy = bring(logits_hbm, logits_ref, logits_sem, 1)
    wait_all(ids_copy)
    mine = lax.axis_index("expert") // SPLIT
    ids = ids_ref[...]
    hit, slot = hits(ids, mine, teams)
    wait_all(logits_copy)
    lifted = jax.nn.sigmoid(logits_ref[...])
    gates = route_scale * lifted / jnp.sum(lifted, axis=0, keepdims=True)
    row = lax.broadcasted_iota(jnp.int32, hit.shape, 0)
    wanted = lax.rem(mine + row, teams)
    gate = jnp.zeros(hit.shape, jnp.float32)
    for j in range(ids.shape[0]):
        gate = gate + jnp.where(ids[j : j + 1, :] == wanted, gates[j : j + 1, :], 0.0)
    table_ref[: hit.shape[0], :] = slot
    table_ref[hit.shape[0] :, :] = gate
    count, features = tokens_ref.shape
    wide = features // SEGMENTS
    tall = CAP * SEGMENTS
    segment, place = fifth((tall, 1), 0)
    column = lax.broadcasted_iota(jnp.int32, (1, SEGMENTS * count), 1)
    same = segment == column // count
    picks = []
    for k in range(teams):
        slots = jnp.concatenate([slot[k : k + 1, :]] * SEGMENTS, axis=1)
        picks.append(jnp.where(same & (slots == place), 1.0, 0.0))
    wait_all(tokens_copy)
    stacked = jnp.concatenate(
        [tokens_ref[:, s * wide : (s + 1) * wide] for s in range(SEGMENTS)], axis=0
    )
    packed = jnp.dot(
        jnp.concatenate(picks, axis=0).astype(jnp.bfloat16),
        stacked,
        preferred_element_type=jnp.float32,
    )
    for k in range(teams):
        out_refs[k][...] = packed[k * tall : (k + 1) * tall].astype(jnp.bfloat16)


def pack_rows(ids, logits, tokens, teams):
    wide = tokens.shape[1] // SEGMENTS
    block = jax.ShapeDtypeStruct((CAP * SEGMENTS, wide), jnp.bfloat16)
    table = jax.ShapeDtypeStruct((16 * pl.cdiv(teams, 8), ids.shape[1]), jnp.float32)
    *packed, table = pl.pallas_call(
        functools.partial(pack_kernel, teams),
        out_shape=[block] * teams + [table],
        in_specs=[HBM] * 3,
        out_specs=[VMEM] * (teams + 1),
        scratch_shapes=[
            pltpu.VMEM(ids.shape, ids.dtype),
            pltpu.VMEM(logits.shape, logits.dtype),
            pltpu.VMEM(tokens.shape, tokens.dtype),
            pltpu.SemaphoreType.DMA((1,)),
            pltpu.SemaphoreType.DMA((1,)),
            pltpu.SemaphoreType.DMA((4,)),
        ],
        name="pack_rows",
    )(ids, logits, tokens)
    return packed, table


def weight_kernel(teams, table_ref, out_ref):
    rows, count = table_ref.shape
    slot = jnp.transpose(table_ref[: rows // 2, :])
    gate = jnp.transpose(table_ref[rows // 2 :, :])
    tall = CAP * SEGMENTS
    depth = out_ref.shape[1]
    column = lax.broadcasted_iota(jnp.int32, (1, depth), 1)
    part = jnp.zeros((1, depth), jnp.int32)
    for g in range(1, depth // tall):
        part = part + jnp.where(column >= g * tall, 1, 0)
    column = column - tall * part
    segment = jnp.zeros((1, depth), jnp.int32)
    for s in range(1, SEGMENTS):
        segment = segment + jnp.where(column >= s * CAP, 1, 0)
    place = (column - CAP * segment).astype(jnp.float32)
    team = jnp.where(part < 3, 0, (part - 1) >> 1)
    low = jnp.where(part < 3, part >> 1, (part - 3) & 1) == 1
    for s in range(SEGMENTS):
        full = jnp.zeros((count, depth), jnp.float32)
        for k in range(teams):
            chosen = (team == k) & (segment == s) & (slot[:, k : k + 1] == place)
            full = full + jnp.where(chosen, gate[:, k : k + 1], 0.0)
        high = full.astype(jnp.bfloat16).astype(jnp.float32)
        out_ref[s * count : (s + 1) * count, :] = jnp.where(low, full - high, high).astype(
            jnp.bfloat16
        )


def blend_weights(table, teams):
    shape = (SEGMENTS * table.shape[1], CAP * SEGMENTS * (1 + 2 * teams))
    return pl.pallas_call(
        functools.partial(weight_kernel, teams),
        out_shape=jax.ShapeDtypeStruct(shape, jnp.bfloat16),
        in_specs=[VMEM],
        out_specs=VMEM,
        compiler_params=params(4 + teams),
        cost_estimate=pl.CostEstimate(flops=6 * 10**9, bytes_accessed=8 * MIB, transcendentals=0),
        name="blend_weights",
    )(table)


def spread_kernel(block_ref, out_ref):
    tall = block_ref.shape[0]
    for q in range(out_ref.shape[0] // tall):
        out_ref[q * tall : (q + 1) * tall, :] = block_ref[...]


def spread(block, copies):
    tall, wide = block.shape
    return pl.pallas_call(
        spread_kernel,
        out_shape=jax.ShapeDtypeStruct((tall * copies, wide), block.dtype),
        in_specs=[VMEM],
        out_specs=VMEM,
        compiler_params=params(4),
        name="spread",
    )(block)


def join_kernel(*refs):
    tall = refs[0].shape[0]
    for i, ref in enumerate(refs[:-1]):
        refs[-1][i * tall : (i + 1) * tall, :] = ref[...]


def join(blocks):
    tall, wide = blocks[0].shape
    return pl.pallas_call(
        join_kernel,
        out_shape=jax.ShapeDtypeStruct((tall * len(blocks), wide), blocks[0].dtype),
        in_specs=[VMEM] * len(blocks),
        out_specs=VMEM,
        compiler_params=params(4),
        name="join",
    )(*blocks)


def packed_down(hidden, down_ref, out_ref, flat):
    count, wide = flat.shape[1:]
    tall = CAP * SEGMENTS
    for s in range(SEGMENTS):
        slot = flat.at[s % 2]
        slot[...] = jnp.dot(
            hidden, down_ref[:, s * wide : (s + 1) * wide], preferred_element_type=jnp.float32
        )
        for b in range(count // CAP):
            start = b * tall + s * CAP
            out_ref[start : start + CAP, :] = slot[b * CAP : (b + 1) * CAP, :]


def expert_kernel(own, *refs):
    pieces = refs[:-8]
    gate_ref, up_ref, down_ref, given_ref, hidden_ref, packed, flat, out = refs[-8:]
    tall = CAP * SEGMENTS
    wide = packed.shape[1]
    units = gate_ref.shape[1]
    start = 0
    for ref in pieces:
        packed[start : start + ref.shape[0], :] = ref[...].astype(jnp.float32)
        start += ref.shape[0]
    count = 2 * own * CAP
    gate_act = jnp.zeros((count, units), jnp.float32)
    up_act = jnp.zeros((count, units), jnp.float32)
    for s in range(SEGMENTS):
        slot = flat.at[s % 2]
        for b in range(2 * own):
            start = b * tall + s * CAP
            slot[b * CAP : (b + 1) * CAP, :] = packed[start : start + CAP, :]
        rows = slot[...].astype(jnp.bfloat16)
        columns = slice(s * wide, (s + 1) * wide)
        gate_act += jnp.dot(rows, gate_ref[columns, :], preferred_element_type=jnp.float32)
        up_act += jnp.dot(rows, up_ref[columns, :], preferred_element_type=jnp.float32)
    hidden = (jax.nn.silu(gate_act) * up_act).astype(jnp.bfloat16)
    half = count // 2
    hidden_ref[...] = hidden[:half]
    packed_down(hidden[half:], down_ref, out, flat.at[:, :half, :])
    given_ref[...] = out[...].astype(jnp.bfloat16)


def expert_half(pieces, own, w_gate, w_up, w_down):
    tall, wide = CAP * SEGMENTS, pieces[0].shape[1]
    features, units = w_gate.shape
    rows = 2 * own * CAP
    return pl.pallas_call(
        functools.partial(expert_kernel, own),
        out_shape=[
            jax.ShapeDtypeStruct((own * tall, wide), jnp.bfloat16),
            jax.ShapeDtypeStruct((own * CAP, units), jnp.bfloat16),
        ],
        in_specs=[VMEM] * (len(pieces) + 3),
        out_specs=[VMEM] * 2,
        scratch_shapes=[
            pltpu.VMEM((2 * own * tall, wide), jnp.float32),
            pltpu.VMEM((2, rows, wide), jnp.float32),
            pltpu.VMEM((own * tall, wide), jnp.float32),
        ],
        compiler_params=params(16 + own),
        cost_estimate=pl.CostEstimate(
            flops=5 * rows * units * features,
            bytes_accessed=6 * features * units,
            transcendentals=rows * units,
        ),
        name="expert_half",
    )(*pieces, w_gate, w_up, w_down)


def kept_kernel(hidden_ref, down_ref, kept_ref, flat):
    packed_down(hidden_ref[...], down_ref, kept_ref, flat)


def kept_half(hidden, w_down):
    count, units = hidden.shape
    features = w_down.shape[1]
    wide = features // SEGMENTS
    return pl.pallas_call(
        kept_kernel,
        out_shape=jax.ShapeDtypeStruct((count * SEGMENTS, wide), jnp.float32),
        in_specs=[VMEM] * 2,
        out_specs=VMEM,
        scratch_shapes=[pltpu.VMEM((2, count, wide), jnp.float32)],
        compiler_params=params(8 + count // 10),
        cost_estimate=pl.CostEstimate(
            flops=2 * count * units * features,
            bytes_accessed=2 * features * units,
            transcendentals=0,
        ),
        name="kept_half",
    )(hidden, w_down)


def add_kernel(kept_ref, taken_ref, *out_refs):
    start = 0
    for out_ref in out_refs:
        rows = slice(start, start + out_ref.shape[0])
        total = kept_ref[rows, :] + taken_ref[rows, :].astype(jnp.float32)
        out_ref[...] = total.astype(out_ref.dtype)
        start += out_ref.shape[0]


def add_cores(kept, taken, teams, chips):
    tall, wide = CAP * SEGMENTS, kept.shape[1]
    outs = [jax.ShapeDtypeStruct((tall, wide), jnp.float32)]
    outs += [jax.ShapeDtypeStruct((tall, wide), jnp.bfloat16)] * (chips - 1)
    outs += [jax.ShapeDtypeStruct((chips * tall, wide), jnp.bfloat16)] * (teams - 1)
    return pl.pallas_call(
        add_kernel,
        out_shape=outs,
        in_specs=[VMEM] * 2,
        out_specs=[VMEM] * len(outs),
        compiler_params=params(4 + 4 * teams),
        name="add_cores",
    )(kept, taken)


def sum_kernel(terms_ref, out_ref):
    tall = out_ref.shape[0]
    total = terms_ref[:tall, :].astype(jnp.float32)
    for q in range(1, terms_ref.shape[0] // tall):
        total = total + terms_ref[q * tall : (q + 1) * tall, :].astype(jnp.float32)
    out_ref[...] = total.astype(out_ref.dtype)


def sum_blocks(terms, chips):
    return pl.pallas_call(
        sum_kernel,
        out_shape=jax.ShapeDtypeStruct((terms.shape[0] // chips, terms.shape[1]), jnp.bfloat16),
        in_specs=[VMEM],
        out_specs=VMEM,
        compiler_params=params(4),
        name="sum_blocks",
    )(terms)


def blend_kernel(chips, weight_ref, *refs):
    *refs, out_hbm, out_ref, sem = refs
    count, features = out_ref.shape
    wide = features // SEGMENTS
    own = refs[0][...]
    for ref in refs[1:chips]:
        own = own + ref[...].astype(jnp.float32)
    high = own.astype(jnp.bfloat16).astype(jnp.float32)
    terms = [high, own - high, high]
    for ref in refs[chips:]:
        terms += [ref[...].astype(jnp.float32)] * 2
    rows = jnp.concatenate(terms, axis=0).astype(jnp.bfloat16)
    copies = []
    for s in range(SEGMENTS):
        columns = pl.ds(s * wide, wide)
        out_ref[:, columns] = jnp.dot(
            weight_ref[s * count : (s + 1) * count, :], rows, preferred_element_type=jnp.float32
        ).astype(jnp.bfloat16)
        copies.append(
            pltpu.make_async_copy(out_ref.at[:, columns], out_hbm.at[:, columns], sem.at[s])
        )
        copies[-1].start()
    wait_all(copies)


def blend(weights, own_blocks, other_blocks, count):
    chips = len(own_blocks)
    features = own_blocks[0].shape[1] * SEGMENTS
    return pl.pallas_call(
        functools.partial(blend_kernel, chips),
        out_shape=jax.ShapeDtypeStruct((count, features), jnp.bfloat16),
        in_specs=[VMEM] * (1 + chips + len(other_blocks)),
        out_specs=HBM,
        scratch_shapes=[
            pltpu.VMEM((count, features), jnp.bfloat16),
            pltpu.SemaphoreType.DMA((SEGMENTS,)),
        ],
        compiler_params=params(16),
        name="blend",
    )(weights, *own_blocks, *other_blocks)


def body(tokens, expert_ids, route_logits, w_gate, w_up, w_down):
    devices = lax.axis_size("expert")
    teams = devices // SPLIT
    chips = SPLIT // CORES
    other_core = [(i, i ^ 1) for i in range(devices)]
    same_core = [
        [t * SPLIT + q * CORES + c for q in range(chips)] for t in range(teams) for c in range(CORES)
    ]
    other_chip = [[(i, i ^ (m * CORES)) for i in range(devices)] for m in range(chips)]
    packed, table = pack_rows(expert_ids.T, route_logits.T, tokens, teams)
    own = [packed[0]]
    for m in range(1, chips):
        own.append(lax.ppermute(packed[0], "expert", other_chip[m]))
    crowds = []
    for k in range(1, teams):
        pairs = [(i, (i + k * SPLIT) % devices) for i in range(devices)]
        block = lax.ppermute(packed[k], "expert", pairs)
        if k == teams - 1:
            block, table = lax.optimization_barrier((block, table))
            weights = blend_weights(table, teams)
        crowds.append(
            lax.all_to_all(
                spread(block, chips),
                "expert",
                split_axis=0,
                concat_axis=0,
                axis_index_groups=same_core,
                tiled=True,
            )
        )
    own, weights = lax.optimization_barrier((own, weights))
    crowds, joined = lax.optimization_barrier((crowds, join(own)))
    swapped = [lax.ppermute(piece, "expert", other_core) for piece in (joined, *crowds)]
    given, hidden = expert_half(
        [*own, *crowds, *swapped], teams * chips, w_gate, w_up, w_down
    )
    taken = lax.ppermute(given, "expert", other_core)
    kept = kept_half(hidden, w_down)
    parts = add_cores(kept, taken, teams, chips)
    others = []
    for k in range(1, teams):
        terms = lax.all_to_all(
            parts[chips + k - 1],
            "expert",
            split_axis=0,
            concat_axis=0,
            axis_index_groups=same_core,
            tiled=True,
        )
        pairs = [(i, (i - k * SPLIT) % devices) for i in range(devices)]
        others.append(lax.ppermute(sum_blocks(terms, chips), "expert", pairs))
    own = [parts[0]]
    for m in range(1, chips):
        own.append(lax.ppermute(parts[m], "expert", other_chip[m]))
    return blend(weights, own, others, tokens.shape[0])


def solution(mesh):
    placed = (
        P(("groups", "expert"), None),
        P(("groups", "expert"), None),
        P(("groups", "expert"), None),
        P(None, "expert"),
        P(None, "expert"),
        P("expert", None),
    )
    return jax.shard_map(
        body, mesh=mesh, in_specs=placed, out_specs=P(("groups", "expert"), None), check_vma=False
    )
```

```python
import functools

import jax
import jax.numpy as jnp
from jax import lax
from jax.experimental import pallas as pl
from jax.experimental.pallas import tpu as pltpu
from jax.sharding import PartitionSpec as P

SPLIT = 8
CAP = 5
CORES = 2
SEGMENTS = 8

route_scale = 2.5

VMEM = pl.BlockSpec(memory_space=pltpu.VMEM)
HBM = pl.BlockSpec(memory_space=pltpu.HBM)
MIB = 1024 * 1024


def hits(ids, mine, teams):
    count = ids.shape[1]
    row = lax.broadcasted_iota(jnp.int32, (8 * pl.cdiv(teams, 8), count), 0)
    wanted = lax.rem(mine + row, teams)
    hit = jnp.zeros(row.shape, jnp.int32)
    for j in range(ids.shape[0]):
        hit = hit + jnp.where(ids[j : j + 1, :] == wanted, 1, 0)
    hit = jnp.where(row < teams, hit, 0).astype(jnp.float32)
    before = lax.broadcasted_iota(jnp.int32, (count, count), 0)
    after = lax.broadcasted_iota(jnp.int32, (count, count), 1)
    earlier = jnp.where(before < after, 1.0, 0.0).astype(jnp.bfloat16)
    slot = jnp.dot(hit.astype(jnp.bfloat16), earlier, preferred_element_type=jnp.float32)
    return hit, jnp.where(hit > 0, slot, -1.0)


def fifth(shape, axis):
    at = lax.broadcasted_iota(jnp.int32, shape, axis)
    segment = jnp.zeros(shape, jnp.int32)
    for s in range(1, SEGMENTS):
        segment = segment + jnp.where(at >= s * CAP, 1, 0)
    return segment, (at - CAP * segment).astype(jnp.float32)


def params(mib):
    return pltpu.CompilerParams(vmem_limit_bytes=int(mib * MIB))


def bring(source, target, semaphores, parts):
    step = source.shape[0] // parts
    copies = []
    for i in range(parts):
        rows = pl.ds(i * step, step)
        copies.append(pltpu.make_async_copy(source.at[rows], target.at[rows], semaphores.at[i]))
        copies[-1].start()
    return copies


def wait_all(copies):
    for copy in copies:
        copy.wait()


def pack_kernel(teams, ids_hbm, logits_hbm, tokens_hbm, *refs):
    *out_refs, table_ref, ids_ref, logits_ref, tokens_ref, ids_sem, logits_sem, tokens_sem = refs
    ids_copy = bring(ids_hbm, ids_ref, ids_sem, 1)
    tokens_copy = bring(tokens_hbm, tokens_ref, tokens_sem, 4)
    logits_copy = bring(logits_hbm, logits_ref, logits_sem, 1)
    wait_all(ids_copy)
    mine = lax.axis_index("expert") // SPLIT
    ids = ids_ref[...]
    hit, slot = hits(ids, mine, teams)
    wait_all(logits_copy)
    lifted = jax.nn.sigmoid(logits_ref[...])
    gates = route_scale * lifted / jnp.sum(lifted, axis=0, keepdims=True)
    row = lax.broadcasted_iota(jnp.int32, hit.shape, 0)
    wanted = lax.rem(mine + row, teams)
    gate = jnp.zeros(hit.shape, jnp.float32)
    for j in range(ids.shape[0]):
        gate = gate + jnp.where(ids[j : j + 1, :] == wanted, gates[j : j + 1, :], 0.0)
    table_ref[: hit.shape[0], :] = slot
    table_ref[hit.shape[0] :, :] = gate
    count, features = tokens_ref.shape
    wide = features // SEGMENTS
    tall = CAP * SEGMENTS
    segment, place = fifth((tall, 1), 0)
    column = lax.broadcasted_iota(jnp.int32, (1, SEGMENTS * count), 1)
    same = segment == column // count
    picks = []
    for k in range(teams):
        slots = jnp.concatenate([slot[k : k + 1, :]] * SEGMENTS, axis=1)
        picks.append(jnp.where(same & (slots == place), 1.0, 0.0))
    wait_all(tokens_copy)
    stacked = jnp.concatenate(
        [tokens_ref[:, s * wide : (s + 1) * wide] for s in range(SEGMENTS)], axis=0
    )
    packed = jnp.dot(
        jnp.concatenate(picks, axis=0).astype(jnp.bfloat16),
        stacked,
        preferred_element_type=jnp.float32,
    )
    for k in range(teams):
        out_refs[k][...] = packed[k * tall : (k + 1) * tall].astype(jnp.bfloat16)


def pack_rows(ids, logits, tokens, teams):
    wide = tokens.shape[1] // SEGMENTS
    block = jax.ShapeDtypeStruct((CAP * SEGMENTS, wide), jnp.bfloat16)
    table = jax.ShapeDtypeStruct((16 * pl.cdiv(teams, 8), ids.shape[1]), jnp.float32)
    *packed, table = pl.pallas_call(
        functools.partial(pack_kernel, teams),
        out_shape=[block] * teams + [table],
        in_specs=[HBM] * 3,
        out_specs=[VMEM] * (teams + 1),
        scratch_shapes=[
            pltpu.VMEM(ids.shape, ids.dtype),
            pltpu.VMEM(logits.shape, logits.dtype),
            pltpu.VMEM(tokens.shape, tokens.dtype),
            pltpu.SemaphoreType.DMA((1,)),
            pltpu.SemaphoreType.DMA((1,)),
            pltpu.SemaphoreType.DMA((4,)),
        ],
        name="pack_rows",
    )(ids, logits, tokens)
    return packed, table


def weight_kernel(teams, table_ref, out_ref):
    rows, count = table_ref.shape
    slot = jnp.transpose(table_ref[: rows // 2, :])
    gate = jnp.transpose(table_ref[rows // 2 :, :])
    tall = CAP * SEGMENTS
    depth = out_ref.shape[1]
    column = lax.broadcasted_iota(jnp.int32, (1, depth), 1)
    part = jnp.zeros((1, depth), jnp.int32)
    for g in range(1, depth // tall):
        part = part + jnp.where(column >= g * tall, 1, 0)
    column = column - tall * part
    segment = jnp.zeros((1, depth), jnp.int32)
    for s in range(1, SEGMENTS):
        segment = segment + jnp.where(column >= s * CAP, 1, 0)
    place = (column - CAP * segment).astype(jnp.float32)
    team = jnp.where(part < 3, 0, (part - 1) >> 1)
    low = jnp.where(part < 3, part >> 1, (part - 3) & 1) == 1
    for s in range(SEGMENTS):
        full = jnp.zeros((count, depth), jnp.float32)
        for k in range(teams):
            chosen = (team == k) & (segment == s) & (slot[:, k : k + 1] == place)
            full = full + jnp.where(chosen, gate[:, k : k + 1], 0.0)
        high = full.astype(jnp.bfloat16).astype(jnp.float32)
        out_ref[s * count : (s + 1) * count, :] = jnp.where(low, full - high, high).astype(
            jnp.bfloat16
        )


def blend_weights(table, teams):
    shape = (SEGMENTS * table.shape[1], CAP * SEGMENTS * (1 + 2 * teams))
    return pl.pallas_call(
        functools.partial(weight_kernel, teams),
        out_shape=jax.ShapeDtypeStruct(shape, jnp.bfloat16),
        in_specs=[VMEM],
        out_specs=VMEM,
        compiler_params=params(4 + teams),
        cost_estimate=pl.CostEstimate(flops=6 * 10**9, bytes_accessed=8 * MIB, transcendentals=0),
        name="blend_weights",
    )(table)


def join_kernel(*refs):
    tall = refs[0].shape[0]
    for i, ref in enumerate(refs[:-1]):
        refs[-1][i * tall : (i + 1) * tall, :] = ref[...]


def join(blocks):
    tall, wide = blocks[0].shape
    return pl.pallas_call(
        join_kernel,
        out_shape=jax.ShapeDtypeStruct((tall * len(blocks), wide), blocks[0].dtype),
        in_specs=[VMEM] * len(blocks),
        out_specs=VMEM,
        compiler_params=params(4),
        name="join",
    )(*blocks)


def packed_down(hidden, down_ref, out_ref, flat):
    count, wide = flat.shape[1:]
    tall = CAP * SEGMENTS
    for s in range(SEGMENTS):
        slot = flat.at[s % 2]
        slot[...] = jnp.dot(
            hidden, down_ref[:, s * wide : (s + 1) * wide], preferred_element_type=jnp.float32
        )
        for b in range(count // CAP):
            start = b * tall + s * CAP
            out_ref[start : start + CAP, :] = slot[b * CAP : (b + 1) * CAP, :]


def expert_kernel(own, count_in, *refs):
    pieces = refs[:count_in]
    gate_ref, up_ref, down_ref = refs[count_in : count_in + 3]
    *given_refs, hidden_ref, packed, flat, out = refs[count_in + 3 :]
    tall = CAP * SEGMENTS
    wide = packed.shape[1]
    units = gate_ref.shape[1]
    start = 0
    for ref in pieces:
        packed[start : start + ref.shape[0], :] = ref[...].astype(jnp.float32)
        start += ref.shape[0]
    count = 2 * own * CAP
    gate_act = jnp.zeros((count, units), jnp.float32)
    up_act = jnp.zeros((count, units), jnp.float32)
    for s in range(SEGMENTS):
        slot = flat.at[s % 2]
        for b in range(2 * own):
            start = b * tall + s * CAP
            slot[b * CAP : (b + 1) * CAP, :] = packed[start : start + CAP, :]
        rows = slot[...].astype(jnp.bfloat16)
        columns = slice(s * wide, (s + 1) * wide)
        gate_act += jnp.dot(rows, gate_ref[columns, :], preferred_element_type=jnp.float32)
        up_act += jnp.dot(rows, up_ref[columns, :], preferred_element_type=jnp.float32)
    hidden = (jax.nn.silu(gate_act) * up_act).astype(jnp.bfloat16)
    half = count // 2
    hidden_ref[...] = hidden[:half]
    packed_down(hidden[half:], down_ref, out, flat.at[:, :half, :])
    for k, given_ref in enumerate(given_refs):
        rows = given_ref.shape[0]
        given_ref[...] = out[k * rows : (k + 1) * rows, :].astype(jnp.bfloat16)


def expert_half(pieces, own, teams, w_gate, w_up, w_down):
    tall, wide = CAP * SEGMENTS, pieces[0].shape[1]
    features, units = w_gate.shape
    rows = 2 * own * CAP
    return pl.pallas_call(
        functools.partial(expert_kernel, own, len(pieces)),
        out_shape=[jax.ShapeDtypeStruct((own // teams * tall, wide), jnp.bfloat16)] * teams
        + [jax.ShapeDtypeStruct((own * CAP, units), jnp.bfloat16)],
        in_specs=[VMEM] * (len(pieces) + 3),
        out_specs=[VMEM] * (teams + 1),
        scratch_shapes=[
            pltpu.VMEM((2 * own * tall, wide), jnp.float32),
            pltpu.VMEM((2, rows, wide), jnp.float32),
            pltpu.VMEM((own * tall, wide), jnp.float32),
        ],
        compiler_params=params(16 + own),
        cost_estimate=pl.CostEstimate(
            flops=5 * rows * units * features,
            bytes_accessed=6 * features * units,
            transcendentals=rows * units,
        ),
        name="expert_half",
    )(*pieces, w_gate, w_up, w_down)


def kept_kernel(hidden_ref, down_ref, kept_ref, flat):
    packed_down(hidden_ref[...], down_ref, kept_ref, flat)


def kept_half(hidden, w_down):
    count, units = hidden.shape
    features = w_down.shape[1]
    wide = features // SEGMENTS
    return pl.pallas_call(
        kept_kernel,
        out_shape=jax.ShapeDtypeStruct((count * SEGMENTS, wide), jnp.float32),
        in_specs=[VMEM] * 2,
        out_specs=VMEM,
        scratch_shapes=[pltpu.VMEM((2, count, wide), jnp.float32)],
        compiler_params=params(8 + count // 10),
        cost_estimate=pl.CostEstimate(
            flops=2 * count * units * features,
            bytes_accessed=2 * features * units,
            transcendentals=0,
        ),
        name="kept_half",
    )(hidden, w_down)


def call(kernel, outs, name, args, mib=4):
    return pl.pallas_call(
        kernel,
        out_shape=[jax.ShapeDtypeStruct(shape, kind) for shape, kind in outs],
        in_specs=[VMEM] * len(args),
        out_specs=[VMEM] * len(outs),
        compiler_params=params(mib),
        name=name,
    )(*args)


def halves(wide):
    cut = 128 * pl.cdiv(wide // 128, 2)
    return slice(0, cut), slice(cut, wide)


def halve_kernel(block_ref, *out_refs):
    for columns, ref in zip(halves(block_ref.shape[1]), out_refs):
        ref[...] = block_ref[:, columns]


def halve(block):
    outs = []
    for columns in halves(block.shape[1]):
        outs.append(((block.shape[0], columns.stop - columns.start), block.dtype))
    return call(halve_kernel, outs, "halve", [block])


def crowd_kernel(left_ref, far_left_ref, right_ref, far_right_ref, out_ref):
    tall = left_ref.shape[0] // 2
    left, right = halves(out_ref.shape[1])
    out_ref[: 2 * tall, left] = left_ref[...]
    out_ref[2 * tall :, left] = far_left_ref[...]
    for m, (ref, at) in enumerate(
        ((right_ref, 0), (far_right_ref, 0), (right_ref, 1), (far_right_ref, 1))
    ):
        out_ref[m * tall : (m + 1) * tall, right] = ref[at * tall : (at + 1) * tall, :]


def gather_team(block, along):
    left, right = halve(block)
    left = join([left, along[1](left)])
    right = join([right, along[2](right)])
    far_left, far_right = along[2](left), along[1](right)
    tall, wide = block.shape
    return call(
        crowd_kernel,
        [((4 * tall, wide), block.dtype)],
        "crowd",
        [left, far_left, right, far_right],
    )[0]


def add_own_kernel(kept_ref, taken_ref, near_ref, away_ref):
    rows = near_ref.shape[0]
    near_ref[...] = kept_ref[:rows, :] + taken_ref[:rows, :].astype(jnp.float32)
    total = kept_ref[rows : 2 * rows, :] + taken_ref[rows:, :].astype(jnp.float32)
    away_ref[...] = total.astype(jnp.bfloat16)


def add_own(kept, taken):
    shape = (taken.shape[0] // 2, taken.shape[1])
    outs = [(shape, jnp.float32), (shape, jnp.bfloat16)]
    return call(add_own_kernel, outs, "add_own", [kept, taken], 8)


def add_other_kernel(first, kept_ref, taken_ref, *out_refs):
    tall = taken_ref.shape[0] // 4
    left, right = halves(taken_ref.shape[1])
    for columns, near, away, near_ref, away_ref in (
        (left, (0, 2), (1, 3), out_refs[0], out_refs[1]),
        (right, (0, 1), (2, 3), out_refs[2], out_refs[3]),
    ):
        for blocks, ref in ((near, near_ref), (away, away_ref)):
            for at, m in enumerate(blocks):
                total = kept_ref[
                    first + m * tall : first + (m + 1) * tall, columns
                ] + taken_ref[m * tall : (m + 1) * tall, columns].astype(jnp.float32)
                ref[at * tall : (at + 1) * tall, :] = total.astype(ref.dtype)


def step_kernel(near_ref, got_ref, here_ref, away_ref):
    tall = here_ref.shape[0]
    total = near_ref[...] + got_ref[...].astype(jnp.float32)
    here_ref[...] = total[:tall]
    away_ref[...] = total[tall:].astype(jnp.bfloat16)


def step(near, got):
    shape = (near.shape[0] // 2, near.shape[1])
    return call(step_kernel, [(shape, jnp.float32), (shape, jnp.bfloat16)], "step", [near, got])


def last_kernel(left_ref, got_left_ref, right_ref, got_right_ref, out_ref):
    left, right = halves(out_ref.shape[1])
    out_ref[:, left] = (left_ref[...] + got_left_ref[...].astype(jnp.float32)).astype(jnp.bfloat16)
    out_ref[:, right] = (right_ref[...] + got_right_ref[...].astype(jnp.float32)).astype(
        jnp.bfloat16
    )


def sum_team(kept, taken, k, along, later):
    rows, wide = taken.shape
    tall = rows // 4
    left, right = (columns.stop - columns.start for columns in halves(wide))
    outs = []
    for size in (left, right):
        outs += [((2 * tall, size), jnp.float32), ((2 * tall, size), jnp.bfloat16)]
    near_left, away_left, near_right, away_right = call(
        functools.partial(add_other_kernel, k * rows), outs, "add_other", [kept, taken], 8
    )
    left, next_left = step(near_left, along[1](away_left))
    next_left, later = lax.optimization_barrier((next_left, later))
    right, next_right = step(near_right, along[2](away_right))
    return call(
        last_kernel,
        [((tall, wide), jnp.bfloat16)],
        "last",
        [left, along[2](next_left), right, along[1](next_right)],
    )[0], later


def blend_kernel(weight_ref, here_ref, got_ref, *refs):
    *refs, out_hbm, out_ref, sem = refs
    count, features = out_ref.shape
    wide = features // SEGMENTS
    own = here_ref[...] + got_ref[...].astype(jnp.float32)
    high = own.astype(jnp.bfloat16).astype(jnp.float32)
    terms = [high, own - high, high]
    for ref in refs:
        terms += [ref[...].astype(jnp.float32)] * 2
    rows = jnp.concatenate(terms, axis=0).astype(jnp.bfloat16)
    copies = []
    for columns in halves(wide):
        size = columns.stop - columns.start
        total = jnp.dot(weight_ref[...], rows[:, columns], preferred_element_type=jnp.float32)
        for s in range(SEGMENTS):
            part = pl.ds(s * wide + columns.start, size)
            out_ref[:, part] = total[s * count : (s + 1) * count].astype(jnp.bfloat16)
            copies.append(
                pltpu.make_async_copy(
                    out_ref.at[:, part], out_hbm.at[:, part], sem.at[len(copies)]
                )
            )
            copies[-1].start()
    wait_all(copies)


def blend(weights, here, got, other_blocks, count):
    features = here.shape[1] * SEGMENTS
    return pl.pallas_call(
        blend_kernel,
        out_shape=jax.ShapeDtypeStruct((count, features), jnp.bfloat16),
        in_specs=[VMEM] * (3 + len(other_blocks)),
        out_specs=HBM,
        scratch_shapes=[
            pltpu.VMEM((count, features), jnp.bfloat16),
            pltpu.SemaphoreType.DMA((2 * SEGMENTS,)),
        ],
        compiler_params=params(16),
        name="blend",
    )(weights, here, got, *other_blocks)


def body(tokens, expert_ids, route_logits, w_gate, w_up, w_down):
    devices = lax.axis_size("expert")
    teams = devices // SPLIT
    chips = SPLIT // CORES
    other_core = [(i, i ^ 1) for i in range(devices)]
    other_chip = [[(i, i ^ (m * CORES)) for i in range(devices)] for m in range(chips)]
    packed, table = pack_rows(expert_ids.T, route_logits.T, tokens, teams)
    along = [functools.partial(lax.ppermute, axis_name="expert", perm=p) for p in other_chip]
    pair = join([packed[0], along[1](packed[0])])
    crowds = []
    for k in range(1, teams):
        pairs = [(i, (i + k * SPLIT) % devices) for i in range(devices)]
        block = lax.ppermute(packed[k], "expert", pairs)
        if k == teams - 1:
            block, table, pair = lax.optimization_barrier((block, table, pair))
            weights = blend_weights(table, teams)
        crowds.append(gather_team(block, along))
    own, weights = lax.optimization_barrier((join([pair, along[2](pair)]), weights))
    own, crowds = lax.optimization_barrier((own, crowds))
    swapped = [lax.ppermute(piece, "expert", other_core) for piece in (own, *crowds)]
    *given, hidden = expert_half(
        [own, *crowds, *swapped], teams * chips, teams, w_gate, w_up, w_down
    )
    taken = [lax.ppermute(piece, "expert", other_core) for piece in given]
    kept = kept_half(hidden, w_down)
    others = []
    for k in range(1, teams):
        pairs = [(i, (i - k * SPLIT) % devices) for i in range(devices)]
        total, taken[0] = sum_team(kept, taken[k], k, along, taken[0])
        others.append(lax.ppermute(total, "expert", pairs))
    near, away = add_own(kept, taken[0])
    here, away = step(near, along[2](away))
    return blend(weights, here, along[1](away), others, tokens.shape[0])


def solution(mesh):
    placed = (
        P(("groups", "expert"), None),
        P(("groups", "expert"), None),
        P(("groups", "expert"), None),
        P(None, "expert"),
        P(None, "expert"),
        P("expert", None),
    )
    return jax.shard_map(
        body, mesh=mesh, in_specs=placed, out_specs=P(("groups", "expert"), None), check_vma=False
    )
```

```python
import functools

import jax
import jax.numpy as jnp
from jax import lax
from jax.experimental import pallas as pl
from jax.experimental.pallas import tpu as pltpu
from jax.sharding import PartitionSpec as P

SPLIT = 8
CAP = 5
CORES = 2
SEGMENTS = 8

route_scale = 2.5

VMEM = pl.BlockSpec(memory_space=pltpu.VMEM)
HBM = pl.BlockSpec(memory_space=pltpu.HBM)
MIB = 1024 * 1024


def hits(ids, mine, teams):
    count = ids.shape[1]
    row = lax.broadcasted_iota(jnp.int32, (8 * pl.cdiv(teams, 8), count), 0)
    wanted = lax.rem(mine + row, teams)
    hit = jnp.zeros(row.shape, jnp.int32)
    for j in range(ids.shape[0]):
        hit = hit + jnp.where(ids[j : j + 1, :] == wanted, 1, 0)
    hit = jnp.where(row < teams, hit, 0).astype(jnp.float32)
    before = lax.broadcasted_iota(jnp.int32, (count, count), 0)
    after = lax.broadcasted_iota(jnp.int32, (count, count), 1)
    earlier = jnp.where(before < after, 1.0, 0.0).astype(jnp.bfloat16)
    slot = jnp.dot(hit.astype(jnp.bfloat16), earlier, preferred_element_type=jnp.float32)
    return hit, jnp.where(hit > 0, slot, -1.0)


def fifth(shape, axis):
    at = lax.broadcasted_iota(jnp.int32, shape, axis)
    segment = jnp.zeros(shape, jnp.int32)
    for s in range(1, SEGMENTS):
        segment = segment + jnp.where(at >= s * CAP, 1, 0)
    return segment, (at - CAP * segment).astype(jnp.float32)


def params(mib):
    return pltpu.CompilerParams(vmem_limit_bytes=int(mib * MIB))


def bring(source, target, semaphores, parts):
    step = source.shape[0] // parts
    copies = []
    for i in range(parts):
        rows = pl.ds(i * step, step)
        copies.append(pltpu.make_async_copy(source.at[rows], target.at[rows], semaphores.at[i]))
        copies[-1].start()
    return copies


def wait_all(copies):
    for copy in copies:
        copy.wait()


def pack_kernel(teams, ids_hbm, logits_hbm, tokens_hbm, *refs):
    *out_refs, table_ref, ids_ref, logits_ref, tokens_ref, ids_sem, logits_sem, tokens_sem = refs
    ids_copy = bring(ids_hbm, ids_ref, ids_sem, 1)
    tokens_copy = bring(tokens_hbm, tokens_ref, tokens_sem, 4)
    logits_copy = bring(logits_hbm, logits_ref, logits_sem, 1)
    wait_all(ids_copy)
    mine = lax.axis_index("expert") // SPLIT
    ids = ids_ref[...]
    hit, slot = hits(ids, mine, teams)
    wait_all(logits_copy)
    lifted = jax.nn.sigmoid(logits_ref[...])
    gates = route_scale * lifted / jnp.sum(lifted, axis=0, keepdims=True)
    row = lax.broadcasted_iota(jnp.int32, hit.shape, 0)
    wanted = lax.rem(mine + row, teams)
    gate = jnp.zeros(hit.shape, jnp.float32)
    for j in range(ids.shape[0]):
        gate = gate + jnp.where(ids[j : j + 1, :] == wanted, gates[j : j + 1, :], 0.0)
    table_ref[: hit.shape[0], :] = slot
    table_ref[hit.shape[0] :, :] = gate
    count, features = tokens_ref.shape
    wide = features // SEGMENTS
    tall = CAP * SEGMENTS
    segment, place = fifth((tall, 1), 0)
    column = lax.broadcasted_iota(jnp.int32, (1, SEGMENTS * count), 1)
    same = segment == column // count
    picks = []
    for k in range(teams):
        slots = jnp.concatenate([slot[k : k + 1, :]] * SEGMENTS, axis=1)
        picks.append(jnp.where(same & (slots == place), 1.0, 0.0))
    wait_all(tokens_copy)
    stacked = jnp.concatenate(
        [tokens_ref[:, s * wide : (s + 1) * wide] for s in range(SEGMENTS)], axis=0
    )
    packed = jnp.dot(
        jnp.concatenate(picks, axis=0).astype(jnp.bfloat16),
        stacked,
        preferred_element_type=jnp.float32,
    )
    for k in range(teams):
        out_refs[k][...] = packed[k * tall : (k + 1) * tall].astype(jnp.bfloat16)


def pack_rows(ids, logits, tokens, teams):
    wide = tokens.shape[1] // SEGMENTS
    block = jax.ShapeDtypeStruct((CAP * SEGMENTS, wide), jnp.bfloat16)
    table = jax.ShapeDtypeStruct((16 * pl.cdiv(teams, 8), ids.shape[1]), jnp.float32)
    *packed, table = pl.pallas_call(
        functools.partial(pack_kernel, teams),
        out_shape=[block] * teams + [table],
        in_specs=[HBM] * 3,
        out_specs=[VMEM] * (teams + 1),
        scratch_shapes=[
            pltpu.VMEM(ids.shape, ids.dtype),
            pltpu.VMEM(logits.shape, logits.dtype),
            pltpu.VMEM(tokens.shape, tokens.dtype),
            pltpu.SemaphoreType.DMA((1,)),
            pltpu.SemaphoreType.DMA((1,)),
            pltpu.SemaphoreType.DMA((4,)),
        ],
        name="pack_rows",
    )(ids, logits, tokens)
    return packed, table


def weight_kernel(teams, table_ref, out_ref):
    rows, count = table_ref.shape
    slot = jnp.transpose(table_ref[: rows // 2, :])
    gate = jnp.transpose(table_ref[rows // 2 :, :])
    tall = CAP * SEGMENTS
    depth = out_ref.shape[1]
    column = lax.broadcasted_iota(jnp.int32, (1, depth), 1)
    part = jnp.zeros((1, depth), jnp.int32)
    for g in range(1, depth // tall):
        part = part + jnp.where(column >= g * tall, 1, 0)
    column = column - tall * part
    segment = jnp.zeros((1, depth), jnp.int32)
    for s in range(1, SEGMENTS):
        segment = segment + jnp.where(column >= s * CAP, 1, 0)
    place = (column - CAP * segment).astype(jnp.float32)
    team = jnp.where(part < 3, 0, (part - 1) >> 1)
    low = jnp.where(part < 3, part >> 1, (part - 3) & 1) == 1
    for s in range(SEGMENTS):
        full = jnp.zeros((count, depth), jnp.float32)
        for k in range(teams):
            chosen = (team == k) & (segment == s) & (slot[:, k : k + 1] == place)
            full = full + jnp.where(chosen, gate[:, k : k + 1], 0.0)
        high = full.astype(jnp.bfloat16).astype(jnp.float32)
        out_ref[s * count : (s + 1) * count, :] = jnp.where(low, full - high, high).astype(
            jnp.bfloat16
        )


def blend_weights(table, teams):
    shape = (SEGMENTS * table.shape[1], CAP * SEGMENTS * (1 + 2 * teams))
    return pl.pallas_call(
        functools.partial(weight_kernel, teams),
        out_shape=jax.ShapeDtypeStruct(shape, jnp.bfloat16),
        in_specs=[VMEM],
        out_specs=VMEM,
        compiler_params=params(4 + teams),
        cost_estimate=pl.CostEstimate(flops=6 * 10**9, bytes_accessed=8 * MIB, transcendentals=0),
        name="blend_weights",
    )(table)


def join_kernel(*refs):
    tall = refs[0].shape[0]
    for i, ref in enumerate(refs[:-1]):
        refs[-1][i * tall : (i + 1) * tall, :] = ref[...]


def join(blocks):
    tall, wide = blocks[0].shape
    return pl.pallas_call(
        join_kernel,
        out_shape=jax.ShapeDtypeStruct((tall * len(blocks), wide), blocks[0].dtype),
        in_specs=[VMEM] * len(blocks),
        out_specs=VMEM,
        compiler_params=params(4),
        name="join",
    )(*blocks)


def packed_down(hidden, down_ref, out_ref, flat):
    count, wide = flat.shape[1:]
    tall = CAP * SEGMENTS
    for s in range(SEGMENTS):
        slot = flat.at[s % 2]
        slot[...] = jnp.dot(
            hidden, down_ref[:, s * wide : (s + 1) * wide], preferred_element_type=jnp.float32
        )
        for b in range(count // CAP):
            start = b * tall + s * CAP
            out_ref[start : start + CAP, :] = slot[b * CAP : (b + 1) * CAP, :]


def unpack_kernel(own_ref, other_ref, out_ref, packed):
    tall = CAP * SEGMENTS
    half = own_ref.shape[0]
    wide = own_ref.shape[1]
    packed[:half, :] = own_ref[...].astype(jnp.float32)
    packed[half:, :] = other_ref[...].astype(jnp.float32)
    for s in range(SEGMENTS):
        for b in range(2 * half // tall):
            start = b * tall + s * CAP
            out_ref[b * CAP : (b + 1) * CAP, s * wide : (s + 1) * wide] = packed[
                start : start + CAP, :
            ]


def unpack(own, other):
    rows, wide = own.shape
    return pl.pallas_call(
        unpack_kernel,
        out_shape=jax.ShapeDtypeStruct((2 * rows // SEGMENTS, wide * SEGMENTS), jnp.float32),
        in_specs=[VMEM] * 2,
        out_specs=VMEM,
        scratch_shapes=[pltpu.VMEM((2 * rows, wide), jnp.float32)],
        compiler_params=params(6),
        name="unpack",
    )(own, other)


def expert_kernel(teams, first_ref, *refs):
    pieces = refs[: 2 * (teams - 1)]
    gate_ref, up_ref, down_ref = refs[2 * (teams - 1) : 2 * teams + 1]
    *given_refs, hidden_ref, packed, flat, out, act = refs[2 * teams + 1 :]
    tall = CAP * SEGMENTS
    wide = packed.shape[1]
    units = gate_ref.shape[1]
    start = 0
    for ref in pieces:
        packed[start : start + ref.shape[0], :] = ref[...].astype(jnp.float32)
        start += ref.shape[0]
    known = first_ref.shape[0]
    count = known * teams
    gate_act = jnp.zeros((count, units), jnp.float32)
    up_act = jnp.zeros((count, units), jnp.float32)
    for s in range(SEGMENTS):
        slot = flat.at[s % 2]
        columns = slice(s * wide, (s + 1) * wide)
        slot[:known, :] = first_ref[:, columns]
        for b in range((count - known) // CAP):
            start = b * tall + s * CAP
            slot[known + b * CAP : known + (b + 1) * CAP, :] = packed[start : start + CAP, :]
        rows = slot[...].astype(jnp.bfloat16)
        gate_act += jnp.dot(rows, gate_ref[columns, :], preferred_element_type=jnp.float32)
        up_act += jnp.dot(rows, up_ref[columns, :], preferred_element_type=jnp.float32)
    act[:count, :] = jax.nn.silu(gate_act) * up_act
    half = known // 2
    for k in range(teams):
        for core in range(CORES):
            source = (CORES * k + core) * half
            target = count + (core * teams + k) * half
            act[target : target + half, :] = act[source : source + half, :]
    hidden = act[count:, :].astype(jnp.bfloat16)
    half = count // 2
    hidden_ref[...] = hidden[:half]
    packed_down(hidden[half:], down_ref, out, flat.at[:, :half, :])
    for k, given_ref in enumerate(given_refs):
        rows = given_ref.shape[0]
        given_ref[...] = out[k * rows : (k + 1) * rows, :].astype(jnp.bfloat16)


def expert_half(first, pieces, w_gate, w_up, w_down):
    teams = 1 + len(pieces) // 2
    block, wide = pieces[0].shape
    features, units = w_gate.shape
    rows = first.shape[0] * teams
    return pl.pallas_call(
        functools.partial(expert_kernel, teams),
        out_shape=[jax.ShapeDtypeStruct((block, wide), jnp.bfloat16)] * teams
        + [jax.ShapeDtypeStruct((rows // 2, units), jnp.bfloat16)],
        in_specs=[VMEM] * (len(pieces) + 4),
        out_specs=[VMEM] * (teams + 1),
        scratch_shapes=[
            pltpu.VMEM((block * len(pieces), wide), jnp.float32),
            pltpu.VMEM((2, rows, wide), jnp.float32),
            pltpu.VMEM((block * teams, wide), jnp.float32),
            pltpu.VMEM((2 * rows, units), jnp.float32),
        ],
        compiler_params=params(16 + 4 * teams),
        cost_estimate=pl.CostEstimate(
            flops=5 * rows * units * features,
            bytes_accessed=6 * features * units,
            transcendentals=rows * units,
        ),
        name="expert_half",
    )(first, *pieces, w_gate, w_up, w_down)


def kept_kernel(hidden_ref, down_ref, kept_ref, flat):
    packed_down(hidden_ref[...], down_ref, kept_ref, flat)


def kept_half(hidden, w_down):
    count, units = hidden.shape
    features = w_down.shape[1]
    wide = features // SEGMENTS
    return pl.pallas_call(
        kept_kernel,
        out_shape=jax.ShapeDtypeStruct((count * SEGMENTS, wide), jnp.float32),
        in_specs=[VMEM] * 2,
        out_specs=VMEM,
        scratch_shapes=[pltpu.VMEM((2, count, wide), jnp.float32)],
        compiler_params=params(8 + count // 10),
        cost_estimate=pl.CostEstimate(
            flops=2 * count * units * features,
            bytes_accessed=2 * features * units,
            transcendentals=0,
        ),
        name="kept_half",
    )(hidden, w_down)


def add_kernel(first, kept_ref, taken_ref, *out_refs):
    tall = out_refs[0].shape[0]
    for b, out_ref in enumerate(out_refs):
        rows = slice(b * tall, (b + 1) * tall)
        total = kept_ref[first + b * tall : first + (b + 1) * tall, :] + taken_ref[
            rows, :
        ].astype(jnp.float32)
        out_ref[...] = total.astype(out_ref.dtype)


def add_cores(kept, taken, k, chips):
    shape = (CAP * SEGMENTS, kept.shape[1])
    outs = [jax.ShapeDtypeStruct(shape, jnp.bfloat16 if m else jnp.float32) for m in range(chips)]
    return pl.pallas_call(
        functools.partial(add_kernel, k * taken.shape[0]),
        out_shape=outs,
        in_specs=[VMEM] * 2,
        out_specs=[VMEM] * len(outs),
        compiler_params=params(6),
        name="add_cores",
    )(kept, taken)


def sum_kernel(*refs):
    total = refs[0][...]
    for ref in refs[1:-1]:
        total = total + ref[...].astype(jnp.float32)
    refs[-1][...] = total.astype(refs[-1].dtype)


def sum_blocks(blocks):
    return pl.pallas_call(
        sum_kernel,
        out_shape=jax.ShapeDtypeStruct(blocks[0].shape, jnp.bfloat16),
        in_specs=[VMEM] * len(blocks),
        out_specs=VMEM,
        compiler_params=params(4),
        name="sum_blocks",
    )(*blocks)


def halves(wide):
    cut = 128 * pl.cdiv(wide // 128, 2)
    return slice(0, cut), slice(cut, wide)


def blend_kernel(chips, weight_ref, *refs):
    *refs, out_hbm, out_ref, sem = refs
    count, features = out_ref.shape
    wide = features // SEGMENTS
    own = refs[0][...]
    for ref in refs[1:chips]:
        own = own + ref[...].astype(jnp.float32)
    high = own.astype(jnp.bfloat16).astype(jnp.float32)
    terms = [high, own - high, high]
    for ref in refs[chips:]:
        terms += [ref[...].astype(jnp.float32)] * 2
    rows = jnp.concatenate(terms, axis=0).astype(jnp.bfloat16)
    copies = []
    for columns in halves(wide):
        size = columns.stop - columns.start
        total = jnp.dot(weight_ref[...], rows[:, columns], preferred_element_type=jnp.float32)
        for s in range(SEGMENTS):
            part = pl.ds(s * wide + columns.start, size)
            out_ref[:, part] = total[s * count : (s + 1) * count].astype(jnp.bfloat16)
            copies.append(
                pltpu.make_async_copy(
                    out_ref.at[:, part], out_hbm.at[:, part], sem.at[len(copies)]
                )
            )
            copies[-1].start()
    wait_all(copies)


def blend(weights, own_blocks, other_blocks, count):
    chips = len(own_blocks)
    features = own_blocks[0].shape[1] * SEGMENTS
    return pl.pallas_call(
        functools.partial(blend_kernel, chips),
        out_shape=jax.ShapeDtypeStruct((count, features), jnp.bfloat16),
        in_specs=[VMEM] * (1 + chips + len(other_blocks)),
        out_specs=HBM,
        scratch_shapes=[
            pltpu.VMEM((count, features), jnp.bfloat16),
            pltpu.SemaphoreType.DMA((2 * SEGMENTS,)),
        ],
        compiler_params=params(16),
        name="blend",
    )(weights, *own_blocks, *other_blocks)


def body(tokens, expert_ids, route_logits, w_gate, w_up, w_down):
    devices = lax.axis_size("expert")
    teams = devices // SPLIT
    chips = SPLIT // CORES
    other_core = [(i, i ^ 1) for i in range(devices)]
    other_chip = [[(i, i ^ (m * CORES)) for i in range(devices)] for m in range(chips)]
    packed, table = pack_rows(expert_ids.T, route_logits.T, tokens, teams)
    def gather(block):
        return [block] + [lax.ppermute(block, "expert", other_chip[m]) for m in range(1, chips)]

    own = gather(packed[0])
    crowds = []
    for k in range(1, teams):
        pairs = [(i, (i + k * SPLIT) % devices) for i in range(devices)]
        block = lax.ppermute(packed[k], "expert", pairs)
        if k == teams - 1:
            block, table = lax.optimization_barrier((block, table))
            weights = blend_weights(table, teams)
        crowds.append(gather(block))
    own, crowds, weights = lax.optimization_barrier((own, crowds, weights))
    own = join(own)
    first = unpack(own, lax.ppermute(own, "expert", other_core))
    pieces = []
    for crowd in crowds:
        crowd = join(crowd)
        pieces += [crowd, lax.ppermute(crowd, "expert", other_core)]
    *given, hidden = expert_half(first, pieces, w_gate, w_up, w_down)
    taken = [lax.ppermute(piece, "expert", other_core) for piece in given]
    kept = kept_half(hidden, w_down)
    others = []
    for k in range(1, teams):
        parts = add_cores(kept, taken[k], k, chips)
        parts, taken[0] = lax.optimization_barrier((parts, taken[0]))
        team = [parts[0]]
        for m in range(1, chips):
            team.append(lax.ppermute(parts[m], "expert", other_chip[m]))
        pairs = [(i, (i - k * SPLIT) % devices) for i in range(devices)]
        others.append(lax.ppermute(sum_blocks(team), "expert", pairs))
    parts = add_cores(kept, taken[0], 0, chips)
    own = [parts[0]]
    for m in range(1, chips):
        own.append(lax.ppermute(parts[m], "expert", other_chip[m]))
    return blend(weights, own, others, tokens.shape[0])


def solution(mesh):
    placed = (
        P(("groups", "expert"), None),
        P(("groups", "expert"), None),
        P(("groups", "expert"), None),
        P(None, "expert"),
        P(None, "expert"),
        P("expert", None),
    )
    return jax.shard_map(
        body, mesh=mesh, in_specs=placed, out_specs=P(("groups", "expert"), None), check_vma=False
    )
```

```python
import functools

import jax
import jax.numpy as jnp
from jax import lax
from jax.experimental import pallas as pl
from jax.experimental.pallas import tpu as pltpu
from jax.sharding import PartitionSpec as P

SPLIT = 8
CAP = 5
CORES = 2
SEGMENTS = 8

route_scale = 2.5

VMEM = pl.BlockSpec(memory_space=pltpu.VMEM)
HBM = pl.BlockSpec(memory_space=pltpu.HBM)
MIB = 1024 * 1024


def hits(ids, mine, teams):
    count = ids.shape[1]
    row = lax.broadcasted_iota(jnp.int32, (8 * pl.cdiv(teams, 8), count), 0)
    wanted = lax.rem(mine + row, teams)
    hit = jnp.zeros(row.shape, jnp.int32)
    for j in range(ids.shape[0]):
        hit = hit + jnp.where(ids[j : j + 1, :] == wanted, 1, 0)
    hit = jnp.where(row < teams, hit, 0).astype(jnp.float32)
    before = lax.broadcasted_iota(jnp.int32, (count, count), 0)
    after = lax.broadcasted_iota(jnp.int32, (count, count), 1)
    earlier = jnp.where(before < after, 1.0, 0.0).astype(jnp.bfloat16)
    slot = jnp.dot(hit.astype(jnp.bfloat16), earlier, preferred_element_type=jnp.float32)
    return hit, jnp.where(hit > 0, slot, -1.0)


def fifth(shape, axis):
    at = lax.broadcasted_iota(jnp.int32, shape, axis)
    segment = jnp.zeros(shape, jnp.int32)
    for s in range(1, SEGMENTS):
        segment = segment + jnp.where(at >= s * CAP, 1, 0)
    return segment, (at - CAP * segment).astype(jnp.float32)


def params(mib):
    return pltpu.CompilerParams(vmem_limit_bytes=int(mib * MIB))


def bring(source, target, semaphores, parts):
    step = source.shape[0] // parts
    copies = []
    for i in range(parts):
        rows = pl.ds(i * step, step)
        copies.append(pltpu.make_async_copy(source.at[rows], target.at[rows], semaphores.at[i]))
        copies[-1].start()
    return copies


def wait_all(copies):
    for copy in copies:
        copy.wait()


def pack_kernel(teams, ids_hbm, logits_hbm, tokens_hbm, *refs):
    *out_refs, table_ref, ids_ref, logits_ref, tokens_ref, ids_sem, logits_sem, tokens_sem = refs
    ids_copy = bring(ids_hbm, ids_ref, ids_sem, 1)
    tokens_copy = bring(tokens_hbm, tokens_ref, tokens_sem, 4)
    logits_copy = bring(logits_hbm, logits_ref, logits_sem, 1)
    wait_all(ids_copy)
    mine = lax.axis_index("expert") // SPLIT
    ids = ids_ref[...]
    hit, slot = hits(ids, mine, teams)
    wait_all(logits_copy)
    lifted = jax.nn.sigmoid(logits_ref[...])
    gates = route_scale * lifted / jnp.sum(lifted, axis=0, keepdims=True)
    row = lax.broadcasted_iota(jnp.int32, hit.shape, 0)
    wanted = lax.rem(mine + row, teams)
    gate = jnp.zeros(hit.shape, jnp.float32)
    for j in range(ids.shape[0]):
        gate = gate + jnp.where(ids[j : j + 1, :] == wanted, gates[j : j + 1, :], 0.0)
    table_ref[: hit.shape[0], :] = slot
    table_ref[hit.shape[0] :, :] = gate
    count, features = tokens_ref.shape
    wide = features // SEGMENTS
    tall = CAP * SEGMENTS
    segment, place = fifth((tall, 1), 0)
    column = lax.broadcasted_iota(jnp.int32, (1, SEGMENTS * count), 1)
    same = segment == column // count
    picks = []
    for k in range(teams):
        slots = jnp.concatenate([slot[k : k + 1, :]] * SEGMENTS, axis=1)
        picks.append(jnp.where(same & (slots == place), 1.0, 0.0))
    wait_all(tokens_copy)
    stacked = jnp.concatenate(
        [tokens_ref[:, s * wide : (s + 1) * wide] for s in range(SEGMENTS)], axis=0
    )
    packed = jnp.dot(
        jnp.concatenate(picks, axis=0).astype(jnp.bfloat16),
        stacked,
        preferred_element_type=jnp.float32,
    )
    for k in range(teams):
        out_refs[k][...] = packed[k * tall : (k + 1) * tall].astype(jnp.bfloat16)


def pack_rows(ids, logits, tokens, teams):
    wide = tokens.shape[1] // SEGMENTS
    block = jax.ShapeDtypeStruct((CAP * SEGMENTS, wide), jnp.bfloat16)
    table = jax.ShapeDtypeStruct((16 * pl.cdiv(teams, 8), ids.shape[1]), jnp.float32)
    *packed, table = pl.pallas_call(
        functools.partial(pack_kernel, teams),
        out_shape=[block] * teams + [table],
        in_specs=[HBM] * 3,
        out_specs=[VMEM] * (teams + 1),
        scratch_shapes=[
            pltpu.VMEM(ids.shape, ids.dtype),
            pltpu.VMEM(logits.shape, logits.dtype),
            pltpu.VMEM(tokens.shape, tokens.dtype),
            pltpu.SemaphoreType.DMA((1,)),
            pltpu.SemaphoreType.DMA((1,)),
            pltpu.SemaphoreType.DMA((4,)),
        ],
        name="pack_rows",
    )(ids, logits, tokens)
    return packed, table


def weight_kernel(teams, table_ref, out_ref):
    rows, count = table_ref.shape
    slot = jnp.transpose(table_ref[: rows // 2, :])
    gate = jnp.transpose(table_ref[rows // 2 :, :])
    tall = CAP * SEGMENTS
    depth = out_ref.shape[1]
    column = lax.broadcasted_iota(jnp.int32, (1, depth), 1)
    part = jnp.zeros((1, depth), jnp.int32)
    for g in range(1, depth // tall):
        part = part + jnp.where(column >= g * tall, 1, 0)
    column = column - tall * part
    segment = jnp.zeros((1, depth), jnp.int32)
    for s in range(1, SEGMENTS):
        segment = segment + jnp.where(column >= s * CAP, 1, 0)
    place = (column - CAP * segment).astype(jnp.float32)
    team = jnp.where(part < 3, 0, (part - 1) >> 1)
    low = jnp.where(part < 3, part >> 1, (part - 3) & 1) == 1
    for s in range(SEGMENTS):
        full = jnp.zeros((count, depth), jnp.float32)
        for k in range(teams):
            chosen = (team == k) & (segment == s) & (slot[:, k : k + 1] == place)
            full = full + jnp.where(chosen, gate[:, k : k + 1], 0.0)
        high = full.astype(jnp.bfloat16).astype(jnp.float32)
        out_ref[s * count : (s + 1) * count, :] = jnp.where(low, full - high, high).astype(
            jnp.bfloat16
        )


def blend_weights(table, teams):
    shape = (SEGMENTS * table.shape[1], CAP * SEGMENTS * (1 + 2 * teams))
    return pl.pallas_call(
        functools.partial(weight_kernel, teams),
        out_shape=jax.ShapeDtypeStruct(shape, jnp.bfloat16),
        in_specs=[VMEM],
        out_specs=VMEM,
        compiler_params=params(4 + teams),
        cost_estimate=pl.CostEstimate(flops=6 * 10**9, bytes_accessed=8 * MIB, transcendentals=0),
        name="blend_weights",
    )(table)


def join_kernel(*refs):
    tall = refs[0].shape[0]
    for i, ref in enumerate(refs[:-1]):
        refs[-1][i * tall : (i + 1) * tall, :] = ref[...]


def join(blocks):
    tall, wide = blocks[0].shape
    return pl.pallas_call(
        join_kernel,
        out_shape=jax.ShapeDtypeStruct((tall * len(blocks), wide), blocks[0].dtype),
        in_specs=[VMEM] * len(blocks),
        out_specs=VMEM,
        compiler_params=params(4),
        name="join",
    )(*blocks)


def packed_down(hidden, down_ref, out_ref, flat):
    count, wide = flat.shape[1:]
    tall = CAP * SEGMENTS
    for s in range(SEGMENTS):
        slot = flat.at[s % 2]
        slot[...] = jnp.dot(
            hidden, down_ref[:, s * wide : (s + 1) * wide], preferred_element_type=jnp.float32
        )
        for b in range(count // CAP):
            start = b * tall + s * CAP
            out_ref[start : start + CAP, :] = slot[b * CAP : (b + 1) * CAP, :]


def unpack_kernel(own_ref, other_ref, out_ref, packed):
    tall = CAP * SEGMENTS
    half = own_ref.shape[0]
    wide = own_ref.shape[1]
    packed[:half, :] = own_ref[...].astype(jnp.float32)
    packed[half:, :] = other_ref[...].astype(jnp.float32)
    for s in range(SEGMENTS):
        for b in range(2 * half // tall):
            start = b * tall + s * CAP
            out_ref[b * CAP : (b + 1) * CAP, s * wide : (s + 1) * wide] = packed[
                start : start + CAP, :
            ]


def unpack(own, other):
    rows, wide = own.shape
    return pl.pallas_call(
        unpack_kernel,
        out_shape=jax.ShapeDtypeStruct((2 * rows // SEGMENTS, wide * SEGMENTS), jnp.float32),
        in_specs=[VMEM] * 2,
        out_specs=VMEM,
        scratch_shapes=[pltpu.VMEM((2 * rows, wide), jnp.float32)],
        compiler_params=params(6),
        name="unpack",
    )(own, other)


def expert_kernel(teams, first_ref, *refs):
    pieces = refs[: 2 * (teams - 1)]
    gate_ref, up_ref, down_ref = refs[2 * (teams - 1) : 2 * teams + 1]
    *given_refs, hidden_ref, packed, flat, out, act = refs[2 * teams + 1 :]
    tall = CAP * SEGMENTS
    wide = packed.shape[1]
    units = gate_ref.shape[1]
    start = 0
    for ref in pieces:
        packed[start : start + ref.shape[0], :] = ref[...].astype(jnp.float32)
        start += ref.shape[0]
    known = first_ref.shape[0]
    count = known * teams
    gate_act = jnp.zeros((count, units), jnp.float32)
    up_act = jnp.zeros((count, units), jnp.float32)
    for s in range(SEGMENTS):
        slot = flat.at[s % 2]
        columns = slice(s * wide, (s + 1) * wide)
        slot[:known, :] = first_ref[:, columns]
        for b in range((count - known) // CAP):
            start = b * tall + s * CAP
            slot[known + b * CAP : known + (b + 1) * CAP, :] = packed[start : start + CAP, :]
        rows = slot[...].astype(jnp.bfloat16)
        gate_act += jnp.dot(rows, gate_ref[columns, :], preferred_element_type=jnp.float32)
        up_act += jnp.dot(rows, up_ref[columns, :], preferred_element_type=jnp.float32)
    act[:count, :] = jax.nn.silu(gate_act) * up_act
    half = known // 2
    for k in range(teams):
        for core in range(CORES):
            source = (CORES * k + core) * half
            target = count + (core * teams + k) * half
            act[target : target + half, :] = act[source : source + half, :]
    hidden = act[count:, :].astype(jnp.bfloat16)
    half = count // 2
    hidden_ref[...] = hidden[:half]
    packed_down(hidden[half:], down_ref, out, flat.at[:, :half, :])
    for k, given_ref in enumerate(given_refs):
        rows = given_ref.shape[0]
        given_ref[...] = out[k * rows : (k + 1) * rows, :].astype(jnp.bfloat16)


def expert_half(first, pieces, w_gate, w_up, w_down):
    teams = 1 + len(pieces) // 2
    block, wide = pieces[0].shape
    features, units = w_gate.shape
    rows = first.shape[0] * teams
    return pl.pallas_call(
        functools.partial(expert_kernel, teams),
        out_shape=[jax.ShapeDtypeStruct((block, wide), jnp.bfloat16)] * teams
        + [jax.ShapeDtypeStruct((rows // 2, units), jnp.bfloat16)],
        in_specs=[VMEM] * (len(pieces) + 4),
        out_specs=[VMEM] * (teams + 1),
        scratch_shapes=[
            pltpu.VMEM((block * len(pieces), wide), jnp.float32),
            pltpu.VMEM((2, rows, wide), jnp.float32),
            pltpu.VMEM((block * teams, wide), jnp.float32),
            pltpu.VMEM((2 * rows, units), jnp.float32),
        ],
        compiler_params=params(16 + 4 * teams),
        cost_estimate=pl.CostEstimate(
            flops=5 * rows * units * features,
            bytes_accessed=6 * features * units,
            transcendentals=rows * units,
        ),
        name="expert_half",
    )(first, *pieces, w_gate, w_up, w_down)


def kept_kernel(hidden_ref, down_ref, kept_ref, flat):
    packed_down(hidden_ref[...], down_ref, kept_ref, flat)


def kept_half(hidden, w_down):
    count, units = hidden.shape
    features = w_down.shape[1]
    wide = features // SEGMENTS
    return pl.pallas_call(
        kept_kernel,
        out_shape=jax.ShapeDtypeStruct((count * SEGMENTS, wide), jnp.float32),
        in_specs=[VMEM] * 2,
        out_specs=VMEM,
        scratch_shapes=[pltpu.VMEM((2, count, wide), jnp.float32)],
        compiler_params=params(8 + count // 10),
        cost_estimate=pl.CostEstimate(
            flops=2 * count * units * features,
            bytes_accessed=2 * features * units,
            transcendentals=0,
        ),
        name="kept_half",
    )(hidden, w_down)


def add_kernel(first, kept_ref, taken_ref, *out_refs):
    tall = out_refs[0].shape[0]
    for b, out_ref in enumerate(out_refs):
        rows = slice(b * tall, (b + 1) * tall)
        total = kept_ref[first + b * tall : first + (b + 1) * tall, :] + taken_ref[
            rows, :
        ].astype(jnp.float32)
        out_ref[...] = total.astype(out_ref.dtype)


def add_cores(kept, taken, k, chips):
    shape = (CAP * SEGMENTS, kept.shape[1])
    outs = [jax.ShapeDtypeStruct(shape, jnp.bfloat16 if m else jnp.float32) for m in range(chips)]
    return pl.pallas_call(
        functools.partial(add_kernel, k * taken.shape[0]),
        out_shape=outs,
        in_specs=[VMEM] * 2,
        out_specs=[VMEM] * len(outs),
        compiler_params=params(6),
        name="add_cores",
    )(kept, taken)


def sum_kernel(*refs):
    total = refs[0][...]
    for ref in refs[1:-1]:
        total = total + ref[...].astype(jnp.float32)
    refs[-1][...] = total.astype(refs[-1].dtype)


def sum_blocks(blocks):
    return pl.pallas_call(
        sum_kernel,
        out_shape=jax.ShapeDtypeStruct(blocks[0].shape, jnp.bfloat16),
        in_specs=[VMEM] * len(blocks),
        out_specs=VMEM,
        compiler_params=params(4),
        name="sum_blocks",
    )(*blocks)


def halves(wide):
    cut = 128 * pl.cdiv(wide // 128, 2)
    return slice(0, cut), slice(cut, wide)


def blend_kernel(chips, weight_ref, *refs):
    *refs, out_hbm, out_ref, sem = refs
    count, features = out_ref.shape
    wide = features // SEGMENTS
    own = refs[0][...]
    for ref in refs[1:chips]:
        own = own + ref[...].astype(jnp.float32)
    high = own.astype(jnp.bfloat16).astype(jnp.float32)
    terms = [high, own - high, high]
    for ref in refs[chips:]:
        terms += [ref[...].astype(jnp.float32)] * 2
    rows = jnp.concatenate(terms, axis=0).astype(jnp.bfloat16)
    copies = []
    for columns in halves(wide):
        size = columns.stop - columns.start
        total = jnp.dot(weight_ref[...], rows[:, columns], preferred_element_type=jnp.float32)
        for s in range(SEGMENTS):
            part = pl.ds(s * wide + columns.start, size)
            out_ref[:, part] = total[s * count : (s + 1) * count].astype(jnp.bfloat16)
            copies.append(
                pltpu.make_async_copy(
                    out_ref.at[:, part], out_hbm.at[:, part], sem.at[len(copies)]
                )
            )
            copies[-1].start()
    wait_all(copies)


def blend(weights, own_blocks, other_blocks, count):
    chips = len(own_blocks)
    features = own_blocks[0].shape[1] * SEGMENTS
    return pl.pallas_call(
        functools.partial(blend_kernel, chips),
        out_shape=jax.ShapeDtypeStruct((count, features), jnp.bfloat16),
        in_specs=[VMEM] * (1 + chips + len(other_blocks)),
        out_specs=HBM,
        scratch_shapes=[
            pltpu.VMEM((count, features), jnp.bfloat16),
            pltpu.SemaphoreType.DMA((2 * SEGMENTS,)),
        ],
        compiler_params=params(16),
        name="blend",
    )(weights, *own_blocks, *other_blocks)


def body(tokens, expert_ids, route_logits, w_gate, w_up, w_down):
    devices = lax.axis_size("expert")
    teams = devices // SPLIT
    chips = SPLIT // CORES
    other_core = [(i, i ^ 1) for i in range(devices)]
    other_chip = [[(i, i ^ (m * CORES)) for i in range(devices)] for m in range(chips)]
    packed, table = pack_rows(expert_ids.T, route_logits.T, tokens, teams)
    def gather(block):
        return [block] + [lax.ppermute(block, "expert", other_chip[m]) for m in range(1, chips)]

    own = gather(packed[0])
    crowds = []
    for k in range(1, teams):
        pairs = [(i, (i + k * SPLIT) % devices) for i in range(devices)]
        block = lax.ppermute(packed[k], "expert", pairs)
        if k == teams - 1:
            block, table = lax.optimization_barrier((block, table))
            weights = blend_weights(table, teams)
        crowds.append(gather(block))
    own, weights, crowds[-1][-1] = lax.optimization_barrier((own, weights, crowds[-1][-1]))
    own = join(own)
    first = unpack(own, lax.ppermute(own, "expert", other_core))
    pieces = []
    for crowd in crowds:
        crowd = join(crowd)
        pieces += [crowd, lax.ppermute(crowd, "expert", other_core)]
    *given, hidden = expert_half(first, pieces, w_gate, w_up, w_down)
    taken = [lax.ppermute(piece, "expert", other_core) for piece in given]
    kept = kept_half(hidden, w_down)
    others = []
    for k in range(1, teams):
        parts = add_cores(kept, taken[k], k, chips)
        parts, later = lax.optimization_barrier((parts, kept))
        team = [parts[0]]
        for m in range(1, chips):
            team.append(lax.ppermute(parts[m], "expert", other_chip[m]))
        pairs = [(i, (i - k * SPLIT) % devices) for i in range(devices)]
        others.append(lax.ppermute(sum_blocks(team), "expert", pairs))
    parts = add_cores(later, taken[0], 0, chips)
    own = [parts[0]]
    for m in range(1, chips):
        own.append(lax.ppermute(parts[m], "expert", other_chip[m]))
    return blend(weights, own, others, tokens.shape[0])


def solution(mesh):
    placed = (
        P(("groups", "expert"), None),
        P(("groups", "expert"), None),
        P(("groups", "expert"), None),
        P(None, "expert"),
        P(None, "expert"),
        P("expert", None),
    )
    return jax.shard_map(
        body, mesh=mesh, in_specs=placed, out_specs=P(("groups", "expert"), None), check_vma=False
    )
```

```python
import functools

import jax
import jax.numpy as jnp
from jax import lax
from jax.experimental import pallas as pl
from jax.experimental.pallas import tpu as pltpu
from jax.sharding import PartitionSpec as P

SPLIT = 8
CAP = 5
CORES = 2
SEGMENTS = 8

route_scale = 2.5

VMEM = pl.BlockSpec(memory_space=pltpu.VMEM)
HBM = pl.BlockSpec(memory_space=pltpu.HBM)
MIB = 1024 * 1024


def hits(ids, mine, teams):
    count = ids.shape[1]
    row = lax.broadcasted_iota(jnp.int32, (8 * pl.cdiv(teams, 8), count), 0)
    wanted = lax.rem(mine + row, teams)
    hit = jnp.zeros(row.shape, jnp.int32)
    for j in range(ids.shape[0]):
        hit = hit + jnp.where(ids[j : j + 1, :] == wanted, 1, 0)
    hit = jnp.where(row < teams, hit, 0).astype(jnp.float32)
    before = lax.broadcasted_iota(jnp.int32, (count, count), 0)
    after = lax.broadcasted_iota(jnp.int32, (count, count), 1)
    earlier = jnp.where(before < after, 1.0, 0.0).astype(jnp.bfloat16)
    slot = jnp.dot(hit.astype(jnp.bfloat16), earlier, preferred_element_type=jnp.float32)
    return hit, jnp.where(hit > 0, slot, -1.0)


def fifth(shape, axis):
    at = lax.broadcasted_iota(jnp.int32, shape, axis)
    segment = jnp.zeros(shape, jnp.int32)
    for s in range(1, SEGMENTS):
        segment = segment + jnp.where(at >= s * CAP, 1, 0)
    return segment, (at - CAP * segment).astype(jnp.float32)


def params(mib):
    return pltpu.CompilerParams(vmem_limit_bytes=int(mib * MIB))


def bring(source, target, semaphores, parts):
    step = source.shape[0] // parts
    copies = []
    for i in range(parts):
        rows = pl.ds(i * step, step)
        copies.append(pltpu.make_async_copy(source.at[rows], target.at[rows], semaphores.at[i]))
        copies[-1].start()
    return copies


def wait_all(copies):
    for copy in copies:
        copy.wait()


def pack_kernel(teams, ids_hbm, logits_hbm, tokens_hbm, *refs):
    *out_refs, table_ref, ids_ref, logits_ref, tokens_ref, ids_sem, logits_sem, tokens_sem = refs
    ids_copy = bring(ids_hbm, ids_ref, ids_sem, 1)
    tokens_copy = bring(tokens_hbm, tokens_ref, tokens_sem, 4)
    logits_copy = bring(logits_hbm, logits_ref, logits_sem, 1)
    wait_all(ids_copy)
    mine = lax.axis_index("expert") // SPLIT
    ids = ids_ref[...]
    hit, slot = hits(ids, mine, teams)
    wait_all(logits_copy)
    lifted = jax.nn.sigmoid(logits_ref[...])
    gates = route_scale * lifted / jnp.sum(lifted, axis=0, keepdims=True)
    row = lax.broadcasted_iota(jnp.int32, hit.shape, 0)
    wanted = lax.rem(mine + row, teams)
    gate = jnp.zeros(hit.shape, jnp.float32)
    for j in range(ids.shape[0]):
        gate = gate + jnp.where(ids[j : j + 1, :] == wanted, gates[j : j + 1, :], 0.0)
    table_ref[: hit.shape[0], :] = slot
    table_ref[hit.shape[0] :, :] = gate
    count, features = tokens_ref.shape
    wide = features // SEGMENTS
    tall = CAP * SEGMENTS
    segment, place = fifth((tall, 1), 0)
    column = lax.broadcasted_iota(jnp.int32, (1, SEGMENTS * count), 1)
    same = segment == column // count
    picks = []
    for k in range(teams):
        slots = jnp.concatenate([slot[k : k + 1, :]] * SEGMENTS, axis=1)
        picks.append(jnp.where(same & (slots == place), 1.0, 0.0))
    wait_all(tokens_copy)
    stacked = jnp.concatenate(
        [tokens_ref[:, s * wide : (s + 1) * wide] for s in range(SEGMENTS)], axis=0
    )
    packed = jnp.dot(
        jnp.concatenate(picks, axis=0).astype(jnp.bfloat16),
        stacked,
        preferred_element_type=jnp.float32,
    )
    for k in range(teams):
        out_refs[k][...] = packed[k * tall : (k + 1) * tall].astype(jnp.bfloat16)


def pack_rows(ids, logits, tokens, teams):
    wide = tokens.shape[1] // SEGMENTS
    block = jax.ShapeDtypeStruct((CAP * SEGMENTS, wide), jnp.bfloat16)
    table = jax.ShapeDtypeStruct((16 * pl.cdiv(teams, 8), ids.shape[1]), jnp.float32)
    *packed, table = pl.pallas_call(
        functools.partial(pack_kernel, teams),
        out_shape=[block] * teams + [table],
        in_specs=[HBM] * 3,
        out_specs=[VMEM] * (teams + 1),
        scratch_shapes=[
            pltpu.VMEM(ids.shape, ids.dtype),
            pltpu.VMEM(logits.shape, logits.dtype),
            pltpu.VMEM(tokens.shape, tokens.dtype),
            pltpu.SemaphoreType.DMA((1,)),
            pltpu.SemaphoreType.DMA((1,)),
            pltpu.SemaphoreType.DMA((4,)),
        ],
        name="pack_rows",
    )(ids, logits, tokens)
    return packed, table


def weight_kernel(teams, table_ref, out_ref):
    rows, count = table_ref.shape
    slot = jnp.transpose(table_ref[: rows // 2, :])
    gate = jnp.transpose(table_ref[rows // 2 :, :])
    tall = CAP * SEGMENTS
    depth = out_ref.shape[1]
    column = lax.broadcasted_iota(jnp.int32, (1, depth), 1)
    part = jnp.zeros((1, depth), jnp.int32)
    for g in range(1, depth // tall):
        part = part + jnp.where(column >= g * tall, 1, 0)
    column = column - tall * part
    segment = jnp.zeros((1, depth), jnp.int32)
    for s in range(1, SEGMENTS):
        segment = segment + jnp.where(column >= s * CAP, 1, 0)
    place = (column - CAP * segment).astype(jnp.float32)
    team = jnp.where(part < 3, 0, (part - 1) >> 1)
    low = jnp.where(part < 3, part >> 1, (part - 3) & 1) == 1
    for s in range(SEGMENTS):
        full = jnp.zeros((count, depth), jnp.float32)
        for k in range(teams):
            chosen = (team == k) & (segment == s) & (slot[:, k : k + 1] == place)
            full = full + jnp.where(chosen, gate[:, k : k + 1], 0.0)
        high = full.astype(jnp.bfloat16).astype(jnp.float32)
        out_ref[s * count : (s + 1) * count, :] = jnp.where(low, full - high, high).astype(
            jnp.bfloat16
        )


def blend_weights(table, teams):
    shape = (SEGMENTS * table.shape[1], CAP * SEGMENTS * (1 + 2 * teams))
    return pl.pallas_call(
        functools.partial(weight_kernel, teams),
        out_shape=jax.ShapeDtypeStruct(shape, jnp.bfloat16),
        in_specs=[VMEM],
        out_specs=VMEM,
        compiler_params=params(4 + teams),
        cost_estimate=pl.CostEstimate(flops=6 * 10**9, bytes_accessed=8 * MIB, transcendentals=0),
        name="blend_weights",
    )(table)


def join_kernel(*refs):
    tall = refs[0].shape[0]
    for i, ref in enumerate(refs[:-1]):
        refs[-1][i * tall : (i + 1) * tall, :] = ref[...]


def join(blocks):
    tall, wide = blocks[0].shape
    return pl.pallas_call(
        join_kernel,
        out_shape=jax.ShapeDtypeStruct((tall * len(blocks), wide), blocks[0].dtype),
        in_specs=[VMEM] * len(blocks),
        out_specs=VMEM,
        compiler_params=params(4),
        name="join",
    )(*blocks)


def packed_down(hidden, down_ref, out_ref, flat):
    count, wide = flat.shape[1:]
    tall = CAP * SEGMENTS
    for s in range(SEGMENTS):
        slot = flat.at[s % 2]
        slot[...] = jnp.dot(
            hidden, down_ref[:, s * wide : (s + 1) * wide], preferred_element_type=jnp.float32
        )
        for b in range(count // CAP):
            start = b * tall + s * CAP
            out_ref[start : start + CAP, :] = slot[b * CAP : (b + 1) * CAP, :]


def unpack_kernel(own_ref, other_ref, out_ref, packed):
    tall = CAP * SEGMENTS
    half = own_ref.shape[0]
    wide = own_ref.shape[1]
    packed[:half, :] = own_ref[...].astype(jnp.float32)
    packed[half:, :] = other_ref[...].astype(jnp.float32)
    for s in range(SEGMENTS):
        for b in range(2 * half // tall):
            start = b * tall + s * CAP
            out_ref[b * CAP : (b + 1) * CAP, s * wide : (s + 1) * wide] = packed[
                start : start + CAP, :
            ]


def unpack(own, other):
    rows, wide = own.shape
    return pl.pallas_call(
        unpack_kernel,
        out_shape=jax.ShapeDtypeStruct((2 * rows // SEGMENTS, wide * SEGMENTS), jnp.float32),
        in_specs=[VMEM] * 2,
        out_specs=VMEM,
        scratch_shapes=[pltpu.VMEM((2 * rows, wide), jnp.float32)],
        compiler_params=params(6),
        name="unpack",
    )(own, other)


def expert_kernel(teams, first_ref, *refs):
    pieces = refs[: 2 * (teams - 1)]
    gate_ref, up_ref, down_ref = refs[2 * (teams - 1) : 2 * teams + 1]
    *given_refs, hidden_ref, packed, flat, out, act = refs[2 * teams + 1 :]
    tall = CAP * SEGMENTS
    wide = packed.shape[1]
    units = gate_ref.shape[1]
    start = 0
    for ref in pieces:
        packed[start : start + ref.shape[0], :] = ref[...].astype(jnp.float32)
        start += ref.shape[0]
    known = first_ref.shape[0]
    count = known * teams
    gate_act = jnp.zeros((count, units), jnp.float32)
    up_act = jnp.zeros((count, units), jnp.float32)
    for s in range(SEGMENTS):
        slot = flat.at[s % 2]
        columns = slice(s * wide, (s + 1) * wide)
        slot[:known, :] = first_ref[:, columns]
        for b in range((count - known) // CAP):
            start = b * tall + s * CAP
            slot[known + b * CAP : known + (b + 1) * CAP, :] = packed[start : start + CAP, :]
        rows = slot[...].astype(jnp.bfloat16)
        gate_act += jnp.dot(rows, gate_ref[columns, :], preferred_element_type=jnp.float32)
        up_act += jnp.dot(rows, up_ref[columns, :], preferred_element_type=jnp.float32)
    act[:count, :] = jax.nn.silu(gate_act) * up_act
    half = known // 2
    for k in range(teams):
        for core in range(CORES):
            source = (CORES * k + core) * half
            target = count + (core * teams + k) * half
            act[target : target + half, :] = act[source : source + half, :]
    hidden = act[count:, :].astype(jnp.bfloat16)
    half = count // 2
    hidden_ref[...] = hidden[:half]
    packed_down(hidden[half:], down_ref, out, flat.at[:, :half, :])
    for k, given_ref in enumerate(given_refs):
        rows = given_ref.shape[0]
        given_ref[...] = out[k * rows : (k + 1) * rows, :].astype(jnp.bfloat16)


def expert_half(first, pieces, w_gate, w_up, w_down):
    teams = 1 + len(pieces) // 2
    block, wide = pieces[0].shape
    features, units = w_gate.shape
    rows = first.shape[0] * teams
    return pl.pallas_call(
        functools.partial(expert_kernel, teams),
        out_shape=[jax.ShapeDtypeStruct((block, wide), jnp.bfloat16)] * teams
        + [jax.ShapeDtypeStruct((rows // 2, units), jnp.bfloat16)],
        in_specs=[VMEM] * (len(pieces) + 4),
        out_specs=[VMEM] * (teams + 1),
        scratch_shapes=[
            pltpu.VMEM((block * len(pieces), wide), jnp.float32),
            pltpu.VMEM((2, rows, wide), jnp.float32),
            pltpu.VMEM((block * teams, wide), jnp.float32),
            pltpu.VMEM((2 * rows, units), jnp.float32),
        ],
        compiler_params=params(16 + 4 * teams),
        cost_estimate=pl.CostEstimate(
            flops=5 * rows * units * features,
            bytes_accessed=6 * features * units,
            transcendentals=rows * units,
        ),
        name="expert_half",
    )(first, *pieces, w_gate, w_up, w_down)


def kept_kernel(hidden_ref, down_ref, kept_ref, flat):
    packed_down(hidden_ref[...], down_ref, kept_ref, flat)


def kept_half(hidden, w_down):
    count, units = hidden.shape
    features = w_down.shape[1]
    wide = features // SEGMENTS
    return pl.pallas_call(
        kept_kernel,
        out_shape=jax.ShapeDtypeStruct((count * SEGMENTS, wide), jnp.float32),
        in_specs=[VMEM] * 2,
        out_specs=VMEM,
        scratch_shapes=[pltpu.VMEM((2, count, wide), jnp.float32)],
        compiler_params=params(8 + count // 10),
        cost_estimate=pl.CostEstimate(
            flops=2 * count * units * features,
            bytes_accessed=2 * features * units,
            transcendentals=0,
        ),
        name="kept_half",
    )(hidden, w_down)


def add_kernel(first, kept_ref, taken_ref, *out_refs):
    tall = out_refs[0].shape[0]
    for b, out_ref in enumerate(out_refs):
        rows = slice(b * tall, (b + 1) * tall)
        total = kept_ref[first + b * tall : first + (b + 1) * tall, :] + taken_ref[
            rows, :
        ].astype(jnp.float32)
        out_ref[...] = total.astype(out_ref.dtype)


def add_cores(kept, taken, k, chips):
    shape = (CAP * SEGMENTS, kept.shape[1])
    outs = [jax.ShapeDtypeStruct(shape, jnp.bfloat16 if m else jnp.float32) for m in range(chips)]
    return pl.pallas_call(
        functools.partial(add_kernel, k * taken.shape[0]),
        out_shape=outs,
        in_specs=[VMEM] * 2,
        out_specs=[VMEM] * len(outs),
        compiler_params=params(6),
        name="add_cores",
    )(kept, taken)


def sum_kernel(*refs):
    total = refs[0][...]
    for ref in refs[1:-1]:
        total = total + ref[...].astype(jnp.float32)
    refs[-1][...] = total.astype(refs[-1].dtype)


def sum_blocks(blocks):
    return pl.pallas_call(
        sum_kernel,
        out_shape=jax.ShapeDtypeStruct(blocks[0].shape, jnp.bfloat16),
        in_specs=[VMEM] * len(blocks),
        out_specs=VMEM,
        compiler_params=params(4),
        name="sum_blocks",
    )(*blocks)


def halves(wide):
    cut = 128 * pl.cdiv(wide // 128, 2)
    return slice(0, cut), slice(cut, wide)


def blend_kernel(chips, weight_ref, *refs):
    *refs, out_hbm, out_ref, sem = refs
    count, features = out_ref.shape
    wide = features // SEGMENTS
    own = refs[0][...]
    for ref in refs[1:chips]:
        own = own + ref[...].astype(jnp.float32)
    high = own.astype(jnp.bfloat16).astype(jnp.float32)
    terms = [high, own - high, high]
    for ref in refs[chips:]:
        terms += [ref[...].astype(jnp.float32)] * 2
    rows = jnp.concatenate(terms, axis=0).astype(jnp.bfloat16)
    copies = []
    for columns in halves(wide):
        size = columns.stop - columns.start
        total = jnp.dot(weight_ref[...], rows[:, columns], preferred_element_type=jnp.float32)
        for s in range(SEGMENTS):
            part = pl.ds(s * wide + columns.start, size)
            out_ref[:, part] = total[s * count : (s + 1) * count].astype(jnp.bfloat16)
            copies.append(
                pltpu.make_async_copy(
                    out_ref.at[:, part], out_hbm.at[:, part], sem.at[len(copies)]
                )
            )
            copies[-1].start()
    wait_all(copies)


def blend(weights, own_blocks, other_blocks, count):
    chips = len(own_blocks)
    features = own_blocks[0].shape[1] * SEGMENTS
    return pl.pallas_call(
        functools.partial(blend_kernel, chips),
        out_shape=jax.ShapeDtypeStruct((count, features), jnp.bfloat16),
        in_specs=[VMEM] * (1 + chips + len(other_blocks)),
        out_specs=HBM,
        scratch_shapes=[
            pltpu.VMEM((count, features), jnp.bfloat16),
            pltpu.SemaphoreType.DMA((2 * SEGMENTS,)),
        ],
        compiler_params=params(16),
        name="blend",
    )(weights, *own_blocks, *other_blocks)


def body(tokens, expert_ids, route_logits, w_gate, w_up, w_down):
    devices = lax.axis_size("expert")
    teams = devices // SPLIT
    chips = SPLIT // CORES
    other_core = [(i, i ^ 1) for i in range(devices)]
    other_chip = [[(i, i ^ (m * CORES)) for i in range(devices)] for m in range(chips)]
    packed, table = pack_rows(expert_ids.T, route_logits.T, tokens, teams)
    def gather(block):
        return [block] + [lax.ppermute(block, "expert", other_chip[m]) for m in range(1, chips)]

    own = gather(packed[0])
    crowds = []
    for k in range(1, teams):
        pairs = [(i, (i + k * SPLIT) % devices) for i in range(devices)]
        block = lax.ppermute(packed[k], "expert", pairs)
        if k == teams - 1:
            block, table = lax.optimization_barrier((block, table))
            weights = blend_weights(table, teams)
        crowds.append(gather(block))
    own, crowds, weights = lax.optimization_barrier((own, crowds, weights))
    own = join(own)
    first = unpack(own, lax.ppermute(own, "expert", other_core))
    pieces = []
    for crowd in crowds:
        crowd = join(crowd)
        pieces += [crowd, lax.ppermute(crowd, "expert", other_core)]
    *given, hidden = expert_half(first, pieces, w_gate, w_up, w_down)
    taken = [lax.ppermute(piece, "expert", other_core) for piece in given]
    kept = kept_half(hidden, w_down)
    others = []
    for k in range(1, teams):
        parts = add_cores(kept, taken[k], k, chips)
        parts, later = lax.optimization_barrier((parts, kept))
        team = [parts[0]]
        for m in reversed(range(1, chips)):
            team.append(lax.ppermute(parts[m], "expert", other_chip[m]))
        pairs = [(i, (i - k * SPLIT) % devices) for i in range(devices)]
        others.append(lax.ppermute(sum_blocks(team), "expert", pairs))
    parts = add_cores(later, taken[0], 0, chips)
    own = [parts[0]]
    for m in reversed(range(1, chips)):
        own.append(lax.ppermute(parts[m], "expert", other_chip[m]))
    return blend(weights, own, others, tokens.shape[0])


def solution(mesh):
    placed = (
        P(("groups", "expert"), None),
        P(("groups", "expert"), None),
        P(("groups", "expert"), None),
        P(None, "expert"),
        P(None, "expert"),
        P("expert", None),
    )
    return jax.shard_map(
        body, mesh=mesh, in_specs=placed, out_specs=P(("groups", "expert"), None), check_vma=False
    )
```

```python
import functools

import jax
import jax.numpy as jnp
from jax import lax
from jax.experimental import pallas as pl
from jax.experimental.pallas import tpu as pltpu
from jax.sharding import PartitionSpec as P

SPLIT = 8
CAP = 5
CORES = 2
SEGMENTS = 8

route_scale = 2.5

VMEM = pl.BlockSpec(memory_space=pltpu.VMEM)
HBM = pl.BlockSpec(memory_space=pltpu.HBM)
MIB = 1024 * 1024


def hits(ids, mine, teams):
    count = ids.shape[1]
    row = lax.broadcasted_iota(jnp.int32, (8 * pl.cdiv(teams, 8), count), 0)
    wanted = lax.rem(mine + row, teams)
    hit = jnp.zeros(row.shape, jnp.int32)
    for j in range(ids.shape[0]):
        hit = hit + jnp.where(ids[j : j + 1, :] == wanted, 1, 0)
    hit = jnp.where(row < teams, hit, 0).astype(jnp.float32)
    before = lax.broadcasted_iota(jnp.int32, (count, count), 0)
    after = lax.broadcasted_iota(jnp.int32, (count, count), 1)
    earlier = jnp.where(before < after, 1.0, 0.0).astype(jnp.bfloat16)
    slot = jnp.dot(hit.astype(jnp.bfloat16), earlier, preferred_element_type=jnp.float32)
    return hit, jnp.where(hit > 0, slot, -1.0)


def fifth(shape, axis):
    at = lax.broadcasted_iota(jnp.int32, shape, axis)
    segment = jnp.zeros(shape, jnp.int32)
    for s in range(1, SEGMENTS):
        segment = segment + jnp.where(at >= s * CAP, 1, 0)
    return segment, (at - CAP * segment).astype(jnp.float32)


def params(mib):
    return pltpu.CompilerParams(vmem_limit_bytes=int(mib * MIB))


def bring(source, target, semaphores, parts):
    step = source.shape[0] // parts
    copies = []
    for i in range(parts):
        rows = pl.ds(i * step, step)
        copies.append(pltpu.make_async_copy(source.at[rows], target.at[rows], semaphores.at[i]))
        copies[-1].start()
    return copies


def wait_all(copies):
    for copy in copies:
        copy.wait()


def pack_kernel(teams, ids_hbm, logits_hbm, tokens_hbm, *refs):
    *out_refs, table_ref, ids_ref, logits_ref, tokens_ref, ids_sem, logits_sem, tokens_sem = refs
    ids_copy = bring(ids_hbm, ids_ref, ids_sem, 1)
    tokens_copy = bring(tokens_hbm, tokens_ref, tokens_sem, 4)
    logits_copy = bring(logits_hbm, logits_ref, logits_sem, 1)
    wait_all(ids_copy)
    mine = lax.axis_index("expert") // SPLIT
    ids = ids_ref[...]
    hit, slot = hits(ids, mine, teams)
    wait_all(logits_copy)
    lifted = jax.nn.sigmoid(logits_ref[...])
    gates = route_scale * lifted / jnp.sum(lifted, axis=0, keepdims=True)
    row = lax.broadcasted_iota(jnp.int32, hit.shape, 0)
    wanted = lax.rem(mine + row, teams)
    gate = jnp.zeros(hit.shape, jnp.float32)
    for j in range(ids.shape[0]):
        gate = gate + jnp.where(ids[j : j + 1, :] == wanted, gates[j : j + 1, :], 0.0)
    table_ref[: hit.shape[0], :] = slot
    table_ref[hit.shape[0] :, :] = gate
    count, features = tokens_ref.shape
    wide = features // SEGMENTS
    tall = CAP * SEGMENTS
    segment, place = fifth((tall, 1), 0)
    column = lax.broadcasted_iota(jnp.int32, (1, SEGMENTS * count), 1)
    same = segment == column // count
    picks = []
    for k in range(teams):
        slots = jnp.concatenate([slot[k : k + 1, :]] * SEGMENTS, axis=1)
        picks.append(jnp.where(same & (slots == place), 1.0, 0.0))
    wait_all(tokens_copy)
    stacked = jnp.concatenate(
        [tokens_ref[:, s * wide : (s + 1) * wide] for s in range(SEGMENTS)], axis=0
    )
    packed = jnp.dot(
        jnp.concatenate(picks, axis=0).astype(jnp.bfloat16),
        stacked,
        preferred_element_type=jnp.float32,
    )
    for k in range(teams):
        out_refs[k][...] = packed[k * tall : (k + 1) * tall].astype(jnp.bfloat16)


def pack_rows(ids, logits, tokens, teams):
    wide = tokens.shape[1] // SEGMENTS
    block = jax.ShapeDtypeStruct((CAP * SEGMENTS, wide), jnp.bfloat16)
    table = jax.ShapeDtypeStruct((16 * pl.cdiv(teams, 8), ids.shape[1]), jnp.float32)
    *packed, table = pl.pallas_call(
        functools.partial(pack_kernel, teams),
        out_shape=[block] * teams + [table],
        in_specs=[HBM] * 3,
        out_specs=[VMEM] * (teams + 1),
        scratch_shapes=[
            pltpu.VMEM(ids.shape, ids.dtype),
            pltpu.VMEM(logits.shape, logits.dtype),
            pltpu.VMEM(tokens.shape, tokens.dtype),
            pltpu.SemaphoreType.DMA((1,)),
            pltpu.SemaphoreType.DMA((1,)),
            pltpu.SemaphoreType.DMA((4,)),
        ],
        name="pack_rows",
    )(ids, logits, tokens)
    return packed, table


def weight_kernel(teams, table_ref, out_ref):
    rows, count = table_ref.shape
    slot = jnp.transpose(table_ref[: rows // 2, :])
    gate = jnp.transpose(table_ref[rows // 2 :, :])
    tall = CAP * SEGMENTS
    depth = out_ref.shape[1]
    column = lax.broadcasted_iota(jnp.int32, (1, depth), 1)
    part = jnp.zeros((1, depth), jnp.int32)
    for g in range(1, depth // tall):
        part = part + jnp.where(column >= g * tall, 1, 0)
    column = column - tall * part
    segment = jnp.zeros((1, depth), jnp.int32)
    for s in range(1, SEGMENTS):
        segment = segment + jnp.where(column >= s * CAP, 1, 0)
    place = (column - CAP * segment).astype(jnp.float32)
    team = jnp.where(part < 3, 0, (part - 1) >> 1)
    low = jnp.where(part < 3, part >> 1, (part - 3) & 1) == 1
    for s in range(SEGMENTS):
        full = jnp.zeros((count, depth), jnp.float32)
        for k in range(teams):
            chosen = (team == k) & (segment == s) & (slot[:, k : k + 1] == place)
            full = full + jnp.where(chosen, gate[:, k : k + 1], 0.0)
        high = full.astype(jnp.bfloat16).astype(jnp.float32)
        out_ref[s * count : (s + 1) * count, :] = jnp.where(low, full - high, high).astype(
            jnp.bfloat16
        )


def blend_weights(table, teams):
    shape = (SEGMENTS * table.shape[1], CAP * SEGMENTS * (1 + 2 * teams))
    return pl.pallas_call(
        functools.partial(weight_kernel, teams),
        out_shape=jax.ShapeDtypeStruct(shape, jnp.bfloat16),
        in_specs=[VMEM],
        out_specs=VMEM,
        compiler_params=params(4 + teams),
        cost_estimate=pl.CostEstimate(flops=6 * 10**9, bytes_accessed=8 * MIB, transcendentals=0),
        name="blend_weights",
    )(table)


def join_kernel(*refs):
    tall = refs[0].shape[0]
    for i, ref in enumerate(refs[:-1]):
        refs[-1][i * tall : (i + 1) * tall, :] = ref[...]


def join(blocks):
    tall, wide = blocks[0].shape
    return pl.pallas_call(
        join_kernel,
        out_shape=jax.ShapeDtypeStruct((tall * len(blocks), wide), blocks[0].dtype),
        in_specs=[VMEM] * len(blocks),
        out_specs=VMEM,
        compiler_params=params(4),
        name="join",
    )(*blocks)


def packed_down(hidden, down_ref, out_ref, flat):
    count, wide = flat.shape[1:]
    tall = CAP * SEGMENTS
    for s in range(SEGMENTS):
        slot = flat.at[s % 2]
        slot[...] = jnp.dot(
            hidden, down_ref[:, s * wide : (s + 1) * wide], preferred_element_type=jnp.float32
        )
        for b in range(count // CAP):
            start = b * tall + s * CAP
            out_ref[start : start + CAP, :] = slot[b * CAP : (b + 1) * CAP, :]


def unpack_kernel(own_ref, other_ref, out_ref, packed):
    tall = CAP * SEGMENTS
    half = own_ref.shape[0]
    wide = own_ref.shape[1]
    packed[:half, :] = own_ref[...].astype(jnp.float32)
    packed[half:, :] = other_ref[...].astype(jnp.float32)
    for s in range(SEGMENTS):
        for b in range(2 * half // tall):
            start = b * tall + s * CAP
            out_ref[b * CAP : (b + 1) * CAP, s * wide : (s + 1) * wide] = packed[
                start : start + CAP, :
            ]


def unpack(own, other):
    rows, wide = own.shape
    return pl.pallas_call(
        unpack_kernel,
        out_shape=jax.ShapeDtypeStruct((2 * rows // SEGMENTS, wide * SEGMENTS), jnp.float32),
        in_specs=[VMEM] * 2,
        out_specs=VMEM,
        scratch_shapes=[pltpu.VMEM((2 * rows, wide), jnp.float32)],
        compiler_params=params(6),
        name="unpack",
    )(own, other)


def expert_kernel(teams, first_ref, *refs):
    pieces = refs[: 2 * (teams - 1)]
    gate_ref, up_ref, down_ref = refs[2 * (teams - 1) : 2 * teams + 1]
    *given_refs, hidden_ref, packed, flat, out, act = refs[2 * teams + 1 :]
    tall = CAP * SEGMENTS
    wide = packed.shape[1]
    units = gate_ref.shape[1]
    start = 0
    for ref in pieces:
        packed[start : start + ref.shape[0], :] = ref[...].astype(jnp.float32)
        start += ref.shape[0]
    known = first_ref.shape[0]
    count = known * teams
    gate_act = jnp.zeros((count, units), jnp.float32)
    up_act = jnp.zeros((count, units), jnp.float32)
    for s in range(SEGMENTS):
        slot = flat.at[s % 2]
        columns = slice(s * wide, (s + 1) * wide)
        slot[:known, :] = first_ref[:, columns]
        for b in range((count - known) // CAP):
            start = b * tall + s * CAP
            slot[known + b * CAP : known + (b + 1) * CAP, :] = packed[start : start + CAP, :]
        rows = slot[...].astype(jnp.bfloat16)
        gate_act += jnp.dot(rows, gate_ref[columns, :], preferred_element_type=jnp.float32)
        up_act += jnp.dot(rows, up_ref[columns, :], preferred_element_type=jnp.float32)
    act[:count, :] = jax.nn.silu(gate_act) * up_act
    half = known // 2
    for k in range(teams):
        for core in range(CORES):
            source = (CORES * k + core) * half
            target = count + (core * teams + k) * half
            act[target : target + half, :] = act[source : source + half, :]
    hidden = act[count:, :].astype(jnp.bfloat16)
    half = count // 2
    hidden_ref[...] = hidden[:half]
    packed_down(hidden[half:], down_ref, out, flat.at[:, :half, :])
    for k, given_ref in enumerate(given_refs):
        rows = given_ref.shape[0]
        given_ref[...] = out[k * rows : (k + 1) * rows, :].astype(jnp.bfloat16)


def expert_half(first, pieces, w_gate, w_up, w_down):
    teams = 1 + len(pieces) // 2
    block, wide = pieces[0].shape
    features, units = w_gate.shape
    rows = first.shape[0] * teams
    return pl.pallas_call(
        functools.partial(expert_kernel, teams),
        out_shape=[jax.ShapeDtypeStruct((block, wide), jnp.bfloat16)] * teams
        + [jax.ShapeDtypeStruct((rows // 2, units), jnp.bfloat16)],
        in_specs=[VMEM] * (len(pieces) + 4),
        out_specs=[VMEM] * (teams + 1),
        scratch_shapes=[
            pltpu.VMEM((block * len(pieces), wide), jnp.float32),
            pltpu.VMEM((2, rows, wide), jnp.float32),
            pltpu.VMEM((block * teams, wide), jnp.float32),
            pltpu.VMEM((2 * rows, units), jnp.float32),
        ],
        compiler_params=params(16 + 4 * teams),
        cost_estimate=pl.CostEstimate(
            flops=5 * rows * units * features,
            bytes_accessed=6 * features * units,
            transcendentals=rows * units,
        ),
        name="expert_half",
    )(first, *pieces, w_gate, w_up, w_down)


def kept_kernel(hidden_ref, down_ref, kept_ref, flat):
    packed_down(hidden_ref[...], down_ref, kept_ref, flat)


def kept_half(hidden, w_down):
    count, units = hidden.shape
    features = w_down.shape[1]
    wide = features // SEGMENTS
    return pl.pallas_call(
        kept_kernel,
        out_shape=jax.ShapeDtypeStruct((count * SEGMENTS, wide), jnp.float32),
        in_specs=[VMEM] * 2,
        out_specs=VMEM,
        scratch_shapes=[pltpu.VMEM((2, count, wide), jnp.float32)],
        compiler_params=params(8 + count // 10),
        cost_estimate=pl.CostEstimate(
            flops=2 * count * units * features,
            bytes_accessed=2 * features * units,
            transcendentals=0,
        ),
        name="kept_half",
    )(hidden, w_down)


def add_kernel(first, kept_ref, taken_ref, *out_refs):
    tall = out_refs[0].shape[0]
    for b, out_ref in enumerate(out_refs):
        rows = slice(b * tall, (b + 1) * tall)
        total = kept_ref[first + b * tall : first + (b + 1) * tall, :] + taken_ref[
            rows, :
        ].astype(jnp.float32)
        out_ref[...] = total.astype(out_ref.dtype)


def add_cores(kept, taken, k, chips):
    shape = (CAP * SEGMENTS, kept.shape[1])
    outs = [jax.ShapeDtypeStruct(shape, jnp.bfloat16 if m else jnp.float32) for m in range(chips)]
    return pl.pallas_call(
        functools.partial(add_kernel, k * taken.shape[0]),
        out_shape=outs,
        in_specs=[VMEM] * 2,
        out_specs=[VMEM] * len(outs),
        compiler_params=params(6),
        name="add_cores",
    )(kept, taken)


def sum_kernel(*refs):
    total = refs[0][...]
    for ref in refs[1:-1]:
        total = total + ref[...].astype(jnp.float32)
    refs[-1][...] = total.astype(refs[-1].dtype)


def sum_blocks(blocks):
    return pl.pallas_call(
        sum_kernel,
        out_shape=jax.ShapeDtypeStruct(blocks[0].shape, jnp.bfloat16),
        in_specs=[VMEM] * len(blocks),
        out_specs=VMEM,
        compiler_params=params(4),
        name="sum_blocks",
    )(*blocks)


def halves(wide):
    cut = 128 * pl.cdiv(wide // 128, 2)
    return slice(0, cut), slice(cut, wide)


def blend_kernel(chips, weight_ref, *refs):
    *refs, out_hbm, out_ref, sem = refs
    count, features = out_ref.shape
    wide = features // SEGMENTS
    own = refs[0][...]
    for ref in refs[1:chips]:
        own = own + ref[...].astype(jnp.float32)
    high = own.astype(jnp.bfloat16).astype(jnp.float32)
    terms = [high, own - high, high]
    for ref in refs[chips:]:
        terms += [ref[...].astype(jnp.float32)] * 2
    rows = jnp.concatenate(terms, axis=0).astype(jnp.bfloat16)
    copies = []
    for columns in halves(wide):
        size = columns.stop - columns.start
        total = jnp.dot(weight_ref[...], rows[:, columns], preferred_element_type=jnp.float32)
        for s in range(SEGMENTS):
            part = pl.ds(s * wide + columns.start, size)
            out_ref[:, part] = total[s * count : (s + 1) * count].astype(jnp.bfloat16)
            copies.append(
                pltpu.make_async_copy(
                    out_ref.at[:, part], out_hbm.at[:, part], sem.at[len(copies)]
                )
            )
            copies[-1].start()
    wait_all(copies)


def blend(weights, own_blocks, other_blocks, count):
    chips = len(own_blocks)
    features = own_blocks[0].shape[1] * SEGMENTS
    return pl.pallas_call(
        functools.partial(blend_kernel, chips),
        out_shape=jax.ShapeDtypeStruct((count, features), jnp.bfloat16),
        in_specs=[VMEM] * (1 + chips + len(other_blocks)),
        out_specs=HBM,
        scratch_shapes=[
            pltpu.VMEM((count, features), jnp.bfloat16),
            pltpu.SemaphoreType.DMA((2 * SEGMENTS,)),
        ],
        compiler_params=params(16),
        name="blend",
    )(weights, *own_blocks, *other_blocks)


def body(tokens, expert_ids, route_logits, w_gate, w_up, w_down):
    devices = lax.axis_size("expert")
    teams = devices // SPLIT
    chips = SPLIT // CORES
    other_core = [(i, i ^ 1) for i in range(devices)]
    other_chip = [[(i, i ^ (m * CORES)) for i in range(devices)] for m in range(chips)]
    packed, table = pack_rows(expert_ids.T, route_logits.T, tokens, teams)
    def gather(block):
        return [block] + [lax.ppermute(block, "expert", other_chip[m]) for m in range(1, chips)]

    own = [packed[0]] + [lax.ppermute(packed[0], "expert", other_chip[m]) for m in range(2, chips)]
    crowds = []
    for k in range(1, teams):
        pairs = [(i, (i + k * SPLIT) % devices) for i in range(devices)]
        block = lax.ppermute(packed[k], "expert", pairs)
        if k == teams - 1:
            block, table, last = lax.optimization_barrier((block, table, packed[0]))
            weights = blend_weights(table, teams)
        crowds.append(gather(block))
    own.insert(1, lax.ppermute(last, "expert", other_chip[1]))
    own, crowds, weights = lax.optimization_barrier((own, crowds, weights))
    own = join(own)
    first = unpack(own, lax.ppermute(own, "expert", other_core))
    pieces = []
    for crowd in crowds:
        crowd = join(crowd)
        pieces += [crowd, lax.ppermute(crowd, "expert", other_core)]
    *given, hidden = expert_half(first, pieces, w_gate, w_up, w_down)
    taken = [lax.ppermute(piece, "expert", other_core) for piece in given]
    kept = kept_half(hidden, w_down)
    others = []
    for k in range(1, teams):
        parts = add_cores(kept, taken[k], k, chips)
        parts, later = lax.optimization_barrier((parts, kept))
        team = [parts[0]]
        for m in reversed(range(1, chips)):
            team.append(lax.ppermute(parts[m], "expert", other_chip[m]))
        pairs = [(i, (i - k * SPLIT) % devices) for i in range(devices)]
        others.append(lax.ppermute(sum_blocks(team), "expert", pairs))
    parts = add_cores(later, taken[0], 0, chips)
    own = [parts[0]]
    for m in reversed(range(1, chips)):
        own.append(lax.ppermute(parts[m], "expert", other_chip[m]))
    return blend(weights, own, others, tokens.shape[0])


def solution(mesh):
    placed = (
        P(("groups", "expert"), None),
        P(("groups", "expert"), None),
        P(("groups", "expert"), None),
        P(None, "expert"),
        P(None, "expert"),
        P("expert", None),
    )
    return jax.shard_map(
        body, mesh=mesh, in_specs=placed, out_specs=P(("groups", "expert"), None), check_vma=False
    )
```

```python
import functools

import jax
import jax.numpy as jnp
from jax import lax
from jax.experimental import pallas as pl
from jax.experimental.pallas import tpu as pltpu
from jax.sharding import PartitionSpec as P

SPLIT = 8
CAP = 5
CORES = 2
SEGMENTS = 8

route_scale = 2.5

VMEM = pl.BlockSpec(memory_space=pltpu.VMEM)
HBM = pl.BlockSpec(memory_space=pltpu.HBM)
MIB = 1024 * 1024


def hits(ids, mine, teams):
    count = ids.shape[1]
    row = lax.broadcasted_iota(jnp.int32, (8 * pl.cdiv(teams, 8), count), 0)
    wanted = lax.rem(mine + row, teams)
    hit = jnp.zeros(row.shape, jnp.int32)
    for j in range(ids.shape[0]):
        hit = hit + jnp.where(ids[j : j + 1, :] == wanted, 1, 0)
    hit = jnp.where(row < teams, hit, 0).astype(jnp.float32)
    before = lax.broadcasted_iota(jnp.int32, (count, count), 0)
    after = lax.broadcasted_iota(jnp.int32, (count, count), 1)
    earlier = jnp.where(before < after, 1.0, 0.0).astype(jnp.bfloat16)
    slot = jnp.dot(hit.astype(jnp.bfloat16), earlier, preferred_element_type=jnp.float32)
    return hit, jnp.where(hit > 0, slot, -1.0)


def fifth(shape, axis):
    at = lax.broadcasted_iota(jnp.int32, shape, axis)
    segment = jnp.zeros(shape, jnp.int32)
    for s in range(1, SEGMENTS):
        segment = segment + jnp.where(at >= s * CAP, 1, 0)
    return segment, (at - CAP * segment).astype(jnp.float32)


def params(mib):
    return pltpu.CompilerParams(vmem_limit_bytes=int(mib * MIB))


def bring(source, target, semaphores, parts):
    step = source.shape[0] // parts
    copies = []
    for i in range(parts):
        rows = pl.ds(i * step, step)
        copies.append(pltpu.make_async_copy(source.at[rows], target.at[rows], semaphores.at[i]))
        copies[-1].start()
    return copies


def wait_all(copies):
    for copy in copies:
        copy.wait()


def pack_kernel(teams, ids_hbm, logits_hbm, tokens_hbm, *refs):
    *out_refs, table_ref, ids_ref, logits_ref, tokens_ref, ids_sem, logits_sem, tokens_sem = refs
    ids_copy = bring(ids_hbm, ids_ref, ids_sem, 1)
    tokens_copy = bring(tokens_hbm, tokens_ref, tokens_sem, 4)
    logits_copy = bring(logits_hbm, logits_ref, logits_sem, 1)
    wait_all(ids_copy)
    mine = lax.axis_index("expert") // SPLIT
    ids = ids_ref[...]
    hit, slot = hits(ids, mine, teams)
    wait_all(logits_copy)
    lifted = jax.nn.sigmoid(logits_ref[...])
    gates = route_scale * lifted / jnp.sum(lifted, axis=0, keepdims=True)
    row = lax.broadcasted_iota(jnp.int32, hit.shape, 0)
    wanted = lax.rem(mine + row, teams)
    gate = jnp.zeros(hit.shape, jnp.float32)
    for j in range(ids.shape[0]):
        gate = gate + jnp.where(ids[j : j + 1, :] == wanted, gates[j : j + 1, :], 0.0)
    table_ref[: hit.shape[0], :] = slot
    table_ref[hit.shape[0] :, :] = gate
    count, features = tokens_ref.shape
    wide = features // SEGMENTS
    tall = CAP * SEGMENTS
    segment, place = fifth((tall, 1), 0)
    column = lax.broadcasted_iota(jnp.int32, (1, SEGMENTS * count), 1)
    same = segment == column // count
    picks = []
    for k in range(teams):
        slots = jnp.concatenate([slot[k : k + 1, :]] * SEGMENTS, axis=1)
        picks.append(jnp.where(same & (slots == place), 1.0, 0.0))
    wait_all(tokens_copy)
    stacked = jnp.concatenate(
        [tokens_ref[:, s * wide : (s + 1) * wide] for s in range(SEGMENTS)], axis=0
    )
    packed = jnp.dot(
        jnp.concatenate(picks, axis=0).astype(jnp.bfloat16),
        stacked,
        preferred_element_type=jnp.float32,
    )
    for k in range(teams):
        out_refs[k][...] = packed[k * tall : (k + 1) * tall].astype(jnp.bfloat16)


def pack_rows(ids, logits, tokens, teams):
    wide = tokens.shape[1] // SEGMENTS
    block = jax.ShapeDtypeStruct((CAP * SEGMENTS, wide), jnp.bfloat16)
    table = jax.ShapeDtypeStruct((16 * pl.cdiv(teams, 8), ids.shape[1]), jnp.float32)
    *packed, table = pl.pallas_call(
        functools.partial(pack_kernel, teams),
        out_shape=[block] * teams + [table],
        in_specs=[HBM] * 3,
        out_specs=[VMEM] * (teams + 1),
        scratch_shapes=[
            pltpu.VMEM(ids.shape, ids.dtype),
            pltpu.VMEM(logits.shape, logits.dtype),
            pltpu.VMEM(tokens.shape, tokens.dtype),
            pltpu.SemaphoreType.DMA((1,)),
            pltpu.SemaphoreType.DMA((1,)),
            pltpu.SemaphoreType.DMA((4,)),
        ],
        name="pack_rows",
    )(ids, logits, tokens)
    return packed, table


def weight_kernel(teams, table_ref, out_ref):
    rows, count = table_ref.shape
    slot = jnp.transpose(table_ref[: rows // 2, :])
    gate = jnp.transpose(table_ref[rows // 2 :, :])
    tall = CAP * SEGMENTS
    depth = out_ref.shape[1]
    column = lax.broadcasted_iota(jnp.int32, (1, depth), 1)
    part = jnp.zeros((1, depth), jnp.int32)
    for g in range(1, depth // tall):
        part = part + jnp.where(column >= g * tall, 1, 0)
    column = column - tall * part
    segment = jnp.zeros((1, depth), jnp.int32)
    for s in range(1, SEGMENTS):
        segment = segment + jnp.where(column >= s * CAP, 1, 0)
    place = (column - CAP * segment).astype(jnp.float32)
    team = jnp.where(part < 3, 0, (part - 1) >> 1)
    low = jnp.where(part < 3, part >> 1, (part - 3) & 1) == 1
    for s in range(SEGMENTS):
        full = jnp.zeros((count, depth), jnp.float32)
        for k in range(teams):
            chosen = (team == k) & (segment == s) & (slot[:, k : k + 1] == place)
            full = full + jnp.where(chosen, gate[:, k : k + 1], 0.0)
        high = full.astype(jnp.bfloat16).astype(jnp.float32)
        out_ref[s * count : (s + 1) * count, :] = jnp.where(low, full - high, high).astype(
            jnp.bfloat16
        )


def blend_weights(table, teams):
    shape = (SEGMENTS * table.shape[1], CAP * SEGMENTS * (1 + 2 * teams))
    return pl.pallas_call(
        functools.partial(weight_kernel, teams),
        out_shape=jax.ShapeDtypeStruct(shape, jnp.bfloat16),
        in_specs=[VMEM],
        out_specs=VMEM,
        compiler_params=params(4 + teams),
        cost_estimate=pl.CostEstimate(flops=6 * 10**9, bytes_accessed=8 * MIB, transcendentals=0),
        name="blend_weights",
    )(table)


def join_kernel(*refs):
    tall = refs[0].shape[0]
    for i, ref in enumerate(refs[:-1]):
        refs[-1][i * tall : (i + 1) * tall, :] = ref[...]


def join(blocks):
    tall, wide = blocks[0].shape
    return pl.pallas_call(
        join_kernel,
        out_shape=jax.ShapeDtypeStruct((tall * len(blocks), wide), blocks[0].dtype),
        in_specs=[VMEM] * len(blocks),
        out_specs=VMEM,
        compiler_params=params(4),
        name="join",
    )(*blocks)


def packed_down(hidden, down_ref, out_ref, flat):
    count, wide = flat.shape[1:]
    tall = CAP * SEGMENTS
    for s in range(SEGMENTS):
        slot = flat.at[s % 2]
        slot[...] = jnp.dot(
            hidden, down_ref[:, s * wide : (s + 1) * wide], preferred_element_type=jnp.float32
        )
        for b in range(count // CAP):
            start = b * tall + s * CAP
            out_ref[start : start + CAP, :] = slot[b * CAP : (b + 1) * CAP, :]


def unpack_kernel(own_ref, other_ref, out_ref, packed):
    tall = CAP * SEGMENTS
    half = own_ref.shape[0]
    wide = own_ref.shape[1]
    packed[:half, :] = own_ref[...].astype(jnp.float32)
    packed[half:, :] = other_ref[...].astype(jnp.float32)
    for s in range(SEGMENTS):
        for b in range(2 * half // tall):
            start = b * tall + s * CAP
            out_ref[b * CAP : (b + 1) * CAP, s * wide : (s + 1) * wide] = packed[
                start : start + CAP, :
            ]


def unpack(own, other):
    rows, wide = own.shape
    return pl.pallas_call(
        unpack_kernel,
        out_shape=jax.ShapeDtypeStruct((2 * rows // SEGMENTS, wide * SEGMENTS), jnp.float32),
        in_specs=[VMEM] * 2,
        out_specs=VMEM,
        scratch_shapes=[pltpu.VMEM((2 * rows, wide), jnp.float32)],
        compiler_params=params(6),
        name="unpack",
    )(own, other)


def expert_kernel(teams, first_ref, *refs):
    pieces = refs[: 2 * (teams - 1)]
    gate_ref, up_ref, down_ref = refs[2 * (teams - 1) : 2 * teams + 1]
    *given_refs, hidden_ref, packed, flat, out, act = refs[2 * teams + 1 :]
    tall = CAP * SEGMENTS
    wide = packed.shape[1]
    units = gate_ref.shape[1]
    start = 0
    for ref in pieces:
        packed[start : start + ref.shape[0], :] = ref[...].astype(jnp.float32)
        start += ref.shape[0]
    known = first_ref.shape[0]
    count = known * teams
    gate_act = jnp.zeros((count, units), jnp.float32)
    up_act = jnp.zeros((count, units), jnp.float32)
    for s in range(SEGMENTS):
        slot = flat.at[s % 2]
        columns = slice(s * wide, (s + 1) * wide)
        slot[:known, :] = first_ref[:, columns]
        for b in range((count - known) // CAP):
            start = b * tall + s * CAP
            slot[known + b * CAP : known + (b + 1) * CAP, :] = packed[start : start + CAP, :]
        rows = slot[...].astype(jnp.bfloat16)
        gate_act += jnp.dot(rows, gate_ref[columns, :], preferred_element_type=jnp.float32)
        up_act += jnp.dot(rows, up_ref[columns, :], preferred_element_type=jnp.float32)
    act[:count, :] = jax.nn.silu(gate_act) * up_act
    half = known // 2
    for k in range(teams):
        for core in range(CORES):
            source = (CORES * k + core) * half
            target = count + (core * teams + k) * half
            act[target : target + half, :] = act[source : source + half, :]
    hidden = act[count:, :].astype(jnp.bfloat16)
    half = count // 2
    hidden_ref[...] = hidden[:half]
    packed_down(hidden[half:], down_ref, out, flat.at[:, :half, :])
    for k, given_ref in enumerate(given_refs):
        rows = given_ref.shape[0]
        given_ref[...] = out[k * rows : (k + 1) * rows, :].astype(jnp.bfloat16)


def expert_half(first, pieces, w_gate, w_up, w_down):
    teams = 1 + len(pieces) // 2
    block, wide = pieces[0].shape
    features, units = w_gate.shape
    rows = first.shape[0] * teams
    return pl.pallas_call(
        functools.partial(expert_kernel, teams),
        out_shape=[jax.ShapeDtypeStruct((block, wide), jnp.bfloat16)] * teams
        + [jax.ShapeDtypeStruct((rows // 2, units), jnp.bfloat16)],
        in_specs=[VMEM] * (len(pieces) + 4),
        out_specs=[VMEM] * (teams + 1),
        scratch_shapes=[
            pltpu.VMEM((block * len(pieces), wide), jnp.float32),
            pltpu.VMEM((2, rows, wide), jnp.float32),
            pltpu.VMEM((block * teams, wide), jnp.float32),
            pltpu.VMEM((2 * rows, units), jnp.float32),
        ],
        compiler_params=params(16 + 4 * teams),
        cost_estimate=pl.CostEstimate(
            flops=5 * rows * units * features,
            bytes_accessed=6 * features * units,
            transcendentals=rows * units,
        ),
        name="expert_half",
    )(first, *pieces, w_gate, w_up, w_down)


def kept_kernel(hidden_ref, down_ref, kept_ref, flat):
    packed_down(hidden_ref[...], down_ref, kept_ref, flat)


def kept_half(hidden, w_down):
    count, units = hidden.shape
    features = w_down.shape[1]
    wide = features // SEGMENTS
    return pl.pallas_call(
        kept_kernel,
        out_shape=jax.ShapeDtypeStruct((count * SEGMENTS, wide), jnp.float32),
        in_specs=[VMEM] * 2,
        out_specs=VMEM,
        scratch_shapes=[pltpu.VMEM((2, count, wide), jnp.float32)],
        compiler_params=params(8 + count // 10),
        cost_estimate=pl.CostEstimate(
            flops=2 * count * units * features,
            bytes_accessed=2 * features * units,
            transcendentals=0,
        ),
        name="kept_half",
    )(hidden, w_down)


def add_kernel(first, kept_ref, taken_ref, *out_refs):
    tall = out_refs[0].shape[0]
    for b, out_ref in enumerate(out_refs):
        rows = slice(b * tall, (b + 1) * tall)
        total = kept_ref[first + b * tall : first + (b + 1) * tall, :] + taken_ref[
            rows, :
        ].astype(jnp.float32)
        out_ref[...] = total.astype(out_ref.dtype)


def add_cores(kept, taken, k, chips):
    shape = (CAP * SEGMENTS, kept.shape[1])
    outs = [jax.ShapeDtypeStruct(shape, jnp.bfloat16 if m else jnp.float32) for m in range(chips)]
    return pl.pallas_call(
        functools.partial(add_kernel, k * taken.shape[0]),
        out_shape=outs,
        in_specs=[VMEM] * 2,
        out_specs=[VMEM] * len(outs),
        compiler_params=params(6),
        name="add_cores",
    )(kept, taken)


def sum_kernel(*refs):
    total = refs[0][...]
    for ref in refs[1:-1]:
        total = total + ref[...].astype(jnp.float32)
    refs[-1][...] = total.astype(refs[-1].dtype)


def sum_blocks(blocks):
    return pl.pallas_call(
        sum_kernel,
        out_shape=jax.ShapeDtypeStruct(blocks[0].shape, jnp.bfloat16),
        in_specs=[VMEM] * len(blocks),
        out_specs=VMEM,
        compiler_params=params(4),
        name="sum_blocks",
    )(*blocks)


def halves(wide):
    cut = 128 * pl.cdiv(wide // 128, 2)
    return slice(0, cut), slice(cut, wide)


def blend_kernel(chips, weight_ref, *refs):
    *refs, out_hbm, out_ref, sem = refs
    count, features = out_ref.shape
    wide = features // SEGMENTS
    own = refs[0][...]
    for ref in refs[1:chips]:
        own = own + ref[...].astype(jnp.float32)
    high = own.astype(jnp.bfloat16).astype(jnp.float32)
    terms = [high, own - high, high]
    for ref in refs[chips:]:
        terms += [ref[...].astype(jnp.float32)] * 2
    rows = jnp.concatenate(terms, axis=0).astype(jnp.bfloat16)
    copies = []
    for columns in halves(wide):
        size = columns.stop - columns.start
        total = jnp.dot(weight_ref[...], rows[:, columns], preferred_element_type=jnp.float32)
        for s in range(SEGMENTS):
            part = pl.ds(s * wide + columns.start, size)
            out_ref[:, part] = total[s * count : (s + 1) * count].astype(jnp.bfloat16)
            copies.append(
                pltpu.make_async_copy(
                    out_ref.at[:, part], out_hbm.at[:, part], sem.at[len(copies)]
                )
            )
            copies[-1].start()
    wait_all(copies)


def blend(weights, own_blocks, other_blocks, count):
    chips = len(own_blocks)
    features = own_blocks[0].shape[1] * SEGMENTS
    return pl.pallas_call(
        functools.partial(blend_kernel, chips),
        out_shape=jax.ShapeDtypeStruct((count, features), jnp.bfloat16),
        in_specs=[VMEM] * (1 + chips + len(other_blocks)),
        out_specs=HBM,
        scratch_shapes=[
            pltpu.VMEM((count, features), jnp.bfloat16),
            pltpu.SemaphoreType.DMA((2 * SEGMENTS,)),
        ],
        compiler_params=params(16),
        name="blend",
    )(weights, *own_blocks, *other_blocks)


def body(tokens, expert_ids, route_logits, w_gate, w_up, w_down):
    devices = lax.axis_size("expert")
    teams = devices // SPLIT
    chips = SPLIT // CORES
    other_core = [(i, i ^ 1) for i in range(devices)]
    other_chip = [[(i, i ^ (m * CORES)) for i in range(devices)] for m in range(chips)]
    packed, table = pack_rows(expert_ids.T, route_logits.T, tokens, teams)
    def gather(block):
        return [block] + [lax.ppermute(block, "expert", other_chip[m]) for m in range(1, chips)]

    own = gather(packed[0])
    crowds = []
    for k in range(1, teams):
        pairs = [(i, (i + k * SPLIT) % devices) for i in range(devices)]
        block = lax.ppermute(packed[k], "expert", pairs)
        if k == teams - 1:
            block, table = lax.optimization_barrier((block, table))
            weights = blend_weights(table, teams)
        crowds.append(gather(block))
    own, weights = lax.optimization_barrier((own, weights))
    own = join(own)
    first = unpack(own, lax.ppermute(own, "expert", other_core))
    pieces = []
    for crowd in crowds:
        crowd = join(crowd)
        pieces += [crowd, lax.ppermute(crowd, "expert", other_core)]
    *given, hidden = expert_half(first, pieces, w_gate, w_up, w_down)
    taken = [lax.ppermute(piece, "expert", other_core) for piece in given]
    kept = kept_half(hidden, w_down)
    others = []
    for k in range(1, teams):
        parts = add_cores(kept, taken[k], k, chips)
        parts, later = lax.optimization_barrier((parts, kept))
        team = [parts[0]]
        for m in reversed(range(1, chips)):
            team.append(lax.ppermute(parts[m], "expert", other_chip[m]))
        pairs = [(i, (i - k * SPLIT) % devices) for i in range(devices)]
        others.append(lax.ppermute(sum_blocks(team), "expert", pairs))
    parts = add_cores(later, taken[0], 0, chips)
    own = [parts[0]]
    for m in reversed(range(1, chips)):
        own.append(lax.ppermute(parts[m], "expert", other_chip[m]))
    return blend(weights, own, others, tokens.shape[0])


def solution(mesh):
    placed = (
        P(("groups", "expert"), None),
        P(("groups", "expert"), None),
        P(("groups", "expert"), None),
        P(None, "expert"),
        P(None, "expert"),
        P("expert", None),
    )
    return jax.shard_map(
        body, mesh=mesh, in_specs=placed, out_specs=P(("groups", "expert"), None), check_vma=False
    )
```

```python
import functools

import jax
import jax.numpy as jnp
from jax import lax
from jax.experimental import pallas as pl
from jax.experimental.pallas import tpu as pltpu
from jax.sharding import PartitionSpec as P

SPLIT = 8
CAP = 5
CORES = 2
SEGMENTS = 8

route_scale = 2.5

VMEM = pl.BlockSpec(memory_space=pltpu.VMEM)
HBM = pl.BlockSpec(memory_space=pltpu.HBM)
MIB = 1024 * 1024


def hits(ids, mine, teams):
    count = ids.shape[1]
    row = lax.broadcasted_iota(jnp.int32, (8 * pl.cdiv(teams, 8), count), 0)
    wanted = lax.rem(mine + row, teams)
    hit = jnp.zeros(row.shape, jnp.int32)
    for j in range(ids.shape[0]):
        hit = hit + jnp.where(ids[j : j + 1, :] == wanted, 1, 0)
    hit = jnp.where(row < teams, hit, 0).astype(jnp.float32)
    before = lax.broadcasted_iota(jnp.int32, (count, count), 0)
    after = lax.broadcasted_iota(jnp.int32, (count, count), 1)
    earlier = jnp.where(before < after, 1.0, 0.0).astype(jnp.bfloat16)
    slot = jnp.dot(hit.astype(jnp.bfloat16), earlier, preferred_element_type=jnp.float32)
    return hit, jnp.where(hit > 0, slot, -1.0)


def fifth(shape, axis):
    at = lax.broadcasted_iota(jnp.int32, shape, axis)
    segment = jnp.zeros(shape, jnp.int32)
    for s in range(1, SEGMENTS):
        segment = segment + jnp.where(at >= s * CAP, 1, 0)
    return segment, (at - CAP * segment).astype(jnp.float32)


def params(mib):
    return pltpu.CompilerParams(vmem_limit_bytes=int(mib * MIB))


def bring(source, target, semaphores, parts):
    step = source.shape[0] // parts
    copies = []
    for i in range(parts):
        rows = pl.ds(i * step, step)
        copies.append(pltpu.make_async_copy(source.at[rows], target.at[rows], semaphores.at[i]))
        copies[-1].start()
    return copies


def wait_all(copies):
    for copy in copies:
        copy.wait()


def pack_kernel(teams, ids_hbm, logits_hbm, tokens_hbm, *refs):
    *out_refs, table_ref, ids_ref, logits_ref, tokens_ref, ids_sem, logits_sem, tokens_sem = refs
    ids_copy = bring(ids_hbm, ids_ref, ids_sem, 1)
    tokens_copy = bring(tokens_hbm, tokens_ref, tokens_sem, 4)
    logits_copy = bring(logits_hbm, logits_ref, logits_sem, 1)
    wait_all(ids_copy)
    mine = lax.axis_index("expert") // SPLIT
    ids = ids_ref[...]
    hit, slot = hits(ids, mine, teams)
    wait_all(logits_copy)
    lifted = jax.nn.sigmoid(logits_ref[...])
    gates = route_scale * lifted / jnp.sum(lifted, axis=0, keepdims=True)
    row = lax.broadcasted_iota(jnp.int32, hit.shape, 0)
    wanted = lax.rem(mine + row, teams)
    gate = jnp.zeros(hit.shape, jnp.float32)
    for j in range(ids.shape[0]):
        gate = gate + jnp.where(ids[j : j + 1, :] == wanted, gates[j : j + 1, :], 0.0)
    table_ref[: hit.shape[0], :] = slot
    table_ref[hit.shape[0] :, :] = gate
    count, features = tokens_ref.shape
    wide = features // SEGMENTS
    tall = CAP * SEGMENTS
    segment, place = fifth((tall, 1), 0)
    column = lax.broadcasted_iota(jnp.int32, (1, SEGMENTS * count), 1)
    same = segment == column // count
    picks = []
    for k in range(teams):
        slots = jnp.concatenate([slot[k : k + 1, :]] * SEGMENTS, axis=1)
        picks.append(jnp.where(same & (slots == place), 1.0, 0.0))
    wait_all(tokens_copy)
    stacked = jnp.concatenate(
        [tokens_ref[:, s * wide : (s + 1) * wide] for s in range(SEGMENTS)], axis=0
    )
    packed = jnp.dot(
        jnp.concatenate(picks, axis=0).astype(jnp.bfloat16),
        stacked,
        preferred_element_type=jnp.float32,
    )
    for k in range(teams):
        out_refs[k][...] = packed[k * tall : (k + 1) * tall].astype(jnp.bfloat16)


def pack_rows(ids, logits, tokens, teams):
    wide = tokens.shape[1] // SEGMENTS
    block = jax.ShapeDtypeStruct((CAP * SEGMENTS, wide), jnp.bfloat16)
    table = jax.ShapeDtypeStruct((16 * pl.cdiv(teams, 8), ids.shape[1]), jnp.float32)
    *packed, table = pl.pallas_call(
        functools.partial(pack_kernel, teams),
        out_shape=[block] * teams + [table],
        in_specs=[HBM] * 3,
        out_specs=[VMEM] * (teams + 1),
        scratch_shapes=[
            pltpu.VMEM(ids.shape, ids.dtype),
            pltpu.VMEM(logits.shape, logits.dtype),
            pltpu.VMEM(tokens.shape, tokens.dtype),
            pltpu.SemaphoreType.DMA((1,)),
            pltpu.SemaphoreType.DMA((1,)),
            pltpu.SemaphoreType.DMA((4,)),
        ],
        name="pack_rows",
    )(ids, logits, tokens)
    return packed, table


def weight_kernel(teams, table_ref, out_ref):
    rows, count = table_ref.shape
    slot = jnp.transpose(table_ref[: rows // 2, :])
    gate = jnp.transpose(table_ref[rows // 2 :, :])
    tall = CAP * SEGMENTS
    depth = out_ref.shape[1]
    column = lax.broadcasted_iota(jnp.int32, (1, depth), 1)
    part = jnp.zeros((1, depth), jnp.int32)
    for g in range(1, depth // tall):
        part = part + jnp.where(column >= g * tall, 1, 0)
    column = column - tall * part
    segment = jnp.zeros((1, depth), jnp.int32)
    for s in range(1, SEGMENTS):
        segment = segment + jnp.where(column >= s * CAP, 1, 0)
    place = (column - CAP * segment).astype(jnp.float32)
    team = jnp.where(part < 3, 0, (part - 1) >> 1)
    low = jnp.where(part < 3, part >> 1, (part - 3) & 1) == 1
    for s in range(SEGMENTS):
        full = jnp.zeros((count, depth), jnp.float32)
        for k in range(teams):
            chosen = (team == k) & (segment == s) & (slot[:, k : k + 1] == place)
            full = full + jnp.where(chosen, gate[:, k : k + 1], 0.0)
        high = full.astype(jnp.bfloat16).astype(jnp.float32)
        out_ref[s * count : (s + 1) * count, :] = jnp.where(low, full - high, high).astype(
            jnp.bfloat16
        )


def blend_weights(table, teams):
    shape = (SEGMENTS * table.shape[1], CAP * SEGMENTS * (1 + 2 * teams))
    return pl.pallas_call(
        functools.partial(weight_kernel, teams),
        out_shape=jax.ShapeDtypeStruct(shape, jnp.bfloat16),
        in_specs=[VMEM],
        out_specs=VMEM,
        compiler_params=params(4 + teams),
        cost_estimate=pl.CostEstimate(flops=6 * 10**9, bytes_accessed=8 * MIB, transcendentals=0),
        name="blend_weights",
    )(table)


def join_kernel(*refs):
    tall = refs[0].shape[0]
    for i, ref in enumerate(refs[:-1]):
        refs[-1][i * tall : (i + 1) * tall, :] = ref[...]


def join(blocks):
    tall, wide = blocks[0].shape
    return pl.pallas_call(
        join_kernel,
        out_shape=jax.ShapeDtypeStruct((tall * len(blocks), wide), blocks[0].dtype),
        in_specs=[VMEM] * len(blocks),
        out_specs=VMEM,
        compiler_params=params(4),
        name="join",
    )(*blocks)


def packed_down(hidden, down_ref, out_ref, flat):
    count, wide = flat.shape[1:]
    tall = CAP * SEGMENTS
    for s in range(SEGMENTS):
        slot = flat.at[s % 2]
        slot[...] = jnp.dot(
            hidden, down_ref[:, s * wide : (s + 1) * wide], preferred_element_type=jnp.float32
        )
        for b in range(count // CAP):
            start = b * tall + s * CAP
            out_ref[start : start + CAP, :] = slot[b * CAP : (b + 1) * CAP, :]


def unpack_kernel(own_ref, other_ref, out_ref, packed):
    tall = CAP * SEGMENTS
    half = own_ref.shape[0]
    wide = own_ref.shape[1]
    packed[:half, :] = own_ref[...].astype(jnp.float32)
    packed[half:, :] = other_ref[...].astype(jnp.float32)
    for s in range(SEGMENTS):
        for b in range(2 * half // tall):
            start = b * tall + s * CAP
            out_ref[b * CAP : (b + 1) * CAP, s * wide : (s + 1) * wide] = packed[
                start : start + CAP, :
            ]


def unpack(own, other):
    rows, wide = own.shape
    return pl.pallas_call(
        unpack_kernel,
        out_shape=jax.ShapeDtypeStruct((2 * rows // SEGMENTS, wide * SEGMENTS), jnp.float32),
        in_specs=[VMEM] * 2,
        out_specs=VMEM,
        scratch_shapes=[pltpu.VMEM((2 * rows, wide), jnp.float32)],
        compiler_params=params(6),
        name="unpack",
    )(own, other)


def expert_kernel(teams, first_ref, *refs):
    pieces = refs[: 4 * (teams - 1)]
    gate_ref, up_ref, down_ref = refs[4 * (teams - 1) : 4 * teams - 1]
    *given_refs, hidden_ref, packed, flat, out, act = refs[4 * teams - 1 :]
    tall = CAP * SEGMENTS
    wide = packed.shape[1]
    units = gate_ref.shape[1]
    start = 0
    for ref in pieces:
        packed[start : start + ref.shape[0], :] = ref[...].astype(jnp.float32)
        start += ref.shape[0]
    known = first_ref.shape[0]
    count = known * teams
    gate_act = jnp.zeros((count, units), jnp.float32)
    up_act = jnp.zeros((count, units), jnp.float32)
    for s in range(SEGMENTS):
        slot = flat.at[s % 2]
        columns = slice(s * wide, (s + 1) * wide)
        slot[:known, :] = first_ref[:, columns]
        for b in range((count - known) // CAP):
            start = b * tall + s * CAP
            slot[known + b * CAP : known + (b + 1) * CAP, :] = packed[start : start + CAP, :]
        rows = slot[...].astype(jnp.bfloat16)
        gate_act += jnp.dot(rows, gate_ref[columns, :], preferred_element_type=jnp.float32)
        up_act += jnp.dot(rows, up_ref[columns, :], preferred_element_type=jnp.float32)
    act[:count, :] = jax.nn.silu(gate_act) * up_act
    half = known // 2
    for k in range(teams):
        for core in range(CORES):
            source = (CORES * k + core) * half
            target = count + (core * teams + k) * half
            act[target : target + half, :] = act[source : source + half, :]
    hidden = act[count:, :].astype(jnp.bfloat16)
    half = count // 2
    hidden_ref[...] = hidden[:half]
    packed_down(hidden[half:], down_ref, out, flat.at[:, :half, :])
    for k, given_ref in enumerate(given_refs):
        rows = given_ref.shape[0]
        given_ref[...] = out[k * rows : (k + 1) * rows, :].astype(jnp.bfloat16)


def expert_half(first, pieces, w_gate, w_up, w_down):
    teams = 1 + len(pieces) // 4
    block, wide = first.shape[0] // 2 * SEGMENTS, pieces[0].shape[1]
    features, units = w_gate.shape
    rows = first.shape[0] * teams
    return pl.pallas_call(
        functools.partial(expert_kernel, teams),
        out_shape=[jax.ShapeDtypeStruct((block, wide), jnp.bfloat16)] * teams
        + [jax.ShapeDtypeStruct((rows // 2, units), jnp.bfloat16)],
        in_specs=[VMEM] * (len(pieces) + 4),
        out_specs=[VMEM] * (teams + 1),
        scratch_shapes=[
            pltpu.VMEM((2 * block * (teams - 1), wide), jnp.float32),
            pltpu.VMEM((2, rows, wide), jnp.float32),
            pltpu.VMEM((block * teams, wide), jnp.float32),
            pltpu.VMEM((2 * rows, units), jnp.float32),
        ],
        compiler_params=params(16 + 4 * teams),
        cost_estimate=pl.CostEstimate(
            flops=5 * rows * units * features,
            bytes_accessed=6 * features * units,
            transcendentals=rows * units,
        ),
        name="expert_half",
    )(first, *pieces, w_gate, w_up, w_down)


def kept_kernel(hidden_ref, down_ref, kept_ref, flat):
    packed_down(hidden_ref[...], down_ref, kept_ref, flat)


def kept_half(hidden, w_down):
    count, units = hidden.shape
    features = w_down.shape[1]
    wide = features // SEGMENTS
    return pl.pallas_call(
        kept_kernel,
        out_shape=jax.ShapeDtypeStruct((count * SEGMENTS, wide), jnp.float32),
        in_specs=[VMEM] * 2,
        out_specs=VMEM,
        scratch_shapes=[pltpu.VMEM((2, count, wide), jnp.float32)],
        compiler_params=params(8 + count // 10),
        cost_estimate=pl.CostEstimate(
            flops=2 * count * units * features,
            bytes_accessed=2 * features * units,
            transcendentals=0,
        ),
        name="kept_half",
    )(hidden, w_down)


def add_kernel(first, kept_ref, taken_ref, *out_refs):
    tall = out_refs[0].shape[0]
    for b, out_ref in enumerate(out_refs):
        rows = slice(b * tall, (b + 1) * tall)
        total = kept_ref[first + b * tall : first + (b + 1) * tall, :] + taken_ref[
            rows, :
        ].astype(jnp.float32)
        out_ref[...] = total.astype(out_ref.dtype)


def add_cores(kept, taken, k, chips):
    shape = (CAP * SEGMENTS, kept.shape[1])
    outs = [jax.ShapeDtypeStruct(shape, jnp.bfloat16 if m else jnp.float32) for m in range(chips)]
    return pl.pallas_call(
        functools.partial(add_kernel, k * taken.shape[0]),
        out_shape=outs,
        in_specs=[VMEM] * 2,
        out_specs=[VMEM] * len(outs),
        compiler_params=params(6),
        name="add_cores",
    )(kept, taken)


def sum_kernel(*refs):
    total = refs[0][...]
    for ref in refs[1:-1]:
        total = total + ref[...].astype(jnp.float32)
    refs[-1][...] = total.astype(refs[-1].dtype)


def sum_blocks(blocks):
    return pl.pallas_call(
        sum_kernel,
        out_shape=jax.ShapeDtypeStruct(blocks[0].shape, jnp.bfloat16),
        in_specs=[VMEM] * len(blocks),
        out_specs=VMEM,
        compiler_params=params(4),
        name="sum_blocks",
    )(*blocks)


def halves(wide):
    cut = 128 * pl.cdiv(wide // 128, 2)
    return slice(0, cut), slice(cut, wide)


def blend_kernel(chips, weight_ref, *refs):
    *refs, out_hbm, out_ref, sem = refs
    count, features = out_ref.shape
    wide = features // SEGMENTS
    own = refs[0][...]
    for ref in refs[1:chips]:
        own = own + ref[...].astype(jnp.float32)
    high = own.astype(jnp.bfloat16).astype(jnp.float32)
    terms = [high, own - high, high]
    for ref in refs[chips:]:
        terms += [ref[...].astype(jnp.float32)] * 2
    rows = jnp.concatenate(terms, axis=0).astype(jnp.bfloat16)
    copies = []
    for columns in halves(wide):
        size = columns.stop - columns.start
        total = jnp.dot(weight_ref[...], rows[:, columns], preferred_element_type=jnp.float32)
        for s in range(SEGMENTS):
            part = pl.ds(s * wide + columns.start, size)
            out_ref[:, part] = total[s * count : (s + 1) * count].astype(jnp.bfloat16)
            copies.append(
                pltpu.make_async_copy(
                    out_ref.at[:, part], out_hbm.at[:, part], sem.at[len(copies)]
                )
            )
            copies[-1].start()
    wait_all(copies)


def blend(weights, own_blocks, other_blocks, count):
    chips = len(own_blocks)
    features = own_blocks[0].shape[1] * SEGMENTS
    return pl.pallas_call(
        functools.partial(blend_kernel, chips),
        out_shape=jax.ShapeDtypeStruct((count, features), jnp.bfloat16),
        in_specs=[VMEM] * (1 + chips + len(other_blocks)),
        out_specs=HBM,
        scratch_shapes=[
            pltpu.VMEM((count, features), jnp.bfloat16),
            pltpu.SemaphoreType.DMA((2 * SEGMENTS,)),
        ],
        compiler_params=params(16),
        name="blend",
    )(weights, *own_blocks, *other_blocks)


def body(tokens, expert_ids, route_logits, w_gate, w_up, w_down):
    devices = lax.axis_size("expert")
    teams = devices // SPLIT
    chips = SPLIT // CORES
    other_core = [(i, i ^ 1) for i in range(devices)]
    other_chip = [[(i, i ^ (m * CORES)) for i in range(devices)] for m in range(chips)]
    packed, table = pack_rows(expert_ids.T, route_logits.T, tokens, teams)
    def gather(block):
        return [block] + [lax.ppermute(block, "expert", other_chip[m]) for m in range(1, chips)]

    own = gather(packed[0])
    crowds = []
    for k in range(1, teams):
        pairs = [(i, (i + k * SPLIT) % devices) for i in range(devices)]
        block = lax.ppermute(packed[k], "expert", pairs)
        if k == teams - 1:
            block, table = lax.optimization_barrier((block, table))
            weights = blend_weights(table, teams)
        crowds.append(gather(block))
    own, weights = lax.optimization_barrier((own, weights))
    own = join(own)
    first = unpack(own, lax.ppermute(own, "expert", other_core))
    order = [0, *reversed(range(1, chips))]
    pieces = []
    for crowd in crowds:
        early, late = join([crowd[m] for m in order[:-1]]), crowd[order[-1]]
        pieces += [early, late]
        pieces += [lax.ppermute(piece, "expert", other_core) for piece in (early, late)]
    *given, hidden = expert_half(first, pieces, w_gate, w_up, w_down)
    taken = [lax.ppermute(piece, "expert", other_core) for piece in given]
    kept = kept_half(hidden, w_down)
    others = []
    for k in range(1, teams):
        parts = add_cores(kept, taken[k], k, chips)
        parts, later = lax.optimization_barrier((parts, kept))
        team = [parts[0]]
        for m, part in zip(order[1:], parts[1:]):
            team.append(lax.ppermute(part, "expert", other_chip[m]))
        pairs = [(i, (i - k * SPLIT) % devices) for i in range(devices)]
        others.append(lax.ppermute(sum_blocks(team), "expert", pairs))
    parts = add_cores(later, taken[0], 0, chips)
    own = [parts[0]]
    for m in reversed(range(1, chips)):
        own.append(lax.ppermute(parts[m], "expert", other_chip[m]))
    return blend(weights, own, others, tokens.shape[0])


def solution(mesh):
    placed = (
        P(("groups", "expert"), None),
        P(("groups", "expert"), None),
        P(("groups", "expert"), None),
        P(None, "expert"),
        P(None, "expert"),
        P("expert", None),
    )
    return jax.shard_map(
        body, mesh=mesh, in_specs=placed, out_specs=P(("groups", "expert"), None), check_vma=False
    )
```

```python
import functools

import jax
import jax.numpy as jnp
from jax import lax
from jax.experimental import pallas as pl
from jax.experimental.pallas import tpu as pltpu
from jax.sharding import PartitionSpec as P

SPLIT = 8
CAP = 5
CORES = 2
SEGMENTS = 8

route_scale = 2.5

ROOM = 8

VMEM = pl.BlockSpec(memory_space=pltpu.VMEM)
HBM = pl.BlockSpec(memory_space=pltpu.HBM)
MIB = 1024 * 1024


def hits(ids, mine, teams):
    count = ids.shape[1]
    row = lax.broadcasted_iota(jnp.int32, (8 * pl.cdiv(teams, 8), count), 0)
    wanted = lax.rem(mine + row, teams)
    hit = jnp.zeros(row.shape, jnp.int32)
    for j in range(ids.shape[0]):
        hit = hit + jnp.where(ids[j : j + 1, :] == wanted, 1, 0)
    hit = jnp.where(row < teams, hit, 0).astype(jnp.float32)
    before = lax.broadcasted_iota(jnp.int32, (count, count), 0)
    after = lax.broadcasted_iota(jnp.int32, (count, count), 1)
    earlier = jnp.where(before < after, 1.0, 0.0).astype(jnp.bfloat16)
    slot = jnp.dot(hit.astype(jnp.bfloat16), earlier, preferred_element_type=jnp.float32)
    return hit, jnp.where(hit > 0, slot, -1.0)


def fifth(shape, axis):
    at = lax.broadcasted_iota(jnp.int32, shape, axis)
    segment = jnp.zeros(shape, jnp.int32)
    for s in range(1, SEGMENTS):
        segment = segment + jnp.where(at >= s * CAP, 1, 0)
    return segment, (at - CAP * segment).astype(jnp.float32)


def params(mib):
    return pltpu.CompilerParams(vmem_limit_bytes=int(mib * MIB))


def bring(source, target, semaphores, parts):
    step = source.shape[0] // parts
    copies = []
    for i in range(parts):
        rows = pl.ds(i * step, step)
        copies.append(pltpu.make_async_copy(source.at[rows], target.at[rows], semaphores.at[i]))
        copies[-1].start()
    return copies


def wait_all(copies):
    for copy in copies:
        copy.wait()


def pack_kernel(teams, ids_hbm, logits_hbm, tokens_hbm, *refs):
    *out_refs, table_ref, ids_ref, logits_ref, tokens_ref, ids_sem, logits_sem, tokens_sem = refs
    ids_copy = bring(ids_hbm, ids_ref, ids_sem, 1)
    tokens_copy = bring(tokens_hbm, tokens_ref, tokens_sem, 4)
    logits_copy = bring(logits_hbm, logits_ref, logits_sem, 1)
    wait_all(ids_copy)
    mine = lax.axis_index("expert") // SPLIT
    ids = ids_ref[...]
    hit, slot = hits(ids, mine, teams)
    wait_all(logits_copy)
    lifted = jax.nn.sigmoid(logits_ref[...])
    gates = route_scale * lifted / jnp.sum(lifted, axis=0, keepdims=True)
    row = lax.broadcasted_iota(jnp.int32, hit.shape, 0)
    wanted = lax.rem(mine + row, teams)
    gate = jnp.zeros(hit.shape, jnp.float32)
    for j in range(ids.shape[0]):
        gate = gate + jnp.where(ids[j : j + 1, :] == wanted, gates[j : j + 1, :], 0.0)
    table_ref[: hit.shape[0], :] = slot
    table_ref[hit.shape[0] :, :] = gate
    count, features = tokens_ref.shape
    wide = features // SEGMENTS
    tall = CAP * SEGMENTS
    segment, place = fifth((tall, 1), 0)
    column = lax.broadcasted_iota(jnp.int32, (1, SEGMENTS * count), 1)
    same = segment == column // count
    picks = []
    for k in range(teams):
        slots = jnp.concatenate([slot[k : k + 1, :]] * SEGMENTS, axis=1)
        picks.append(jnp.where(same & (slots == place), 1.0, 0.0))
    wait_all(tokens_copy)
    stacked = jnp.concatenate(
        [tokens_ref[:, s * wide : (s + 1) * wide] for s in range(SEGMENTS)], axis=0
    )
    packed = jnp.dot(
        jnp.concatenate(picks, axis=0).astype(jnp.bfloat16),
        stacked,
        preferred_element_type=jnp.float32,
    )
    for k in range(teams):
        out_refs[k][...] = packed[k * tall : (k + 1) * tall].astype(jnp.bfloat16)


def pack_rows(ids, logits, tokens, teams):
    wide = tokens.shape[1] // SEGMENTS
    block = jax.ShapeDtypeStruct((CAP * SEGMENTS, wide), jnp.bfloat16)
    table = jax.ShapeDtypeStruct((16 * pl.cdiv(teams, 8), ids.shape[1]), jnp.float32)
    *packed, table = pl.pallas_call(
        functools.partial(pack_kernel, teams),
        out_shape=[block] * teams + [table],
        in_specs=[HBM] * 3,
        out_specs=[VMEM] * (teams + 1),
        scratch_shapes=[
            pltpu.VMEM(ids.shape, ids.dtype),
            pltpu.VMEM(logits.shape, logits.dtype),
            pltpu.VMEM(tokens.shape, tokens.dtype),
            pltpu.SemaphoreType.DMA((1,)),
            pltpu.SemaphoreType.DMA((1,)),
            pltpu.SemaphoreType.DMA((4,)),
        ],
        name="pack_rows",
    )(ids, logits, tokens)
    return packed, table


def weight_kernel(teams, table_ref, out_ref):
    rows, count = table_ref.shape
    slot = jnp.transpose(table_ref[: rows // 2, :])
    gate = jnp.transpose(table_ref[rows // 2 :, :])
    tall = CAP * SEGMENTS
    depth = out_ref.shape[1]
    column = lax.broadcasted_iota(jnp.int32, (1, depth), 1)
    part = jnp.zeros((1, depth), jnp.int32)
    for g in range(1, depth // tall):
        part = part + jnp.where(column >= g * tall, 1, 0)
    column = column - tall * part
    segment = jnp.zeros((1, depth), jnp.int32)
    for s in range(1, SEGMENTS):
        segment = segment + jnp.where(column >= s * CAP, 1, 0)
    place = (column - CAP * segment).astype(jnp.float32)
    team = jnp.where(part < 3, 0, (part - 1) >> 1)
    low = jnp.where(part < 3, part >> 1, (part - 3) & 1) == 1
    for s in range(SEGMENTS):
        full = jnp.zeros((count, depth), jnp.float32)
        for k in range(teams):
            chosen = (team == k) & (segment == s) & (slot[:, k : k + 1] == place)
            full = full + jnp.where(chosen, gate[:, k : k + 1], 0.0)
        high = full.astype(jnp.bfloat16).astype(jnp.float32)
        out_ref[s * count : (s + 1) * count, :] = jnp.where(low, full - high, high).astype(
            jnp.bfloat16
        )


def blend_weights(table, teams):
    shape = (SEGMENTS * table.shape[1], CAP * SEGMENTS * (1 + 2 * teams))
    return pl.pallas_call(
        functools.partial(weight_kernel, teams),
        out_shape=jax.ShapeDtypeStruct(shape, jnp.bfloat16),
        in_specs=[VMEM],
        out_specs=VMEM,
        compiler_params=params(4 + teams),
        cost_estimate=pl.CostEstimate(flops=6 * 10**9, bytes_accessed=8 * MIB, transcendentals=0),
        name="blend_weights",
    )(table)


def join_kernel(*refs):
    blocks = [ref[...].astype(jnp.float32) for ref in refs[:-1]]
    refs[-1][...] = jnp.concatenate(blocks, axis=0).astype(refs[-1].dtype)


def join(blocks):
    tall, wide = blocks[0].shape
    return pl.pallas_call(
        join_kernel,
        out_shape=jax.ShapeDtypeStruct((tall * len(blocks), wide), blocks[0].dtype),
        in_specs=[VMEM] * len(blocks),
        out_specs=VMEM,
        compiler_params=params(4),
        name="join",
    )(*blocks)


def packed_down(hidden, down_ref, out_ref, flat):
    count, wide = hidden.shape[0], flat.shape[2]
    tall = CAP * SEGMENTS
    for s in range(SEGMENTS):
        slot = flat.at[s % 2]
        slot[:count, :] = jnp.dot(
            hidden, down_ref[:, s * wide : (s + 1) * wide], preferred_element_type=jnp.float32
        )
        for b in range(count // CAP):
            start = b * tall + s * CAP
            out_ref[start : start + CAP, :] = slot[b * CAP : (b + 1) * CAP, :]


def unpack_kernel(own_ref, other_ref, out_ref, packed):
    tall = CAP * SEGMENTS
    half = own_ref.shape[0]
    wide = own_ref.shape[1]
    packed[:half, :] = own_ref[...].astype(jnp.float32)
    packed[half : 2 * half, :] = other_ref[...].astype(jnp.float32)
    for s in range(SEGMENTS):
        for b in range(2 * half // tall):
            start = b * tall + s * CAP
            out_ref[b * CAP : (b + 1) * CAP, s * wide : (s + 1) * wide] = packed[
                start : start + CAP, :
            ]


def unpack(own, other):
    rows, wide = own.shape
    return pl.pallas_call(
        unpack_kernel,
        out_shape=jax.ShapeDtypeStruct(
            (2 * rows // SEGMENTS + ROOM, wide * SEGMENTS), jnp.float32
        ),
        in_specs=[VMEM] * 2,
        out_specs=VMEM,
        scratch_shapes=[pltpu.VMEM((2 * rows + ROOM, wide), jnp.float32)],
        compiler_params=params(6),
        name="unpack",
    )(own, other)


def expert_kernel(teams, first_ref, *refs):
    pieces = refs[: 2 * (teams - 1)]
    gate_ref, up_ref, down_ref = refs[2 * (teams - 1) : 2 * teams + 1]
    *given_refs, hidden_ref, packed, flat, out, act = refs[2 * teams + 1 :]
    tall = CAP * SEGMENTS
    wide = packed.shape[1]
    units = gate_ref.shape[1]
    start = 0
    for ref in pieces:
        packed[start : start + ref.shape[0], :] = ref[...].astype(jnp.float32)
        start += ref.shape[0]
    known = first_ref.shape[0] - ROOM
    count = known * teams
    gate_act = jnp.zeros((count, units), jnp.float32)
    up_act = jnp.zeros((count, units), jnp.float32)
    for s in range(SEGMENTS):
        slot = flat.at[s % 2]
        columns = slice(s * wide, (s + 1) * wide)
        slot[:known, :] = first_ref[:known, columns]
        for b in range((count - known) // CAP):
            start = b * tall + s * CAP
            slot[known + b * CAP : known + (b + 1) * CAP, :] = packed[start : start + CAP, :]
        rows = slot[:count, :].astype(jnp.bfloat16)
        gate_act += jnp.dot(rows, gate_ref[columns, :], preferred_element_type=jnp.float32)
        up_act += jnp.dot(rows, up_ref[columns, :], preferred_element_type=jnp.float32)
    act[:count, :] = jax.nn.silu(gate_act) * up_act
    half = known // 2
    for k in range(teams):
        for core in range(CORES):
            source = (CORES * k + core) * half
            target = count + (core * teams + k) * half
            act[target : target + half, :] = act[source : source + half, :]
    half = count // 2
    hidden_ref[...] = act[count : count + half, :].astype(jnp.bfloat16)
    given = act[count + half : 2 * count, :].astype(jnp.bfloat16)
    packed_down(given, down_ref, out, flat)
    for k, given_ref in enumerate(given_refs):
        rows = given_ref.shape[0]
        given_ref[...] = out[k * rows : (k + 1) * rows, :].astype(jnp.bfloat16)


def expert_half(first, pieces, w_gate, w_up, w_down):
    teams = 1 + len(pieces) // 2
    block, wide = pieces[0].shape
    features, units = w_gate.shape
    rows = (first.shape[0] - ROOM) * teams
    return pl.pallas_call(
        functools.partial(expert_kernel, teams),
        out_shape=[jax.ShapeDtypeStruct((block, wide), jnp.bfloat16)] * teams
        + [jax.ShapeDtypeStruct((rows // 2, units), jnp.bfloat16)],
        in_specs=[VMEM] * (len(pieces) + 4),
        out_specs=[VMEM] * (teams + 1),
        scratch_shapes=[
            pltpu.VMEM((block * len(pieces) + ROOM, wide), jnp.float32),
            pltpu.VMEM((2, rows + ROOM, wide), jnp.float32),
            pltpu.VMEM((block * teams + ROOM, wide), jnp.float32),
            pltpu.VMEM((2 * rows + ROOM, units), jnp.float32),
        ],
        compiler_params=params(16 + 4 * teams),
        cost_estimate=pl.CostEstimate(
            flops=5 * rows * units * features,
            bytes_accessed=6 * features * units,
            transcendentals=rows * units,
        ),
        name="expert_half",
    )(first, *pieces, w_gate, w_up, w_down)


def kept_kernel(hidden_ref, down_ref, kept_ref, flat):
    packed_down(hidden_ref[...], down_ref, kept_ref, flat)


def kept_half(hidden, w_down):
    count, units = hidden.shape
    features = w_down.shape[1]
    wide = features // SEGMENTS
    return pl.pallas_call(
        kept_kernel,
        out_shape=jax.ShapeDtypeStruct((count * SEGMENTS + ROOM, wide), jnp.float32),
        in_specs=[VMEM] * 2,
        out_specs=VMEM,
        scratch_shapes=[pltpu.VMEM((2, count + ROOM, wide), jnp.float32)],
        compiler_params=params(8 + count // 10),
        cost_estimate=pl.CostEstimate(
            flops=2 * count * units * features,
            bytes_accessed=2 * features * units,
            transcendentals=0,
        ),
        name="kept_half",
    )(hidden, w_down)


def add_kernel(first, kept_ref, taken_ref, *out_refs):
    tall = out_refs[0].shape[0]
    total = kept_ref[first : first + taken_ref.shape[0], :] + taken_ref[...].astype(jnp.float32)
    for b, out_ref in enumerate(out_refs):
        out_ref[...] = total[b * tall : (b + 1) * tall].astype(out_ref.dtype)


def add_cores(kept, taken, k, chips):
    shape = (CAP * SEGMENTS, kept.shape[1])
    outs = [jax.ShapeDtypeStruct(shape, jnp.bfloat16 if m else jnp.float32) for m in range(chips)]
    return pl.pallas_call(
        functools.partial(add_kernel, k * taken.shape[0]),
        out_shape=outs,
        in_specs=[VMEM] * 2,
        out_specs=[VMEM] * len(outs),
        compiler_params=params(6),
        name="add_cores",
    )(kept, taken)


def sum_kernel(*refs):
    total = refs[0][...]
    for ref in refs[1:-1]:
        total = total + ref[...].astype(jnp.float32)
    refs[-1][...] = total.astype(refs[-1].dtype)


def sum_blocks(blocks):
    return pl.pallas_call(
        sum_kernel,
        out_shape=jax.ShapeDtypeStruct(blocks[0].shape, jnp.bfloat16),
        in_specs=[VMEM] * len(blocks),
        out_specs=VMEM,
        compiler_params=params(4),
        name="sum_blocks",
    )(*blocks)


def halves(wide):
    cut = 128 * pl.cdiv(wide // 128, 2)
    return slice(0, cut), slice(cut, wide)


def blend_kernel(chips, weight_ref, *refs):
    *refs, out_hbm, out_ref, sem = refs
    count, features = out_ref.shape
    wide = features // SEGMENTS
    own = refs[0][...]
    for ref in refs[1:chips]:
        own = own + ref[...].astype(jnp.float32)
    high = own.astype(jnp.bfloat16).astype(jnp.float32)
    terms = [high, own - high, high]
    for ref in refs[chips:]:
        terms += [ref[...].astype(jnp.float32)] * 2
    rows = jnp.concatenate(terms, axis=0).astype(jnp.bfloat16)
    copies = []
    for columns in halves(wide):
        size = columns.stop - columns.start
        total = jnp.dot(weight_ref[...], rows[:, columns], preferred_element_type=jnp.float32)
        for s in range(SEGMENTS):
            part = pl.ds(s * wide + columns.start, size)
            out_ref[:, part] = total[s * count : (s + 1) * count].astype(jnp.bfloat16)
            copies.append(
                pltpu.make_async_copy(
                    out_ref.at[:, part], out_hbm.at[:, part], sem.at[len(copies)]
                )
            )
            copies[-1].start()
    wait_all(copies)


def blend(weights, own_blocks, other_blocks, count):
    chips = len(own_blocks)
    features = own_blocks[0].shape[1] * SEGMENTS
    return pl.pallas_call(
        functools.partial(blend_kernel, chips),
        out_shape=jax.ShapeDtypeStruct((count, features), jnp.bfloat16),
        in_specs=[VMEM] * (1 + chips + len(other_blocks)),
        out_specs=HBM,
        scratch_shapes=[
            pltpu.VMEM((count, features), jnp.bfloat16),
            pltpu.SemaphoreType.DMA((2 * SEGMENTS,)),
        ],
        compiler_params=params(16),
        name="blend",
    )(weights, *own_blocks, *other_blocks)


def body(tokens, expert_ids, route_logits, w_gate, w_up, w_down):
    devices = lax.axis_size("expert")
    teams = devices // SPLIT
    chips = SPLIT // CORES
    other_core = [(i, i ^ 1) for i in range(devices)]
    other_chip = [[(i, i ^ (m * CORES)) for i in range(devices)] for m in range(chips)]
    packed, table = pack_rows(expert_ids.T, route_logits.T, tokens, teams)
    def gather(block):
        return [block] + [lax.ppermute(block, "expert", other_chip[m]) for m in range(1, chips)]

    own = gather(packed[0])
    crowds = []
    for k in range(1, teams):
        pairs = [(i, (i + k * SPLIT) % devices) for i in range(devices)]
        block = lax.ppermute(packed[k], "expert", pairs)
        if k == teams - 1:
            block, table = lax.optimization_barrier((block, table))
            weights = blend_weights(table, teams)
        crowds.append(gather(block))
    own, weights = lax.optimization_barrier((own, weights))
    own = join(own)
    first = unpack(own, lax.ppermute(own, "expert", other_core))
    pieces = []
    for crowd in crowds:
        crowd = join(crowd)
        pieces += [crowd, lax.ppermute(crowd, "expert", other_core)]
    *given, hidden = expert_half(first, pieces, w_gate, w_up, w_down)
    taken = [lax.ppermute(piece, "expert", other_core) for piece in given]
    kept = kept_half(hidden, w_down)
    others = []
    for k in range(1, teams):
        parts = add_cores(kept, taken[k], k, chips)
        parts, later = lax.optimization_barrier((parts, kept))
        team = [parts[0]]
        for m in reversed(range(1, chips)):
            team.append(lax.ppermute(parts[m], "expert", other_chip[m]))
        pairs = [(i, (i - k * SPLIT) % devices) for i in range(devices)]
        others.append(lax.ppermute(sum_blocks(team), "expert", pairs))
    parts = add_cores(later, taken[0], 0, chips)
    own = [parts[0]]
    for m in reversed(range(1, chips)):
        own.append(lax.ppermute(parts[m], "expert", other_chip[m]))
    return blend(weights, own, others, tokens.shape[0])


def solution(mesh):
    placed = (
        P(("groups", "expert"), None),
        P(("groups", "expert"), None),
        P(("groups", "expert"), None),
        P(None, "expert"),
        P(None, "expert"),
        P("expert", None),
    )
    return jax.shard_map(
        body, mesh=mesh, in_specs=placed, out_specs=P(("groups", "expert"), None), check_vma=False
    )
```

```python
import functools

import jax
import jax.numpy as jnp
from jax import lax
from jax.experimental import pallas as pl
from jax.experimental.pallas import tpu as pltpu
from jax.sharding import PartitionSpec as P

SPLIT = 8
CAP = 5
CORES = 2
SEGMENTS = 8

route_scale = 2.5

ROOM = 8

VMEM = pl.BlockSpec(memory_space=pltpu.VMEM)
HBM = pl.BlockSpec(memory_space=pltpu.HBM)
MIB = 1024 * 1024


def hits(ids, mine, teams):
    count = ids.shape[1]
    row = lax.broadcasted_iota(jnp.int32, (8 * pl.cdiv(teams, 8), count), 0)
    wanted = lax.rem(mine + row, teams)
    hit = jnp.zeros(row.shape, jnp.int32)
    for j in range(ids.shape[0]):
        hit = hit + jnp.where(ids[j : j + 1, :] == wanted, 1, 0)
    hit = jnp.where(row < teams, hit, 0).astype(jnp.float32)
    before = lax.broadcasted_iota(jnp.int32, (count, count), 0)
    after = lax.broadcasted_iota(jnp.int32, (count, count), 1)
    earlier = jnp.where(before < after, 1.0, 0.0).astype(jnp.bfloat16)
    slot = jnp.dot(hit.astype(jnp.bfloat16), earlier, preferred_element_type=jnp.float32)
    return hit, jnp.where(hit > 0, slot, -1.0)


def fifth(shape, axis):
    at = lax.broadcasted_iota(jnp.int32, shape, axis)
    segment = jnp.zeros(shape, jnp.int32)
    for s in range(1, SEGMENTS):
        segment = segment + jnp.where(at >= s * CAP, 1, 0)
    return segment, (at - CAP * segment).astype(jnp.float32)


def params(mib):
    return pltpu.CompilerParams(vmem_limit_bytes=int(mib * MIB))


def bring(source, target, semaphores, parts):
    step = source.shape[0] // parts
    copies = []
    for i in range(parts):
        rows = pl.ds(i * step, step)
        copies.append(pltpu.make_async_copy(source.at[rows], target.at[rows], semaphores.at[i]))
        copies[-1].start()
    return copies


def wait_all(copies):
    for copy in copies:
        copy.wait()


def pack_kernel(teams, ids_hbm, logits_hbm, tokens_hbm, *refs):
    *out_refs, table_ref, ids_ref, logits_ref, tokens_ref, ids_sem, logits_sem, tokens_sem = refs
    ids_copy = bring(ids_hbm, ids_ref, ids_sem, 1)
    tokens_copy = bring(tokens_hbm, tokens_ref, tokens_sem, 4)
    logits_copy = bring(logits_hbm, logits_ref, logits_sem, 1)
    wait_all(ids_copy)
    mine = lax.axis_index("expert") // SPLIT
    ids = ids_ref[...]
    hit, slot = hits(ids, mine, teams)
    wait_all(logits_copy)
    lifted = jax.nn.sigmoid(logits_ref[...])
    gates = route_scale * lifted / jnp.sum(lifted, axis=0, keepdims=True)
    row = lax.broadcasted_iota(jnp.int32, hit.shape, 0)
    wanted = lax.rem(mine + row, teams)
    gate = jnp.zeros(hit.shape, jnp.float32)
    for j in range(ids.shape[0]):
        gate = gate + jnp.where(ids[j : j + 1, :] == wanted, gates[j : j + 1, :], 0.0)
    table_ref[: hit.shape[0], :] = slot
    table_ref[hit.shape[0] :, :] = gate
    count, features = tokens_ref.shape
    wide = features // SEGMENTS
    tall = CAP * SEGMENTS
    segment, place = fifth((tall, 1), 0)
    column = lax.broadcasted_iota(jnp.int32, (1, SEGMENTS * count), 1)
    same = segment == column // count
    picks = []
    for k in range(teams):
        slots = jnp.concatenate([slot[k : k + 1, :]] * SEGMENTS, axis=1)
        picks.append(jnp.where(same & (slots == place), 1.0, 0.0))
    wait_all(tokens_copy)
    stacked = jnp.concatenate(
        [tokens_ref[:, s * wide : (s + 1) * wide] for s in range(SEGMENTS)], axis=0
    )
    packed = jnp.dot(
        jnp.concatenate(picks, axis=0).astype(jnp.bfloat16),
        stacked,
        preferred_element_type=jnp.float32,
    )
    for k in range(teams):
        out_refs[k][...] = packed[k * tall : (k + 1) * tall].astype(jnp.bfloat16)


def pack_rows(ids, logits, tokens, teams):
    wide = tokens.shape[1] // SEGMENTS
    block = jax.ShapeDtypeStruct((CAP * SEGMENTS, wide), jnp.bfloat16)
    table = jax.ShapeDtypeStruct((16 * pl.cdiv(teams, 8), ids.shape[1]), jnp.float32)
    *packed, table = pl.pallas_call(
        functools.partial(pack_kernel, teams),
        out_shape=[block] * teams + [table],
        in_specs=[HBM] * 3,
        out_specs=[VMEM] * (teams + 1),
        scratch_shapes=[
            pltpu.VMEM(ids.shape, ids.dtype),
            pltpu.VMEM(logits.shape, logits.dtype),
            pltpu.VMEM(tokens.shape, tokens.dtype),
            pltpu.SemaphoreType.DMA((1,)),
            pltpu.SemaphoreType.DMA((1,)),
            pltpu.SemaphoreType.DMA((4,)),
        ],
        name="pack_rows",
    )(ids, logits, tokens)
    return packed, table


def weight_kernel(teams, table_ref, out_ref):
    rows, count = table_ref.shape
    slot = jnp.transpose(table_ref[: rows // 2, :])
    gate = jnp.transpose(table_ref[rows // 2 :, :])
    tall = CAP * SEGMENTS
    depth = out_ref.shape[1]
    column = lax.broadcasted_iota(jnp.int32, (1, depth), 1)
    part = jnp.zeros((1, depth), jnp.int32)
    for g in range(1, depth // tall):
        part = part + jnp.where(column >= g * tall, 1, 0)
    column = column - tall * part
    segment = jnp.zeros((1, depth), jnp.int32)
    for s in range(1, SEGMENTS):
        segment = segment + jnp.where(column >= s * CAP, 1, 0)
    place = (column - CAP * segment).astype(jnp.float32)
    team = jnp.where(part < 3, 0, (part - 1) >> 1)
    low = jnp.where(part < 3, part >> 1, (part - 3) & 1) == 1
    for s in range(SEGMENTS):
        full = jnp.zeros((count, depth), jnp.float32)
        for k in range(teams):
            chosen = (team == k) & (segment == s) & (slot[:, k : k + 1] == place)
            full = full + jnp.where(chosen, gate[:, k : k + 1], 0.0)
        high = full.astype(jnp.bfloat16).astype(jnp.float32)
        out_ref[s * count : (s + 1) * count, :] = jnp.where(low, full - high, high).astype(
            jnp.bfloat16
        )


def blend_weights(table, teams):
    shape = (SEGMENTS * table.shape[1], CAP * SEGMENTS * (1 + 2 * teams))
    return pl.pallas_call(
        functools.partial(weight_kernel, teams),
        out_shape=jax.ShapeDtypeStruct(shape, jnp.bfloat16),
        in_specs=[VMEM],
        out_specs=VMEM,
        compiler_params=params(4 + teams),
        cost_estimate=pl.CostEstimate(flops=6 * 10**9, bytes_accessed=8 * MIB, transcendentals=0),
        name="blend_weights",
    )(table)


def join_kernel(*refs):
    blocks = [ref[...].astype(jnp.float32) for ref in refs[:-1]]
    refs[-1][...] = jnp.concatenate(blocks, axis=0).astype(refs[-1].dtype)


def join(blocks):
    tall, wide = blocks[0].shape
    return pl.pallas_call(
        join_kernel,
        out_shape=jax.ShapeDtypeStruct((tall * len(blocks), wide), blocks[0].dtype),
        in_specs=[VMEM] * len(blocks),
        out_specs=VMEM,
        compiler_params=params(4),
        name="join",
    )(*blocks)


def packed_down(hidden, down_ref, out_ref, flat):
    count, wide = hidden.shape[0], flat.shape[2]
    tall = CAP * SEGMENTS
    for s in range(SEGMENTS):
        slot = flat.at[s % 2]
        slot[:count, :] = jnp.dot(
            hidden, down_ref[:, s * wide : (s + 1) * wide], preferred_element_type=jnp.float32
        )
        for b in range(count // CAP):
            start = b * tall + s * CAP
            out_ref[start : start + CAP, :] = slot[b * CAP : (b + 1) * CAP, :]


def unpack_kernel(own_ref, other_ref, out_ref, packed):
    tall = CAP * SEGMENTS
    half = own_ref.shape[0]
    wide = own_ref.shape[1]
    packed[:half, :] = own_ref[...].astype(jnp.float32)
    packed[half : 2 * half, :] = other_ref[...].astype(jnp.float32)
    for s in range(SEGMENTS):
        for b in range(2 * half // tall):
            start = b * tall + s * CAP
            out_ref[b * CAP : (b + 1) * CAP, s * wide : (s + 1) * wide] = packed[
                start : start + CAP, :
            ]


def unpack(own, other):
    rows, wide = own.shape
    return pl.pallas_call(
        unpack_kernel,
        out_shape=jax.ShapeDtypeStruct(
            (2 * rows // SEGMENTS + ROOM, wide * SEGMENTS), jnp.float32
        ),
        in_specs=[VMEM] * 2,
        out_specs=VMEM,
        scratch_shapes=[pltpu.VMEM((2 * rows + ROOM, wide), jnp.float32)],
        compiler_params=params(6),
        name="unpack",
    )(own, other)


def expert_kernel(teams, first_ref, *refs):
    pieces = refs[: 2 * (teams - 1)]
    gate_ref, up_ref, down_ref = refs[2 * (teams - 1) : 2 * teams + 1]
    *given_refs, hidden_ref, packed, flat, out, act = refs[2 * teams + 1 :]
    tall = CAP * SEGMENTS
    wide = packed.shape[1]
    units = gate_ref.shape[1]
    start = 0
    for ref in pieces:
        packed[start : start + ref.shape[0], :] = ref[...].astype(jnp.float32)
        start += ref.shape[0]
    known = first_ref.shape[0] - ROOM
    count = known * teams
    gate_act = jnp.zeros((count, units), jnp.float32)
    up_act = jnp.zeros((count, units), jnp.float32)
    for s in range(SEGMENTS):
        slot = flat.at[s % 2]
        columns = slice(s * wide, (s + 1) * wide)
        slot[:known, :] = first_ref[:known, columns]
        for b in range((count - known) // CAP):
            start = b * tall + s * CAP
            slot[known + b * CAP : known + (b + 1) * CAP, :] = packed[start : start + CAP, :]
        rows = slot[:count, :].astype(jnp.bfloat16)
        gate_act += jnp.dot(rows, gate_ref[columns, :], preferred_element_type=jnp.float32)
        up_act += jnp.dot(rows, up_ref[columns, :], preferred_element_type=jnp.float32)
    act[:count, :] = jax.nn.silu(gate_act) * up_act
    half = known // 2
    for k in range(teams):
        for core in range(CORES):
            source = (CORES * k + core) * half
            target = count + (core * teams + k) * half
            act[target : target + half, :] = act[source : source + half, :]
    half = count // 2
    hidden_ref[...] = act[count : count + half, :].astype(jnp.bfloat16)
    given = act[count + half : 2 * count, :].astype(jnp.bfloat16)
    packed_down(given, down_ref, out, flat)
    for k, given_ref in enumerate(given_refs):
        rows = given_ref.shape[0]
        given_ref[...] = out[k * rows : (k + 1) * rows, :].astype(jnp.bfloat16)


def expert_half(first, pieces, w_gate, w_up, w_down):
    teams = 1 + len(pieces) // 2
    block, wide = pieces[0].shape
    features, units = w_gate.shape
    rows = (first.shape[0] - ROOM) * teams
    return pl.pallas_call(
        functools.partial(expert_kernel, teams),
        out_shape=[jax.ShapeDtypeStruct((block, wide), jnp.bfloat16)] * teams
        + [jax.ShapeDtypeStruct((rows // 2, units), jnp.bfloat16)],
        in_specs=[VMEM] * (len(pieces) + 4),
        out_specs=[VMEM] * (teams + 1),
        scratch_shapes=[
            pltpu.VMEM((block * len(pieces) + ROOM, wide), jnp.float32),
            pltpu.VMEM((2, rows + ROOM, wide), jnp.float32),
            pltpu.VMEM((block * teams + ROOM, wide), jnp.float32),
            pltpu.VMEM((2 * rows + ROOM, units), jnp.float32),
        ],
        compiler_params=params(16 + 4 * teams),
        cost_estimate=pl.CostEstimate(
            flops=5 * rows * units * features,
            bytes_accessed=6 * features * units,
            transcendentals=rows * units,
        ),
        name="expert_half",
    )(first, *pieces, w_gate, w_up, w_down)


def kept_kernel(hidden_ref, down_ref, kept_ref, flat):
    packed_down(hidden_ref[...], down_ref, kept_ref, flat)


def kept_half(hidden, w_down):
    count, units = hidden.shape
    features = w_down.shape[1]
    wide = features // SEGMENTS
    return pl.pallas_call(
        kept_kernel,
        out_shape=jax.ShapeDtypeStruct((count * SEGMENTS + ROOM, wide), jnp.float32),
        in_specs=[VMEM] * 2,
        out_specs=VMEM,
        scratch_shapes=[pltpu.VMEM((2, count + ROOM, wide), jnp.float32)],
        compiler_params=params(8 + count // 10),
        cost_estimate=pl.CostEstimate(
            flops=2 * count * units * features,
            bytes_accessed=2 * features * units,
            transcendentals=0,
        ),
        name="kept_half",
    )(hidden, w_down)


def add_kernel(first, kept_ref, taken_ref, *out_refs):
    tall = out_refs[0].shape[0]
    total = kept_ref[first : first + taken_ref.shape[0], :] + taken_ref[...].astype(jnp.float32)
    for b, out_ref in enumerate(out_refs):
        out_ref[...] = total[b * tall : (b + 1) * tall].astype(out_ref.dtype)


def add_cores(kept, taken, k, chips):
    shape = (CAP * SEGMENTS, kept.shape[1])
    outs = [jax.ShapeDtypeStruct(shape, jnp.bfloat16 if m else jnp.float32) for m in range(chips)]
    return pl.pallas_call(
        functools.partial(add_kernel, k * taken.shape[0]),
        out_shape=outs,
        in_specs=[VMEM] * 2,
        out_specs=[VMEM] * len(outs),
        compiler_params=params(6),
        name="add_cores",
    )(kept, taken)


def sum_kernel(*refs):
    total = refs[0][...]
    for ref in refs[1:-1]:
        total = total + ref[...].astype(jnp.float32)
    refs[-1][...] = total.astype(refs[-1].dtype)


def sum_blocks(blocks):
    return pl.pallas_call(
        sum_kernel,
        out_shape=jax.ShapeDtypeStruct(blocks[0].shape, jnp.bfloat16),
        in_specs=[VMEM] * len(blocks),
        out_specs=VMEM,
        compiler_params=params(4),
        name="sum_blocks",
    )(*blocks)


def settle_kernel(block_ref, out_ref):
    out_ref[...] = block_ref[...].astype(jnp.float32)


def settle(block):
    return pl.pallas_call(
        settle_kernel,
        out_shape=jax.ShapeDtypeStruct(block.shape, jnp.float32),
        in_specs=[VMEM],
        out_specs=VMEM,
        compiler_params=params(4),
        cost_estimate=pl.CostEstimate(flops=3 * 10**9, bytes_accessed=MIB, transcendentals=0),
        name="settle",
    )(block)


def partial_kernel(*refs):
    total = refs[0][...]
    for ref in refs[1:-1]:
        total = total + ref[...].astype(jnp.float32)
    refs[-1][...] = total


def partial_sum(blocks):
    return pl.pallas_call(
        partial_kernel,
        out_shape=jax.ShapeDtypeStruct(blocks[0].shape, jnp.float32),
        in_specs=[VMEM] * len(blocks),
        out_specs=VMEM,
        compiler_params=params(4),
        cost_estimate=pl.CostEstimate(flops=300 * 10**6, bytes_accessed=MIB, transcendentals=0),
        name="partial_sum",
    )(*blocks)


def halves(wide):
    cut = 128 * pl.cdiv(wide // 128, 2)
    return slice(0, cut), slice(cut, wide)


def blend_kernel(chips, weight_ref, *refs):
    *refs, out_hbm, out_ref, sem = refs
    count, features = out_ref.shape
    wide = features // SEGMENTS
    own = refs[0][...]
    for ref in refs[1:chips]:
        own = own + ref[...].astype(jnp.float32)
    high = own.astype(jnp.bfloat16).astype(jnp.float32)
    terms = [high, own - high, high]
    for ref in refs[chips:]:
        terms += [ref[...].astype(jnp.float32)] * 2
    rows = jnp.concatenate(terms, axis=0).astype(jnp.bfloat16)
    copies = []
    for columns in halves(wide):
        size = columns.stop - columns.start
        total = jnp.dot(weight_ref[...], rows[:, columns], preferred_element_type=jnp.float32)
        for s in range(SEGMENTS):
            part = pl.ds(s * wide + columns.start, size)
            out_ref[:, part] = total[s * count : (s + 1) * count].astype(jnp.bfloat16)
            copies.append(
                pltpu.make_async_copy(
                    out_ref.at[:, part], out_hbm.at[:, part], sem.at[len(copies)]
                )
            )
            copies[-1].start()
    wait_all(copies)


def blend(weights, own_blocks, other_blocks, count):
    chips = len(own_blocks)
    features = own_blocks[0].shape[1] * SEGMENTS
    return pl.pallas_call(
        functools.partial(blend_kernel, chips),
        out_shape=jax.ShapeDtypeStruct((count, features), jnp.bfloat16),
        in_specs=[VMEM] * (1 + chips + len(other_blocks)),
        out_specs=HBM,
        scratch_shapes=[
            pltpu.VMEM((count, features), jnp.bfloat16),
            pltpu.SemaphoreType.DMA((2 * SEGMENTS,)),
        ],
        compiler_params=params(16),
        name="blend",
    )(weights, *own_blocks, *other_blocks)


def body(tokens, expert_ids, route_logits, w_gate, w_up, w_down):
    devices = lax.axis_size("expert")
    teams = devices // SPLIT
    chips = SPLIT // CORES
    other_core = [(i, i ^ 1) for i in range(devices)]
    other_chip = [[(i, i ^ (m * CORES)) for i in range(devices)] for m in range(chips)]
    packed, table = pack_rows(expert_ids.T, route_logits.T, tokens, teams)
    def gather(block):
        return [block] + [lax.ppermute(block, "expert", other_chip[m]) for m in range(1, chips)]

    own = gather(packed[0])
    crowds = []
    for k in range(1, teams):
        pairs = [(i, (i + k * SPLIT) % devices) for i in range(devices)]
        block = lax.ppermute(packed[k], "expert", pairs)
        if k == teams - 1:
            block, table = lax.optimization_barrier((block, table))
            weights = blend_weights(table, teams)
        crowds.append(gather(block))
    own, weights = lax.optimization_barrier((own, weights))
    own = join(own)
    first = unpack(own, lax.ppermute(own, "expert", other_core))
    pieces = []
    for crowd in crowds:
        crowd = join(crowd)
        pieces += [crowd, lax.ppermute(crowd, "expert", other_core)]
    *given, hidden = expert_half(first, pieces, w_gate, w_up, w_down)
    taken = [lax.ppermute(piece, "expert", other_core) for piece in given]
    kept = kept_half(hidden, w_down)
    totals = []
    for k in range(1, teams):
        parts = add_cores(kept, taken[k], k, chips)
        parts, later = lax.optimization_barrier((parts, kept))
        team = [parts[0]]
        for m in reversed(range(1, chips)):
            team.append(lax.ppermute(parts[m], "expert", other_chip[m]))
        totals.append(sum_blocks(team))
    parts = list(add_cores(later, taken[0], 0, chips))
    totals, parts[1] = lax.optimization_barrier((totals, parts[1]))
    others = []
    for k in range(1, teams):
        pairs = [(i, (i - k * SPLIT) % devices) for i in range(devices)]
        others.append(settle(lax.ppermute(totals[k - 1], "expert", pairs)))
    own = [parts[0]]
    for m in reversed(range(2, chips)):
        own.append(lax.ppermute(parts[m], "expert", other_chip[m]))
    own = [partial_sum(own), lax.ppermute(parts[1], "expert", other_chip[1])]
    return blend(weights, own, others, tokens.shape[0])


def solution(mesh):
    placed = (
        P(("groups", "expert"), None),
        P(("groups", "expert"), None),
        P(("groups", "expert"), None),
        P(None, "expert"),
        P(None, "expert"),
        P("expert", None),
    )
    return jax.shard_map(
        body, mesh=mesh, in_specs=placed, out_specs=P(("groups", "expert"), None), check_vma=False
    )
```
